128 devices in a mesh: gx: 8 (over y, x_lo), gy: 8 (over x_hi, z), ga: 2 (over core).
Axes of the slice: x: 4 (x_hi: 2, x_lo: 2; x = x_hi * 2 + x_lo), y: 4, z: 4, core: 2. Of those that a mesh axis runs over, the one named last changes fastest.
Arguments:
- fields: float32 [5, 16, 128, 2048], P(None, 'ga', 'gx', 'gy'), may hold values from -6 to 6
- stiffness: float32 [16, 128, 2048], P('ga', 'gx', 'gy'), may hold values from 0.25 to 4
- lift_weight: float32 [5, 32], replicated, may hold values from -2.5 to 2.5
- lift_bias: float32 [32], replicated, may hold values from -3 to 3
- mix_weight: bfloat16 [32, 32], replicated, may hold values from -0.5 to 0.5
- spectral_weight: float32 [8, 32, 32, 32, 128], P('ga', 'gy', None, 'gx'), may hold values from -0.48 to 0.48
- output_bias: float32 [32], replicated, may hold values from -3 to 3
Outputs:
- layer_out: bfloat16 [16, 32, 64, 1024], P('ga', None, 'gx', 'gy')
The draws below stay inside these ranges and needn't reach their ends.
All inputs are finite; a program needn't handle non-finite values.
Results may differ from the reference program's by a relative error of at most 0.01.
Values may be sent and summed in bfloat16 or wider, within the bound.
No kernel may reach another device: no remote copies, remote signals or barrier semaphores. Data moves between devices by JAX's collectives and lax.ppermute only.
A program may use at most 128 MiB of HBM per device.

```python
import math
import jax
import jax.numpy as jnp
from jax import lax

NZ = 16
STEPS = 3
C = 32
MX = 32
MY = 64
MZ = 8
NX = 128
NY = 2048


wave_count = 48


def wave_tables(key, term_count):
    key_list = jax.random.split(key, 4)
    east_reach = max(1, min(MX // 2 - 1, NX // 16))
    north_reach = max(1, min(MY // 2 - 1, NY // 16))
    east_wave = jax.random.randint(key_list[0], (term_count,), -east_reach, east_reach + 1, dtype=jnp.int32)
    north_wave = jax.random.randint(key_list[1], (term_count,), -north_reach, north_reach + 1, dtype=jnp.int32)
    east_shift = jax.random.uniform(key_list[2], (term_count, 1), jnp.float32, 0.0, 2.0 * math.pi)
    north_shift = jax.random.uniform(key_list[3], (term_count, 1), jnp.float32, 0.0, 2.0 * math.pi)
    east_index = jnp.arange(NX, dtype=jnp.int32)
    north_index = jnp.arange(NY, dtype=jnp.int32)
    east_angle = jnp.mod(east_wave[:, None] * east_index[None, :], NX).astype(jnp.float32) * (2.0 * math.pi / NX) + east_shift
    north_angle = jnp.mod(north_wave[:, None] * north_index[None, :], NY).astype(jnp.float32) * (2.0 * math.pi / NY) + north_shift
    return (jnp.cos(east_angle), jnp.sin(east_angle), jnp.cos(north_angle), jnp.sin(north_angle))


def smooth_field(key, amplitude):
    east_cos, east_sin, north_cos, north_sin = wave_tables(key, amplitude.shape[-1])
    first = jnp.einsum('...j,jx,jy->...xy', amplitude, east_cos, north_cos)
    second = jnp.einsum('...j,jx,jy->...xy', amplitude, east_sin, north_sin)
    return first - second


def draw_fields(key, part):
    key_list = jax.random.split(key, 3)
    depth_index = jnp.arange(NZ, dtype=jnp.int32)
    orders = jnp.arange(5, dtype=jnp.int32)
    depth_angle = jnp.mod(orders[:, None] * depth_index[None, :], NZ).astype(jnp.float32) * (2.0 * math.pi / NZ)
    profile = jnp.stack([jnp.cos(depth_angle), jnp.sin(depth_angle)], axis=1)
    target = 2.5
    jagged = jax.random.normal(key_list[2], (5, NZ, NX, NY), jnp.float32)
    weights_depth = jax.random.normal(key_list[0], (5, wave_count, 5, 2), jnp.float32) * (target / math.sqrt(2.5 * wave_count))
    amplitude = jnp.einsum('fjkp,kpz->fzj', weights_depth, profile)
    smooth = smooth_field(key_list[1], amplitude)
    return jnp.clip(smooth + jagged, -6.0, 6.0)


def draw_stiffness(key, part):
    key_list = jax.random.split(key, 3)
    amplitude = jax.random.normal(key_list[0], (NZ, wave_count), jnp.float32) * (1.0 / math.sqrt(0.5 * wave_count))
    smooth = smooth_field(key_list[1], amplitude)
    jagged = jax.random.uniform(key_list[2], (NZ, NX, NY), jnp.float32, -1.0, 1.0)
    level = 0.5 + 0.3 * smooth + 0.25 * jagged
    level = jnp.clip(level, 0.0, 1.0)
    return 0.25 * jnp.exp(level * math.log(16.0))


def block_levels(rng, shape, pieces, smallest, top_value):
    factor_of, own = 1.0, jax.random.fold_in(rng, 6)
    for position, blocks in pieces:
        heights = jnp.exp(jax.random.uniform(jax.random.fold_in(own, position), (blocks,), jnp.float32, smallest / len(pieces), top_value / len(pieces)))
        factor_of = factor_of * jnp.repeat(heights, shape[position] // blocks).reshape([-1 if axis == position else 1 for axis in range(len(shape))])
    return factor_of


def gaussian(rng, dims, width, bound, cuts=(), kind=jnp.bfloat16):
    result = width * jax.random.normal(rng, dims, jnp.float32)
    if cuts:
        result = result * block_levels(rng, dims, cuts, -0.22, 0.18)
    return jnp.clip(result, -bound, bound).astype(kind)


def setup_inputs(seed: int = 0) -> dict:
    keys = jax.random.split(jax.random.key(seed), 8)
    return {
        "fields": draw_fields(jax.random.fold_in(keys[7], 71), 0),
        "stiffness": draw_stiffness(jax.random.fold_in(keys[7], 71), 0),
        "lift_weight": gaussian(keys[2], (5, C), 5 ** -0.5, 2.5, (), jnp.float32),
        "lift_bias": gaussian(keys[3], (C,), 0.5, 3.0, (), jnp.float32),
        "mix_weight": gaussian(keys[4], (C, C), (4 * C) ** -0.5, 0.5),
        "spectral_weight": gaussian(keys[5], (MZ, MX, C, C, 2 * MY), 0.08, 0.48, ((0, 2), (1, 8), (3, 8)), jnp.float32),
        "output_bias": gaussian(keys[6], (C,), 0.5, 3.0, (), jnp.float32),
    }


courant_half = 0.1
smooth_half = 0.15
mean_flow = (0.3, -0.2, 0.1)
highest = lax.Precision.HIGHEST

def step_interior(padded, stiff_part):
    center = padded[:, 1:-1, 1:-1, 1:-1]
    upper_depth = padded[:, 2:, 1:-1, 1:-1]
    lower_depth = padded[:, :-2, 1:-1, 1:-1]
    upper_east = padded[:, 1:-1, 2:, 1:-1]
    lower_east = padded[:, 1:-1, :-2, 1:-1]
    upper_north = padded[:, 1:-1, 1:-1, 2:]
    lower_north = padded[:, 1:-1, 1:-1, :-2]
    slope_depth = upper_depth - lower_depth
    slope_east = upper_east - lower_east
    slope_north = upper_north - lower_north
    curvature = upper_depth + lower_depth + upper_east + lower_east + upper_north + lower_north - 6.0 * center
    transport = mean_flow[0] * slope_east + mean_flow[1] * slope_north + mean_flow[2] * slope_depth
    diverge = slope_east[1] + slope_north[2] + slope_depth[3]
    coupling = jnp.stack([diverge, slope_east[4], slope_north[4], slope_depth[4], stiff_part * diverge])
    return center - courant_half * (transport + coupling) + smooth_half * curvature

def coarsen(fields_now):
    extent = fields_now.shape
    blocks = fields_now.reshape(extent[0], extent[1], extent[2] // 2, 2, extent[3] // 2, 2)
    return 0.25 * (blocks[:, :, :, 0, :, 0] + blocks[:, :, :, 1, :, 0] + blocks[:, :, :, 0, :, 1] + blocks[:, :, :, 1, :, 1])

def angles(frequencies, points, length):
    product = jnp.mod(frequencies[:, None] * points[None, :], length)
    return product.astype(jnp.float32) * (2.0 * math.pi / length)

def centered(number):
    return jnp.arange(number, dtype=jnp.int32) - number // 2

def forward_east_table(points, length, mode_count):
    phases = angles(centered(mode_count), points, length)
    factor = 1.0 / math.sqrt(length)
    return (jnp.stack([jnp.cos(phases).T, -jnp.sin(phases).T], axis=1) * factor).astype(jnp.bfloat16)

def forward_north_table(points, length, mode_count):
    phases = angles(centered(mode_count), points, length)
    factor = 1.0 / math.sqrt(length)
    cosines = jnp.cos(phases).T * factor
    sines = jnp.sin(phases).T * factor
    return jnp.stack([jnp.concatenate([cosines, -sines], axis=1), jnp.concatenate([sines, cosines], axis=1)], axis=0)

def inverse_north_table(points, length, mode_count):
    phases = angles(centered(mode_count), points, length)
    factor = 1.0 / math.sqrt(length)
    cosines = jnp.cos(phases) * factor
    sines = jnp.sin(phases) * factor
    return jnp.concatenate([jnp.stack([cosines, sines], axis=1), jnp.stack([-sines, cosines], axis=1)], axis=0)

def inverse_east_table(points, length, mode_count):
    phases = angles(centered(mode_count), points, length)
    factor = 1.0 / math.sqrt(length)
    return jnp.stack([jnp.cos(phases) * factor, -jnp.sin(phases) * factor], axis=1)

def forward_depth(values, points, frequencies, length):
    phases = angles(frequencies, points, length)
    factor = 1.0 / math.sqrt(length)
    cosines = jnp.cos(phases) * factor
    sines = jnp.sin(phases) * factor
    halfway = values.shape[-1] // 2
    real_in = values[..., :halfway]
    imag_in = values[..., halfway:]
    real_part = jnp.einsum('zcmn,kz->kcmn', real_in, cosines, precision=highest) + jnp.einsum('zcmn,kz->kcmn', imag_in, sines, precision=highest)
    imag_part = jnp.einsum('zcmn,kz->kcmn', imag_in, cosines, precision=highest) - jnp.einsum('zcmn,kz->kcmn', real_in, sines, precision=highest)
    return jnp.concatenate([real_part, imag_part], axis=-1)

def mix_channels(coeffs, weight):
    halfway = coeffs.shape[-1] // 2
    real_in = coeffs[..., :halfway]
    imag_in = coeffs[..., halfway:]
    weight_real = weight[..., :halfway]
    weight_imag = weight[..., halfway:]
    real_part = jnp.einsum('kcmn,kmcon->komn', real_in, weight_real, precision=highest) - jnp.einsum('kcmn,kmcon->komn', imag_in, weight_imag, precision=highest)
    imag_part = jnp.einsum('kcmn,kmcon->komn', imag_in, weight_real, precision=highest) + jnp.einsum('kcmn,kmcon->komn', real_in, weight_imag, precision=highest)
    return jnp.concatenate([real_part, imag_part], axis=-1)

def inverse_depth(values, frequencies, points, length):
    phases = angles(frequencies, points, length)
    factor = 1.0 / math.sqrt(length)
    cosines = jnp.cos(phases) * factor
    sines = jnp.sin(phases) * factor
    halfway = values.shape[-1] // 2
    real_in = values[..., :halfway]
    imag_in = values[..., halfway:]
    real_part = jnp.einsum('komn,kz->zomn', real_in, cosines, precision=highest) - jnp.einsum('komn,kz->zomn', imag_in, sines, precision=highest)
    imag_part = jnp.einsum('komn,kz->zomn', imag_in, cosines, precision=highest) + jnp.einsum('komn,kz->zomn', real_in, sines, precision=highest)
    return jnp.concatenate([real_part, imag_part], axis=-1)

def reference(fields, stiffness, lift_weight, lift_bias, mix_weight, spectral_weight, output_bias):
    fields_now = fields
    for repeat in range(STEPS):
        padded = jnp.pad(fields_now, ((0, 0), (1, 1), (1, 1), (1, 1)), mode='wrap')
        fields_now = step_interior(padded, stiffness)
    filtered = coarsen(fields_now)
    length_depth = filtered.shape[1]
    length_east = filtered.shape[2]
    length_north = filtered.shape[3]
    by_plane = jnp.transpose(filtered, (1, 0, 2, 3))

    def lift_plane(plane_fields):
        lifted_plane = jnp.einsum('fxy,fc->cxy', plane_fields, lift_weight, precision=highest) + lift_bias[:, None, None]
        return jax.nn.gelu(lifted_plane, approximate=True).astype(jnp.bfloat16)
    lifted = lax.map(lift_plane, by_plane)
    east_points = jnp.arange(length_east, dtype=jnp.int32)
    north_points = jnp.arange(length_north, dtype=jnp.int32)
    table_east = forward_east_table(east_points, length_east, MX).astype(jnp.float32)
    table_north = forward_north_table(north_points, length_north, MY)

    def plane_modes(lift_slice):
        east_modes = jnp.einsum('cxy,xpm->cpmy', lift_slice.astype(jnp.float32), table_east, precision=highest)
        return jnp.einsum('cpmy,pyq->cmq', east_modes, table_north, precision=highest)
    north_modes = lax.map(plane_modes, lifted)
    depth_points = jnp.arange(length_depth, dtype=jnp.int32)
    depth_frequencies = jnp.arange(MZ, dtype=jnp.int32)
    coeffs = forward_depth(north_modes, depth_points, depth_frequencies, length_depth)
    mixed_modes = mix_channels(coeffs, spectral_weight)
    back_depth = inverse_depth(mixed_modes, depth_frequencies, depth_points, length_depth)
    back_north_table = inverse_north_table(north_points, length_north, MY)
    back_east_table = inverse_east_table(east_points, length_east, MX)
    mix_wide = mix_weight.astype(jnp.float32)

    def plane_output(paired):
        lift_slice, modes_plane = paired
        back_north = jnp.einsum('omq,qpy->ompy', modes_plane, back_north_table, precision=highest)
        spectral = jnp.einsum('ompy,mpx->oxy', back_north, back_east_table, precision=highest).astype(jnp.bfloat16)
        direct = jnp.einsum('cxy,co->oxy', lift_slice.astype(jnp.float32), mix_wide, precision=highest)
        summed = direct + output_bias[:, None, None] + spectral.astype(jnp.float32)
        return jax.nn.gelu(summed, approximate=True).astype(jnp.bfloat16)
    return lax.map(plane_output, (lifted, back_depth))
```

```python
import functools
import math

import jax
import jax.numpy as jnp
import numpy as np
from jax import lax
from jax.experimental import pallas as pl
from jax.experimental.pallas import tpu as pltpu
from jax.sharding import PartitionSpec as P

NZ, C, MX, MY, MZ, GX, GY = 16, 32, 32, 64, 8, 64, 1024
ZL, XL, YL = 8, 16, 256
F32, BF16 = jnp.float32, jnp.bfloat16
ROOT = math.sqrt(2.0 / math.pi)
VMEM = pl.BlockSpec(memory_space=pltpu.VMEM)
SMEM = pl.BlockSpec(memory_space=pltpu.SMEM)


def cos_sin(freq, points, length):
    turn = np.mod(np.outer(freq, points), length) * (2.0 * np.pi / length)
    return np.cos(turn), np.sin(turn)


def split(table):
    table = np.asarray(table, np.float32)
    high = table.astype(jnp.bfloat16)
    low = (table - high.astype(np.float32)).astype(jnp.bfloat16)
    return high, low


@functools.cache
def tables():
    out = {}
    pairs = np.zeros((YL, YL // 2), np.float32)
    pairs[np.arange(YL), np.arange(YL) // 2] = 0.25
    out["pairs"] = pairs.astype(jnp.bfloat16)
    ky = np.arange(MY) - MY // 2
    cy, sy = cos_sin(ky, np.arange(GY), GY)
    rows = np.concatenate([cy, -sy]) / math.sqrt(GY)
    out["yf"] = np.concatenate(split(rows))
    rows = np.concatenate([cy, -sy]) / math.sqrt(GY)
    high, low = split(rows)
    out["yi"] = np.concatenate([high, high, low])
    kz = np.arange(MZ)
    cz, sz = (t / math.sqrt(NZ) for t in cos_sin(kz, np.arange(ZL), NZ))
    eye = np.eye(C)

    def kron_f(t):
        return np.einsum("kz,cd->czkd", t, eye).reshape(C * ZL, 2, 4 * C)

    zf = np.zeros((2, C * ZL, 2, 2, 4 * C))
    zf[0, :, :, 0], zf[1, :, :, 0] = kron_f(cz), kron_f(sz)
    zf[1, :, :, 1], zf[0, :, :, 1] = kron_f(cz), -kron_f(sz)
    out["zf"] = np.stack(split(zf.reshape(2 * C * ZL, 8 * 2 * C)))
    zi = np.zeros((2, 2, 4, C, 2, ZL, C))
    for half in range(2):
        for k in range(4):
            for z in range(ZL):
                c, s = cz[4 * half + k, z] * eye, sz[4 * half + k, z] * eye
                zi[half, 0, k, :, 0, z], zi[half, 1, k, :, 0, z] = c, -s
                zi[half, 1, k, :, 1, z], zi[half, 0, k, :, 1, z] = c, s
    out["zi"] = np.stack(split(zi.reshape(16 * C, 2 * ZL * C)))
    kx = np.arange(MX) - MX // 2
    cx, sx = cos_sin(kx, np.arange(GX), GX)
    cr = (cx / 8.0).astype(np.float32).astype(jnp.bfloat16).astype(np.float64)
    sr = (-sx / 8.0).astype(np.float32).astype(jnp.bfloat16).astype(np.float64)
    cr, sr = cr.reshape(8, 4, GX), sr.reshape(8, 4, GX)
    xf = np.zeros((2, 8, 4, 4, 4, GX, 2, 2))
    for k in range(4):
        for a in range(2):
            sign = -1.0 if (k * a) % 2 else 1.0
            xf[0, :, k, :, k, :, a, 0] = sign * cr
            xf[0, :, k, :, k, :, a, 1] = -sign * sr
            xf[1, :, k, :, k, :, a, 0] = sign * sr
            xf[1, :, k, :, k, :, a, 1] = sign * cr
    out["xf"] = xf.reshape(256, 1024).astype(np.float32).astype(jnp.bfloat16)
    ex = np.zeros((4, 4, C, C, 4), np.float32)
    for k in range(4):
        for c in range(C):
            ex[k, k, c, c] = 1.0
    out["ex"] = ex.reshape(4, 128, 128).astype(jnp.bfloat16)
    rm = np.zeros((8, C, 4, 4, 8, 4), np.float32)
    for i in range(8):
        for o in range(4):
            rm[i, :, o, :, i, o] = 1.0
    out["rm"] = rm.reshape(1024, 128).astype(jnp.bfloat16)
    mask = np.zeros((2, 8, 4, 4, 4, C), np.float32)
    for k in range(4):
        mask[:, :, k, :, k] = 1.0
    out["mask"] = mask.reshape(256, 128)
    ic, is_ = (cx / 8.0).T.reshape(GX, 8, 1, 4), (sx / 8.0).T.reshape(GX, 8, 1, 4)
    xi = np.zeros((2, GX, 2, 8, 4, 4))
    xi[0, :, 0], xi[0, :, 1] = ic, -is_
    xi[1, :, 0], xi[1, :, 1] = is_, ic
    out["xi"] = np.stack(split(xi.reshape(128, 256)))
    return out


def halves(value):
    high = value.astype(BF16)
    return high, (value - high.astype(F32)).astype(BF16)


def dot(a, b, contract=((1,), (0,))):
    return lax.dot_general(a, b, (contract, ((), ())), preferred_element_type=F32)


def dot3(a, b_ref):
    high, low = halves(a)
    return dot(high, b_ref[0]) + dot(low, b_ref[0]) + dot(high, b_ref[1])


def gelu(v):
    return 0.5 * v * (1.0 + jnp.tanh(ROOT * (v + 0.044715 * (v * v * v))))


def call(kernel, outs, in_specs, scratch=(), mib=16, flops=10**7, size=2**20):
    return pl.pallas_call(
        kernel,
        out_shape=[jax.ShapeDtypeStruct(s, d) for s, d in outs],
        in_specs=in_specs,
        out_specs=[VMEM] * len(outs),
        scratch_shapes=list(scratch),
        compiler_params=pltpu.CompilerParams(vmem_limit_bytes=mib << 20),
        cost_estimate=pl.CostEstimate(flops=flops, bytes_accessed=size, transcendentals=0),
    )


NEEDED = list(range(8)) + [8, 9, 14, 15]


def pack_x(f, s, fp, sp, low, high, rows):
    for field in range(6):
        for which, whole in enumerate(((s, sp) if field == 5 else (f.at[field], fp.at[field]))):
            for h in range(2):
                rows[which, field, h] = whole[:, 128 * h : 128 * h + 128]
    for field in range(6):
        for h in range(2):
            for which, count in ((0, 3), (1, 2)):
                for d in range(count):
                    at = 24 * which + 8 * d
                    first = rows[which, field, h, pl.ds(d, 8, stride=XL), :]
                    last = rows[which, field, h, pl.ds(XL - 1 - d, 8, stride=XL), :]
                    low[field, h, at : at + 8, :] = first
                    high[field, h, at : at + 8, :] = last


def pack_y(f, s, fp, sp, up, down, xh, low, high):
    xh[...] = jnp.zeros_like(xh)
    lane = lax.broadcasted_iota(jnp.int32, (24, 128), 1) // 8
    for field in range(6):
        for h in range(2):
            for base, at, count in ((0, 0, 3), (64, 24, 2)):
                for d in range(count):
                    take = slice(at + 8 * d, at + 8 * d + 8)
                    xh[field, h, pl.ds(base + d, 8, stride=8), :] = up[field, h, take, :]
                    xh[field, h, pl.ds(base + 7 - d, 8, stride=8), :] = down[field, h, take, :]
        lows = jnp.zeros((24, 128), F32)
        highs = jnp.zeros((24, 128), F32)
        for slot in NEEDED:
            own, other = (s, sp) if field == 5 else (f.at[field], fp.at[field])
            ref = own if slot < 8 else other
            part = slice(16 * (slot % 8), 16 * (slot % 8) + 16)
            edge = slice(8 * slot, 8 * slot + 8)
            here = lane == slot
            first = jnp.concatenate([ref[part, :128], xh[field, 0, edge, :]], axis=0)
            last = jnp.concatenate([ref[part, 128:], xh[field, 1, edge, :]], axis=0)
            lows = jnp.where(here, pltpu.roll(first, (8 * slot) % 128, 1), lows)
            highs = jnp.where(here, pltpu.roll(last, (8 * slot + 8) % 128, 1), highs)
        low[field] = lows
        high[field] = highs


def stencil(f, s, fp, sp, xh, ylow, yhigh, pairs, wide, narrow, a, b, stiff, last, sums):
    near = lax.broadcasted_iota(jnp.int32, (24, 128), 1) < 64
    for zi in range(14):
        slot = zi - 3 if 3 <= zi < 11 else (13 + zi if zi < 3 else zi - 3)
        part = slice(16 * (slot % 8), 16 * (slot % 8) + 16)
        for field in range(6):
            if field == 5 and zi in (0, 13):
                continue
            own, other = (s, sp) if field == 5 else (f, fp)
            ref = own if slot < 8 else other
            to = stiff.at[zi] if field == 5 else a.at[field, zi]
            to[0:16, 0:256] = ref[part, :] if field == 5 else ref[field, part, :]
            for h in range(2):
                edge = xh[field, h, 8 * slot : 8 * slot + 8, :]
                to[16:24, 128 * h : 128 * h + 128] = edge
            to[:, 256:384] = jnp.where(
                near,
                pltpu.roll(ylow[field], (128 - 8 * slot) % 128, 1),
                pltpu.roll(yhigh[field], (120 - 8 * slot) % 128, 1),
            )

    def advance(src, zi):
        new, east, north, depth = [], [], [], []
        for field in range(5):
            mid = src[field, zi]
            up, down = src[field, zi + 1], src[field, zi - 1]
            xp, xm = pltpu.roll(mid, 23, 0), pltpu.roll(mid, 1, 0)
            yp, ym = pltpu.roll(mid, 383, 1), pltpu.roll(mid, 1, 1)
            total = 0.1 * mid + 0.12 * xp + 0.18 * xm + 0.17 * yp + 0.13 * ym
            new.append(total + 0.14 * up + 0.16 * down)
            east.append(xp - xm if field in (1, 4) else None)
            north.append(yp - ym if field in (2, 4) else None)
            depth.append(up - down if field in (3, 4) else None)
        div = 0.1 * (east[1] + north[2] + depth[3])
        new[0] = new[0] - div
        new[1] = new[1] - 0.1 * east[4]
        new[2] = new[2] - 0.1 * north[4]
        new[3] = new[3] - 0.1 * depth[4]
        new[4] = new[4] - stiff[zi] * div
        return new

    for step, (src, dst) in enumerate(((a, b), (b, a), (a, None))):
        first, end = 1 + step, 13 - step

        def body(zi, carry, src=src, dst=dst):
            new = advance(src, zi)
            for field in range(5):
                if dst is None:
                    rows = pl.ds(pl.multiple_of((zi - 3) * 16, 16), 16)
                    for h in range(2):
                        last[field, h, rows, :] = new[field][0:16, 128 * h : 128 * h + 128]
                else:
                    dst[field, zi] = new[field]
            return carry

        lax.fori_loop(first, end, body, 0)

    for x in range(8):
        for field in range(5):
            at = 40 * x + 8 * field
            for h in range(2):
                even = last[field, h, pl.ds(2 * x, 8, stride=16), :]
                odd = last[field, h, pl.ds(2 * x + 1, 8, stride=16), :]
                sums[at : at + 8, 128 * h : 128 * h + 128] = even + odd
    value = sums[...]
    high = value.astype(BF16)
    rest = value - high.astype(F32)
    mid, low = halves(rest)
    table = pairs[...]
    mean = dot(high, table) + dot(mid, table) + dot(low, table)
    wide[...] = mean
    mean = mean.reshape(8, 40, 128)
    narrow[...] = jnp.concatenate([mean, jnp.zeros((8, 8, 128), F32)], axis=1).astype(BF16)


def lift_rows(values, weight, bias):
    rows = []
    for c in range(C):
        v = bias[c] + values[0] * weight[0, c]
        for field in range(1, 5):
            v = v + values[field] * weight[field, c]
        rows.append(gelu(v))
    return jnp.concatenate(rows, axis=0).astype(BF16)


def pointwise(wide, weight, bias, mix, obias, out):
    def body(z, carry):
        values = [wide[pl.ds(8 * field + z, 8, stride=40), :] for field in range(5)]
        out[z] = dot(mix[...], lift_rows(values, weight, bias)) + obias[...]
        return carry

    lax.fori_loop(0, ZL, body, 0)


def forward(got, weight, bias, yf, zf, out, lifted):
    for j in range(8):
        block = got[j].astype(F32)
        values = [block[8 * field : 8 * field + 8] for field in range(5)]
        lifted[:, 128 * j : 128 * j + 128] = lift_rows(values, weight, bias)
    modes = dot(yf[...], lifted[...], ((1,), (1,)))
    modes = modes[:128] + modes[128:]
    modes = jnp.concatenate([modes[:64], modes[64:]], axis=1)
    result = dot3(modes, zf)
    for part in range(4):
        out[:, part, :] = result[:, 128 * part : 128 * part + 128]


def mix_modes(got, weights, xf, ex, rm, mask, xi, out):
    high, low = halves(got[...])
    spread_high = jnp.concatenate([dot(high, ex[k]).astype(BF16) for k in range(4)], axis=0)
    spread_low = jnp.concatenate([dot(low, ex[k]).astype(BF16) for k in range(4)], axis=0)
    modes = dot(xf[...], spread_high) + dot(xf[...], spread_low)
    real, imag = modes[:128], modes[128:]
    total = jnp.zeros((256, 128), F32)
    for i in range(8):
        wr = weights[8 * i : 8 * i + 8, 0:16, :].astype(F32).reshape(128, 128)
        wi = weights[8 * i : 8 * i + 8, 16:32, :].astype(F32).reshape(128, 128)
        part = jnp.concatenate([wr * real - wi * imag, wr * imag + wi * real], axis=0)
        p_high, p_low = halves(part)
        table = rm[128 * i : 128 * i + 128, :]
        total = total + dot(p_high, table) + dot(p_low, table)
    total = total * mask[...]
    t_high, t_low = halves(total)
    back = dot(xi[0], t_high) + dot(xi[0], t_low) + dot(xi[1], t_high)
    odd = (lax.broadcasted_iota(jnp.int32, (64, 128), 1) // 32) % 2 == 1
    for ri in range(2):
        value = back[64 * ri : 64 * ri + 64]
        out[:, ri, :] = value
        out[:, 2 + ri, :] = jnp.where(odd, -value, value)


def inverse(got, zi, yi, out):
    modes = jnp.concatenate([got[:, part, :] for part in range(4)], axis=1)
    by_z = dot3(modes, zi)
    by_z = jnp.concatenate([by_z[:, :256], by_z[:, 256:]], axis=0)
    high, low = halves(by_z)
    stacked = jnp.concatenate([high, low, high], axis=0)
    for j in range(8):
        block = dot(stacked, yi[:, 128 * j : 128 * j + 128], ((0,), (0,)))
        out[j] = block.astype(BF16)


def finish(got, direct, out, rows):
    for x in range(8):
        rows[256 * x : 256 * x + 256, :] = got[x].astype(F32)

    def body(z, carry):
        for o in range(C):
            spectral = rows[pl.ds(C * z + o, 8, stride=256), :]
            total = direct[z, 8 * o : 8 * o + 8, :] + spectral
            out[z, o] = gelu(total).astype(BF16)
        return carry

    lax.fori_loop(0, ZL, body, 0)


def turn_weights(weights, out):
    for chunk in range(16):
        turned = weights[128 * chunk : 128 * chunk + 128, :].T
        for ri in range(2):
            out[:, 16 * ri + chunk, :] = turned[64 * ri : 64 * ri + 64]


def shards(fields, stiffness, lift_weight, lift_bias, mix_weight, spectral_weight, output_bias):
    table = {name: jnp.asarray(value) for name, value in tables().items()}
    everyone = ("gx", "gy", "ga")

    def exchange(value, axis):
        return lax.all_to_all(value, axis, split_axis=0, concat_axis=0, tiled=True)

    def shift(value, axis, by):
        return lax.ppermute(value, axis, [(i, (i + by) % 8) for i in range(8)])

    [turned] = call(turn_weights, [((64, 32, 128), F32)], [VMEM], mib=8)(
        spectral_weight.reshape(2048, 128)
    )
    weights = exchange(turned, ("gx", "gy"))

    f = fields.reshape(5, 128, 256)
    s = stiffness.reshape(128, 256)
    swap = [(0, 1), (1, 0)]
    fp, sp = lax.ppermute(f, "ga", swap), lax.ppermute(s, "ga", swap)
    message = ((6, 2, 40, 128), F32)
    copied = [pltpu.VMEM((2, 6, 2, 128, 128), F32)]
    low, high = call(pack_x, [message, message], [VMEM] * 4, copied)(f, s, fp, sp)
    up, down = shift(low, "gx", -1), shift(high, "gx", 1)
    message = ((6, 24, 128), F32)
    xh, low, high = call(pack_y, [((6, 2, 128, 128), F32), message, message], [VMEM] * 6)(
        f, s, fp, sp, up, down
    )
    ylow, yhigh = shift(low, "gy", -1), shift(high, "gy", 1)
    wide, narrow = call(
        stencil,
        [((320, 128), F32), ((8, 48, 128), BF16)],
        [VMEM] * 8,
        [
            pltpu.VMEM((5, 14, 24, 384), F32),
            pltpu.VMEM((5, 14, 24, 384), F32),
            pltpu.VMEM((14, 24, 384), F32),
            pltpu.VMEM((5, 2, 128, 128), F32),
            pltpu.VMEM((320, 256), F32),
        ],
        mib=24,
    )(f, s, fp, sp, xh, ylow, yhigh, table["pairs"])

    columns = exchange(narrow, "gy")
    spread = jnp.einsum("co,xy->oxcy", mix_weight, jnp.eye(8, dtype=BF16)).reshape(256, 256)
    obias = jnp.broadcast_to(jnp.repeat(output_bias, 8)[:, None], (256, 128))
    [direct] = call(
        pointwise, [((8, 256, 128), F32)], [VMEM, SMEM, SMEM, VMEM, VMEM], flops=3 * 10**8
    )(wide, lift_weight, lift_bias, spread, obias)

    [modes] = call(
        forward,
        [((64, 4, 128), F32)],
        [VMEM, SMEM, SMEM, VMEM, VMEM],
        [pltpu.VMEM((256, 1024), BF16)],
    )(columns, lift_weight, lift_bias, table["yf"], table["zf"])
    modes = exchange(modes.reshape(128, 2, 128), everyone)
    [mixed] = call(mix_modes, [((64, 4, 128), F32)], [VMEM] * 7, mib=24)(
        modes.reshape(256, 128),
        weights,
        table["xf"],
        table["ex"],
        table["rm"],
        table["mask"],
        table["xi"],
    )
    mixed = exchange(mixed.reshape(128, 2, 128), everyone)
    [spectral] = call(inverse, [((8, 256, 128), BF16)], [VMEM] * 3)(
        mixed.reshape(64, 4, 128), table["zi"], table["yi"]
    )
    spectral = exchange(spectral, "gy")
    [out] = call(
        finish, [((8, 32, 8, 128), BF16)], [VMEM] * 2, [pltpu.VMEM((2048, 128), F32)]
    )(spectral, direct)
    return out


def solution(mesh):
    placed = (
        P(None, "ga", "gx", "gy"),
        P("ga", "gx", "gy"),
        P(),
        P(),
        P(),
        P("ga", "gy", None, "gx", None),
        P(),
    )
    return jax.shard_map(
        shards, mesh=mesh, in_specs=placed, out_specs=P("ga", None, "gx", "gy"), check_vma=False
    )
```

```python
import functools
import math

import jax
import jax.numpy as jnp
import numpy as np
from jax import lax
from jax.experimental import pallas as pl
from jax.experimental.pallas import tpu as pltpu
from jax.sharding import PartitionSpec as P

NZ, C, MX, MY, MZ, GX, GY = 16, 32, 32, 64, 8, 64, 1024
ZL, XL, YL = 8, 16, 256
F32, BF16 = jnp.float32, jnp.bfloat16
ROOT = math.sqrt(2.0 / math.pi)
VMEM = pl.BlockSpec(memory_space=pltpu.VMEM)
SMEM = pl.BlockSpec(memory_space=pltpu.SMEM)


def cos_sin(freq, points, length):
    turn = np.mod(np.outer(freq, points), length) * (2.0 * np.pi / length)
    return np.cos(turn), np.sin(turn)


def split(table):
    table = np.asarray(table, np.float32)
    high = table.astype(jnp.bfloat16)
    low = (table - high.astype(np.float32)).astype(jnp.bfloat16)
    return high, low


@functools.cache
def tables():
    out = {}
    pairs = np.zeros((YL, YL // 2), np.float32)
    pairs[np.arange(YL), np.arange(YL) // 2] = 0.25
    out["pairs"] = pairs.astype(jnp.bfloat16)
    ky = np.arange(MY) - MY // 2
    cy, sy = cos_sin(ky, np.arange(GY), GY)
    rows = np.concatenate([cy, -sy]) / math.sqrt(GY)
    out["yf"] = np.concatenate(split(rows))
    rows = np.concatenate([cy, -sy]) / math.sqrt(GY)
    high, low = split(rows)
    out["yi"] = np.concatenate([high, high, low])
    kz = np.arange(MZ)
    cz, sz = (t / math.sqrt(NZ) for t in cos_sin(kz, np.arange(ZL), NZ))
    eye = np.eye(C)

    def kron_f(t):
        return np.einsum("kz,cd->czkd", t, eye).reshape(C * ZL, 2, 4 * C)

    zf = np.zeros((2, C * ZL, 2, 2, 4 * C))
    zf[0, :, :, 0], zf[1, :, :, 0] = kron_f(cz), kron_f(sz)
    zf[1, :, :, 1], zf[0, :, :, 1] = kron_f(cz), -kron_f(sz)
    out["zf"] = np.stack(split(zf.reshape(2 * C * ZL, 8 * 2 * C)))
    zi = np.zeros((2, 2, 4, C, 2, ZL, C))
    for half in range(2):
        for k in range(4):
            for z in range(ZL):
                c, s = cz[4 * half + k, z] * eye, sz[4 * half + k, z] * eye
                zi[half, 0, k, :, 0, z], zi[half, 1, k, :, 0, z] = c, -s
                zi[half, 1, k, :, 1, z], zi[half, 0, k, :, 1, z] = c, s
    out["zi"] = np.stack(split(zi.reshape(16 * C, 2 * ZL * C)))
    kx = np.arange(MX) - MX // 2
    cx, sx = cos_sin(kx, np.arange(GX), GX)
    cr = (cx / 8.0).astype(np.float32).astype(jnp.bfloat16).astype(np.float64)
    sr = (-sx / 8.0).astype(np.float32).astype(jnp.bfloat16).astype(np.float64)
    cr, sr = cr.reshape(8, 4, GX), sr.reshape(8, 4, GX)
    xf = np.zeros((2, 8, 4, 4, 4, GX, 2, 2))
    for k in range(4):
        for a in range(2):
            sign = -1.0 if (k * a) % 2 else 1.0
            xf[0, :, k, :, k, :, a, 0] = sign * cr
            xf[0, :, k, :, k, :, a, 1] = -sign * sr
            xf[1, :, k, :, k, :, a, 0] = sign * sr
            xf[1, :, k, :, k, :, a, 1] = sign * cr
    xf = xf.reshape(256, 4, 256).transpose(1, 0, 2).reshape(1024, 256)
    xf = xf.astype(np.float32).astype(jnp.bfloat16)
    ic, is_ = (cx / 8.0).T.reshape(GX, 8, 1, 4), (sx / 8.0).T.reshape(GX, 8, 1, 4)
    xi = np.zeros((2, GX, 2, 8, 4, 4))
    xi[0, :, 0], xi[0, :, 1] = ic, -is_
    xi[1, :, 0], xi[1, :, 1] = is_, ic
    out["x"] = np.concatenate([xf, *split(xi.reshape(128, 256))]).reshape(5, 256, 256)
    return out


def halves(value):
    high = value.astype(BF16)
    return high, (value - high.astype(F32)).astype(BF16)


def dot(a, b, contract=((1,), (0,))):
    return lax.dot_general(a, b, (contract, ((), ())), preferred_element_type=F32)


def dot3(a, b_ref):
    high, low = halves(a)
    return dot(high, b_ref[0]) + dot(low, b_ref[0]) + dot(high, b_ref[1])


def gelu(v):
    return 0.5 * v * (1.0 + jnp.tanh(ROOT * (v + 0.044715 * (v * v * v))))


def call(kernel, outs, in_specs, scratch=(), mib=16, flops=10**7, size=2**20):
    return pl.pallas_call(
        kernel,
        out_shape=[jax.ShapeDtypeStruct(s, d) for s, d in outs],
        in_specs=in_specs,
        out_specs=[VMEM] * len(outs),
        scratch_shapes=list(scratch),
        compiler_params=pltpu.CompilerParams(vmem_limit_bytes=mib << 20),
        cost_estimate=pl.CostEstimate(flops=flops, bytes_accessed=size, transcendentals=0),
    )


NEEDED = list(range(8)) + [8, 9, 14, 15]


def pack_x(f, s, fp, sp, low, high, rows):
    for field in range(6):
        for which, whole in enumerate(((s, sp) if field == 5 else (f.at[field], fp.at[field]))):
            for h in range(2):
                rows[which, field, h] = whole[:, 128 * h : 128 * h + 128]
    for field in range(6):
        for h in range(2):
            for which, count in ((0, 3), (1, 2)):
                for d in range(count):
                    at = 24 * which + 8 * d
                    first = rows[which, field, h, pl.ds(d, 8, stride=XL), :]
                    last = rows[which, field, h, pl.ds(XL - 1 - d, 8, stride=XL), :]
                    low[field, h, at : at + 8, :] = first
                    high[field, h, at : at + 8, :] = last


def pack_y(f, s, fp, sp, up, down, xh, low, high):
    xh[...] = jnp.zeros_like(xh)
    lane = lax.broadcasted_iota(jnp.int32, (24, 128), 1) // 8
    for field in range(6):
        for h in range(2):
            for base, at, count in ((0, 0, 3), (64, 24, 2)):
                for d in range(count):
                    take = slice(at + 8 * d, at + 8 * d + 8)
                    xh[field, h, pl.ds(base + d, 8, stride=8), :] = up[field, h, take, :]
                    xh[field, h, pl.ds(base + 7 - d, 8, stride=8), :] = down[field, h, take, :]
        lows = jnp.zeros((24, 128), F32)
        highs = jnp.zeros((24, 128), F32)
        for slot in NEEDED:
            own, other = (s, sp) if field == 5 else (f.at[field], fp.at[field])
            ref = own if slot < 8 else other
            part = slice(16 * (slot % 8), 16 * (slot % 8) + 16)
            edge = slice(8 * slot, 8 * slot + 8)
            here = lane == slot
            first = jnp.concatenate([ref[part, :128], xh[field, 0, edge, :]], axis=0)
            last = jnp.concatenate([ref[part, 128:], xh[field, 1, edge, :]], axis=0)
            lows = jnp.where(here, pltpu.roll(first, (8 * slot) % 128, 1), lows)
            highs = jnp.where(here, pltpu.roll(last, (8 * slot + 8) % 128, 1), highs)
        low[field] = lows
        high[field] = highs


def stencil(f, s, fp, sp, xh, ylow, yhigh, pairs, after, wide, narrow, a, b, stiff, last, sums):
    near = lax.broadcasted_iota(jnp.int32, (24, 128), 1) < 64
    for zi in range(14):
        slot = zi - 3 if 3 <= zi < 11 else (13 + zi if zi < 3 else zi - 3)
        part = slice(16 * (slot % 8), 16 * (slot % 8) + 16)
        for field in range(6):
            if field == 5 and zi in (0, 13):
                continue
            own, other = (s, sp) if field == 5 else (f, fp)
            ref = own if slot < 8 else other
            to = stiff.at[zi] if field == 5 else a.at[field, zi]
            to[0:16, 0:256] = ref[part, :] if field == 5 else ref[field, part, :]
            for h in range(2):
                edge = xh[field, h, 8 * slot : 8 * slot + 8, :]
                to[16:24, 128 * h : 128 * h + 128] = edge
            to[:, 256:384] = jnp.where(
                near,
                pltpu.roll(ylow[field], (128 - 8 * slot) % 128, 1),
                pltpu.roll(yhigh[field], (120 - 8 * slot) % 128, 1),
            )

    def advance(src, zi):
        new, east, north, depth = [], [], [], []
        for field in range(5):
            mid = src[field, zi]
            up, down = src[field, zi + 1], src[field, zi - 1]
            xp, xm = pltpu.roll(mid, 23, 0), pltpu.roll(mid, 1, 0)
            yp, ym = pltpu.roll(mid, 383, 1), pltpu.roll(mid, 1, 1)
            total = 0.1 * mid + 0.12 * xp + 0.18 * xm + 0.17 * yp + 0.13 * ym
            new.append(total + 0.14 * up + 0.16 * down)
            east.append(xp - xm if field in (1, 4) else None)
            north.append(yp - ym if field in (2, 4) else None)
            depth.append(up - down if field in (3, 4) else None)
        div = 0.1 * (east[1] + north[2] + depth[3])
        new[0] = new[0] - div
        new[1] = new[1] - 0.1 * east[4]
        new[2] = new[2] - 0.1 * north[4]
        new[3] = new[3] - 0.1 * depth[4]
        new[4] = new[4] - stiff[zi] * div
        return new

    for step, (src, dst) in enumerate(((a, b), (b, a), (a, None))):
        first, end = 1 + step, 13 - step

        def body(zi, carry, src=src, dst=dst):
            new = advance(src, zi)
            for field in range(5):
                if dst is None:
                    rows = pl.ds(pl.multiple_of((zi - 3) * 16, 16), 16)
                    for h in range(2):
                        last[field, h, rows, :] = new[field][0:16, 128 * h : 128 * h + 128]
                else:
                    dst[field, zi] = new[field]
            return carry

        lax.fori_loop(first, end, body, 0)

    for x in range(8):
        for field in range(5):
            at = 40 * x + 8 * field
            for h in range(2):
                even = last[field, h, pl.ds(2 * x, 8, stride=16), :]
                odd = last[field, h, pl.ds(2 * x + 1, 8, stride=16), :]
                sums[at : at + 8, 128 * h : 128 * h + 128] = even + odd
    value = sums[...]
    high = value.astype(BF16)
    rest = value - high.astype(F32)
    mid, low = halves(rest)
    table = pairs[...]
    mean = dot(high, table) + dot(mid, table) + dot(low, table)
    wide[...] = mean
    mean = mean.reshape(8, 40, 128)
    narrow[...] = jnp.concatenate([mean, jnp.zeros((8, 8, 128), F32)], axis=1).astype(BF16)


def lift_rows(values, weight, bias):
    rows = []
    for c in range(C):
        v = bias[c] + values[0] * weight[0, c]
        for field in range(1, 5):
            v = v + values[field] * weight[field, c]
        rows.append(gelu(v))
    return jnp.concatenate(rows, axis=0).astype(BF16)


def pointwise(wide, weight, bias, mix, obias, out):
    def body(z, carry):
        values = [wide[pl.ds(8 * field + z, 8, stride=40), :] for field in range(5)]
        out[z] = dot(mix[...], lift_rows(values, weight, bias)) + obias[...]
        return carry

    lax.fori_loop(0, ZL, body, 0)


def forward(got, weight, bias, yf, zf, out, lifted):
    for j in range(8):
        block = got[j].astype(F32)
        values = [block[8 * field : 8 * field + 8] for field in range(5)]
        lifted[:, 128 * j : 128 * j + 128] = lift_rows(values, weight, bias)
    modes = dot(yf[...], lifted[...], ((1,), (1,)))
    modes = modes[:128] + modes[128:]
    modes = jnp.concatenate([modes[:64], modes[64:]], axis=1)
    result = dot3(modes, zf)
    for part in range(4):
        out[:, part, :] = result[:, 128 * part : 128 * part + 128]


def iotas(shape):
    return lax.broadcasted_iota(jnp.int32, shape, 0), lax.broadcasted_iota(jnp.int32, shape, 1)


def mix_modes(got, weights, x_tables, out):
    high, low = halves(got[...])
    row, lane = iotas((128, 128))
    modes = jnp.zeros((256, 128), F32)
    for k in range(4):
        spread = (row == 32 * k + lane // 4).astype(BF16)
        modes = modes + dot(x_tables[k], dot(high, spread).astype(BF16))
        modes = modes + dot(x_tables[k], dot(low, spread).astype(BF16))
    real, imag = modes[:128], modes[128:]
    total = jnp.zeros((256, 128), F32)
    for i in range(8):
        wr = weights[8 * i : 8 * i + 8, 0:16, :].astype(F32).reshape(128, 128)
        wi = weights[8 * i : 8 * i + 8, 16:32, :].astype(F32).reshape(128, 128)
        part = jnp.concatenate([wr * real - wi * imag, wr * imag + wi * real], axis=0)
        p_high, p_low = halves(part)
        gather = (lane % 32 == 4 * i + row % 4).astype(BF16)
        total = total + dot(p_high, gather) + dot(p_low, gather)
    row, lane = iotas((256, 128))
    total = jnp.where((row // 4) % 4 == lane // 32, total, 0.0)
    t_high, t_low = halves(total)
    back_high, back_low = x_tables[4, :128], x_tables[4, 128:]
    back = dot(back_high, t_high) + dot(back_high, t_low) + dot(back_low, t_high)
    odd = (lax.broadcasted_iota(jnp.int32, (64, 128), 1) // 32) % 2 == 1
    for ri in range(2):
        value = back[64 * ri : 64 * ri + 64]
        out[:, ri, :] = value
        out[:, 2 + ri, :] = jnp.where(odd, -value, value)


def inverse(got, zi, yi, out):
    modes = jnp.concatenate([got[:, part, :] for part in range(4)], axis=1)
    by_z = dot3(modes, zi)
    by_z = jnp.concatenate([by_z[:, :256], by_z[:, 256:]], axis=0)
    high, low = halves(by_z)
    stacked = jnp.concatenate([high, low, high], axis=0)
    for j in range(8):
        block = dot(stacked, yi[:, 128 * j : 128 * j + 128], ((0,), (0,)))
        out[j] = block.astype(BF16)


def finish(got, direct, out, rows):
    for x in range(8):
        rows[256 * x : 256 * x + 256, :] = got[x].astype(F32)

    def body(z, carry):
        for o in range(C):
            spectral = rows[pl.ds(C * z + o, 8, stride=256), :]
            total = direct[z, 8 * o : 8 * o + 8, :] + spectral
            out[z, o] = gelu(total).astype(BF16)
        return carry

    lax.fori_loop(0, ZL, body, 0)


def turn_weights(weights, out):
    for chunk in range(16):
        turned = weights[128 * chunk : 128 * chunk + 128, :].T
        for ri in range(2):
            out[:, 16 * ri + chunk, :] = turned[64 * ri : 64 * ri + 64]


def shards(fields, stiffness, lift_weight, lift_bias, mix_weight, spectral_weight, output_bias):
    table = {name: jnp.asarray(value) for name, value in tables().items()}
    everyone = ("gx", "gy", "ga")

    def exchange(value, axis):
        return lax.all_to_all(value, axis, split_axis=0, concat_axis=0, tiled=True)

    def shift(value, axis, by):
        return lax.ppermute(value, axis, [(i, (i + by) % 8) for i in range(8)])

    [turned] = call(turn_weights, [((64, 32, 128), F32)], [VMEM], mib=8)(
        spectral_weight.reshape(2048, 128)
    )
    weights = exchange(turned, ("gx", "gy"))

    f = fields.reshape(5, 128, 256)
    s = stiffness.reshape(128, 256)
    swap = [(0, 1), (1, 0)]
    fp, sp = lax.ppermute(f, "ga", swap), lax.ppermute(s, "ga", swap)
    message = ((6, 2, 40, 128), F32)
    copied = [pltpu.VMEM((2, 6, 2, 128, 128), F32)]
    low, high = call(pack_x, [message, message], [VMEM] * 4, copied)(f, s, fp, sp)
    up, down = shift(low, "gx", -1), shift(high, "gx", 1)
    message = ((6, 24, 128), F32)
    xh, low, high = call(pack_y, [((6, 2, 128, 128), F32), message, message], [VMEM] * 6)(
        f, s, fp, sp, up, down
    )
    ylow, yhigh = shift(low, "gy", -1), shift(high, "gy", 1)
    wide, narrow = call(
        stencil,
        [((320, 128), F32), ((8, 48, 128), BF16)],
        [VMEM] * 8 + [pl.BlockSpec(memory_space=pl.ANY)],
        [
            pltpu.VMEM((5, 14, 24, 384), F32),
            pltpu.VMEM((5, 14, 24, 384), F32),
            pltpu.VMEM((14, 24, 384), F32),
            pltpu.VMEM((5, 2, 128, 128), F32),
            pltpu.VMEM((320, 256), F32),
        ],
        mib=24,
    )(f, s, fp, sp, xh, ylow, yhigh, table["pairs"], weights)

    columns = exchange(narrow, "gy")
    spread = jnp.einsum("co,xy->oxcy", mix_weight, jnp.eye(8, dtype=BF16)).reshape(256, 256)
    obias = jnp.broadcast_to(jnp.repeat(output_bias, 8)[:, None], (256, 128))
    [direct] = call(
        pointwise, [((8, 256, 128), F32)], [VMEM, SMEM, SMEM, VMEM, VMEM], flops=3 * 10**8
    )(wide, lift_weight, lift_bias, spread, obias)

    [modes] = call(
        forward,
        [((64, 4, 128), F32)],
        [VMEM, SMEM, SMEM, VMEM, VMEM],
        [pltpu.VMEM((256, 1024), BF16)],
    )(columns, lift_weight, lift_bias, table["yf"], table["zf"])
    modes = exchange(modes.reshape(128, 2, 128), everyone)
    [mixed] = call(mix_modes, [((64, 4, 128), F32)], [VMEM] * 3, mib=24)(
        modes.reshape(256, 128), weights, table["x"]
    )
    mixed = exchange(mixed.reshape(128, 2, 128), everyone)
    [spectral] = call(inverse, [((8, 256, 128), BF16)], [VMEM] * 3)(
        mixed.reshape(64, 4, 128), table["zi"], table["yi"]
    )
    spectral = exchange(spectral, "gy")
    [out] = call(
        finish, [((8, 32, 8, 128), BF16)], [VMEM] * 2, [pltpu.VMEM((2048, 128), F32)]
    )(spectral, direct)
    return out


def solution(mesh):
    placed = (
        P(None, "ga", "gx", "gy"),
        P("ga", "gx", "gy"),
        P(),
        P(),
        P(),
        P("ga", "gy", None, "gx", None),
        P(),
    )
    return jax.shard_map(
        shards, mesh=mesh, in_specs=placed, out_specs=P("ga", None, "gx", "gy"), check_vma=False
    )
```

```python
import functools
import math

import jax
import jax.numpy as jnp
import numpy as np
from jax import lax
from jax.experimental import pallas as pl
from jax.experimental.pallas import tpu as pltpu
from jax.sharding import PartitionSpec as P

NZ, C, MX, MY, MZ, GX, GY = 16, 32, 32, 64, 8, 64, 1024
ZL, XL, YL = 8, 16, 256
F32, BF16 = jnp.float32, jnp.bfloat16
ROOT = math.sqrt(2.0 / math.pi)
VMEM = pl.BlockSpec(memory_space=pltpu.VMEM)
SMEM = pl.BlockSpec(memory_space=pltpu.SMEM)


def cos_sin(freq, points, length):
    turn = np.mod(np.outer(freq, points), length) * (2.0 * np.pi / length)
    return np.cos(turn), np.sin(turn)


def split(table):
    table = np.asarray(table, np.float32)
    high = table.astype(jnp.bfloat16)
    low = (table - high.astype(np.float32)).astype(jnp.bfloat16)
    return high, low


@functools.cache
def tables():
    out = {}
    pairs = np.zeros((YL, YL // 2), np.float32)
    pairs[np.arange(YL), np.arange(YL) // 2] = 0.25
    out["pairs"] = pairs.astype(jnp.bfloat16)
    ky = np.arange(MY) - MY // 2
    cy, sy = cos_sin(ky, np.arange(GY), GY)
    rows = np.concatenate([cy, -sy]) / math.sqrt(GY)
    out["yf"] = np.concatenate(split(rows))
    rows = np.concatenate([cy, -sy]) / math.sqrt(GY)
    high, low = split(rows)
    out["yi"] = np.concatenate([high, high, low])
    kz = np.arange(MZ)
    cz, sz = (t / math.sqrt(NZ) for t in cos_sin(kz, np.arange(ZL), NZ))
    eye = np.eye(C)

    def kron_f(t):
        return np.einsum("kz,cd->czkd", t, eye).reshape(C * ZL, 2, 4 * C)

    zf = np.zeros((2, C * ZL, 2, 2, 4 * C))
    zf[0, :, :, 0], zf[1, :, :, 0] = kron_f(cz), kron_f(sz)
    zf[1, :, :, 1], zf[0, :, :, 1] = kron_f(cz), -kron_f(sz)
    out["zf"] = np.stack(split(zf.reshape(2 * C * ZL, 8 * 2 * C)))
    zi = np.zeros((2, 2, 4, C, 2, ZL, C))
    for half in range(2):
        for k in range(4):
            for z in range(ZL):
                c, s = cz[4 * half + k, z] * eye, sz[4 * half + k, z] * eye
                zi[half, 0, k, :, 0, z], zi[half, 1, k, :, 0, z] = c, -s
                zi[half, 1, k, :, 1, z], zi[half, 0, k, :, 1, z] = c, s
    out["zi"] = np.stack(split(zi.reshape(16 * C, 2 * ZL * C)))
    kx = np.arange(MX) - MX // 2
    cx, sx = cos_sin(kx, np.arange(GX), GX)
    cr = (cx / 8.0).astype(np.float32).astype(jnp.bfloat16).astype(np.float64)
    sr = (-sx / 8.0).astype(np.float32).astype(jnp.bfloat16).astype(np.float64)
    cr, sr = cr.reshape(8, 4, 8, 2, 4), sr.reshape(8, 4, 8, 2, 4)
    xf = np.zeros((4, 2, 8, 4, 4, 8, 4, 2, 2, 2))
    for k in range(4):
        for a in range(2):
            for h in range(2):
                sign = -1.0 if k * (h ^ a) % 2 else 1.0
                real, imag = sign * cr[:, :, :, a], sign * sr[:, :, :, a]
                xf[k, 0, :, k, :, :, :, h, a, 0] = real
                xf[k, 0, :, k, :, :, :, h, a, 1] = -imag
                xf[k, 1, :, k, :, :, :, h, a, 0] = imag
                xf[k, 1, :, k, :, :, :, h, a, 1] = real
    xf = xf.reshape(1024, 256).astype(np.float32).astype(jnp.bfloat16)
    ic, is_ = (cx / 8.0).T.reshape(GX, 8, 1, 4), (sx / 8.0).T.reshape(GX, 8, 1, 4)
    xi = np.zeros((2, GX, 2, 8, 4, 4))
    xi[0, :, 0], xi[0, :, 1] = ic, -is_
    xi[1, :, 0], xi[1, :, 1] = is_, ic
    out["x"] = np.concatenate([xf, *split(xi.reshape(128, 256))]).reshape(5, 256, 256)
    return out


def halves(value):
    high = value.astype(BF16)
    return high, (value - high.astype(F32)).astype(BF16)


def dot(a, b, contract=((1,), (0,))):
    return lax.dot_general(a, b, (contract, ((), ())), preferred_element_type=F32)


def dot3(a, b_ref):
    high, low = halves(a)
    return dot(high, b_ref[0]) + dot(low, b_ref[0]) + dot(high, b_ref[1])


def gelu(v):
    return 0.5 * v * (1.0 + jnp.tanh(ROOT * (v + 0.044715 * (v * v * v))))


def call(kernel, outs, in_specs, scratch=(), mib=16, flops=10**7, size=2**20):
    return pl.pallas_call(
        kernel,
        out_shape=[jax.ShapeDtypeStruct(s, d) for s, d in outs],
        in_specs=in_specs,
        out_specs=[VMEM] * len(outs),
        scratch_shapes=list(scratch),
        compiler_params=pltpu.CompilerParams(vmem_limit_bytes=mib << 20),
        cost_estimate=pl.CostEstimate(flops=flops, bytes_accessed=size, transcendentals=0),
    )


def rows_of(refs, field, slot, half):
    f, s, fp, sp = refs
    own, other = (s, sp) if field == 5 else (f.at[field], fp.at[field])
    start = 16 * (slot % 8) + 8 * half
    return (own if slot < 8 else other)[pl.ds(pl.multiple_of(start, 8), 8), :]


def pack_x(f, s, fp, sp, message, rows):
    bottom = lax.axis_index("ga") == 0
    for field in range(6):
        for which, whole in enumerate(((s, sp) if field == 5 else (f.at[field], fp.at[field]))):
            for h in range(2):
                rows[which, field, h] = whole[:, 128 * h : 128 * h + 128]
    for field in range(6):
        for h in range(2):
            for which in range(2):
                for d in range(3):
                    first = rows[which, field, h, pl.ds(d, 8, stride=XL), :]
                    last = rows[which, field, h, pl.ds(XL - 1 - d, 8, stride=XL), :]
                    at = 24 * which + 8 * d
                    message[field, h, at : at + 8, :] = jnp.where(bottom, first, last)


def pack_y(f, s, fp, sp, message, outer, low, high):
    refs = (f, s, fp, sp)
    a = lax.axis_index("ga")
    row = lax.broadcasted_iota(jnp.int32, (8, 128), 0)
    beyond = jnp.where(a == 1, row, 7 - row) < 3
    lane = lax.broadcasted_iota(jnp.int32, (16, 128), 1) // 4
    lows, highs = jnp.zeros((16, 128), F32), jnp.zeros((16, 128), F32)
    for field in range(6):
        for h in range(2):
            for which in range(2):
                for d in range(3):
                    at = 24 * which + 8 * d
                    value = message[field, h, at : at + 8, :]
                    to = 64 * (1 - which)
                    outer[field, h, pl.ds(to + d, 8, stride=8), :] = value
                    outer[field, h, pl.ds(to + 7 - d, 8, stride=8), :] = value
        for slot in range(16):
            inner, block = rows_of(refs, field, slot, a), rows_of(refs, field, slot, 1 - a)
            edge = slice(8 * slot, 8 * slot + 8)
            for h in range(2):
                kept = block[:, 128 * h : 128 * h + 128]
                outer[field, h, edge, :] = jnp.where(beyond, outer[field, h, edge, :], kept)
            base = 64 * (field % 2) + 4 * slot
            here = lane == base // 4
            first = jnp.concatenate([inner[:, :128], outer[field, 0, edge, :]], axis=0)
            last = jnp.concatenate([inner[:, 128:], outer[field, 1, edge, :]], axis=0)
            lows = jnp.where(here, pltpu.roll(first, base, 1) if base else first, lows)
            highs = jnp.where(here, pltpu.roll(last, (base + 4) % 128, 1) if base != 124 else last, highs)
        if field % 2:
            low[field // 2] = lows
            high[field // 2] = highs


def stencil(
    f, s, fp, sp, outer, ylow, yhigh, pairs, after, keep, send, narrow, a, b, stiff, last, sums
):
    refs = (f, s, fp, sp)
    core = lax.axis_index("ga")
    near = lax.broadcasted_iota(jnp.int32, (16, 128), 1) < 64
    for field in range(6):
        for slot in range(16):
            to = stiff.at[slot] if field == 5 else a.at[field, slot]
            to[0:8, 0:256] = rows_of(refs, field, slot, core)
            for h in range(2):
                edge = outer[field, h, 8 * slot : 8 * slot + 8, :]
                to[8:16, 128 * h : 128 * h + 128] = edge
            base = 64 * (field % 2) + 4 * slot
            above, below = ylow[field // 2], yhigh[field // 2]
            above = pltpu.roll(above, 128 - base, 1) if base else above
            below = pltpu.roll(below, 124 - base, 1) if base != 124 else below
            to[:, 256:384] = jnp.where(near, above, below)

    def advance(src, slot, crop):
        new, east, north, depth = [], [], [], []
        for field in range(5):
            mid = src[field, slot]
            up, down = src[field, (slot + 1) & 15], src[field, (slot + 15) & 15]
            xp, xm = pltpu.roll(mid, 15, 0), pltpu.roll(mid, 1, 0)
            yp, ym = pltpu.roll(mid, 383, 1), pltpu.roll(mid, 1, 1)
            if crop:
                mid, up, down, xp, xm, yp, ym = (
                    v[0:8, 0:256] for v in (mid, up, down, xp, xm, yp, ym)
                )
            total = 0.1 * mid + 0.12 * xp + 0.18 * xm + 0.17 * yp + 0.13 * ym
            new.append(total + 0.14 * up + 0.16 * down)
            east.append(xp - xm if field in (1, 4) else None)
            north.append(yp - ym if field in (2, 4) else None)
            depth.append(up - down if field in (3, 4) else None)
        div = 0.1 * (east[1] + north[2] + depth[3])
        new[0] = new[0] - div
        new[1] = new[1] - 0.1 * east[4]
        new[2] = new[2] - 0.1 * north[4]
        new[3] = new[3] - 0.1 * depth[4]
        new[4] = new[4] - (stiff[slot, 0:8, 0:256] if crop else stiff[slot]) * div
        return new

    for src, dst in ((a, b), (b, a), (a, None)):

        def body(slot, carry, src=src, dst=dst):
            new = advance(src, slot, dst is None)
            for field in range(5):
                if dst is None:
                    rows = pl.ds(pl.multiple_of(slot * 8, 8), 8)
                    for h in range(2):
                        last[field, h, rows, :] = new[field][:, 128 * h : 128 * h + 128]
                else:
                    dst[field, slot] = new[field]
            return carry

        lax.fori_loop(0, 16, body, 0)

    for half in range(2):
        for x in range(4):
            for field in range(5):
                at = 160 * half + 40 * x + 8 * field
                for h in range(2):
                    even = last[field, h, pl.ds(64 * half + 2 * x, 8, stride=8), :]
                    odd = last[field, h, pl.ds(64 * half + 2 * x + 1, 8, stride=8), :]
                    sums[at : at + 8, 128 * h : 128 * h + 128] = even + odd
    value = sums[...]
    high = value.astype(BF16)
    rest = value - high.astype(F32)
    mid, low = halves(rest)
    table = pairs[...]
    mean = dot(high, table) + dot(mid, table) + dot(low, table)
    keep[...] = mean[:160]
    send[...] = mean[160:]
    for half in range(2):
        for x in range(4):
            at = 160 * half + 40 * x
            block = jnp.concatenate([mean[at : at + 40], jnp.zeros((8, 128), F32)], axis=0)
            narrow[2 * x + half] = block.astype(BF16)


def lift_rows(values, weight, bias):
    rows = []
    for c in range(C):
        v = bias[c] + values[0] * weight[0, c]
        for field in range(1, 5):
            v = v + values[field] * weight[field, c]
        rows.append(gelu(v))
    return jnp.concatenate(rows, axis=0).astype(BF16)


def pointwise(keep, got, weight, bias, mix, obias, out, wide):
    a = lax.axis_index("ga")
    wide[pl.ds(pl.multiple_of(160 * a, 8), 160), :] = keep[...]
    wide[pl.ds(pl.multiple_of(160 * (1 - a), 8), 160), :] = got[...]

    def body(z, carry):
        values = [wide[pl.ds(8 * field + z, 8, stride=40), :] for field in range(5)]
        out[z] = dot(mix[...], lift_rows(values, weight, bias)) + obias[...]
        return carry

    lax.fori_loop(0, ZL, body, 0)


def forward(got, weight, bias, yf, zf, out, lifted):
    for j in range(8):
        block = got[j].astype(F32)
        values = [block[8 * field : 8 * field + 8] for field in range(5)]
        lifted[:, 128 * j : 128 * j + 128] = lift_rows(values, weight, bias)
    modes = dot(yf[...], lifted[...], ((1,), (1,)))
    modes = modes[:128] + modes[128:]
    modes = jnp.concatenate([modes[:64], modes[64:]], axis=1)
    result = dot3(modes, zf)
    for part in range(4):
        out[:, part, :] = result[:, 128 * part : 128 * part + 128]


def iotas(shape):
    return lax.broadcasted_iota(jnp.int32, shape, 0), lax.broadcasted_iota(jnp.int32, shape, 1)


def mix_modes(got, weights, x_tables, out):
    high, low = halves(got[...])
    row, lane = iotas((128, 128))
    modes = jnp.zeros((256, 128), F32)
    for k in range(4):
        spread = (row == 32 * k + lane // 4).astype(BF16)
        modes = modes + dot(x_tables[k], dot(high, spread).astype(BF16))
        modes = modes + dot(x_tables[k], dot(low, spread).astype(BF16))
    real, imag = modes[:128], modes[128:]
    total = jnp.zeros((256, 128), F32)
    for i in range(8):
        wr = weights[8 * i : 8 * i + 8, 0:16, :].astype(F32).reshape(128, 128)
        wi = weights[8 * i : 8 * i + 8, 16:32, :].astype(F32).reshape(128, 128)
        part = jnp.concatenate([wr * real - wi * imag, wr * imag + wi * real], axis=0)
        p_high, p_low = halves(part)
        gather = (lane % 32 == 4 * i + row % 4).astype(BF16)
        total = total + dot(p_high, gather) + dot(p_low, gather)
    row, lane = iotas((256, 128))
    total = jnp.where((row // 4) % 4 == lane // 32, total, 0.0)
    t_high, t_low = halves(total)
    back_high, back_low = x_tables[4, :128], x_tables[4, 128:]
    back = dot(back_high, t_high) + dot(back_high, t_low) + dot(back_low, t_high)
    odd = (lax.broadcasted_iota(jnp.int32, (64, 128), 1) // 32) % 2 == 1
    for ri in range(2):
        value = back[64 * ri : 64 * ri + 64]
        out[:, ri, :] = value
        out[:, 2 + ri, :] = jnp.where(odd, -value, value)


def inverse(got, zi, yi, out):
    modes = jnp.concatenate([got[:, part, :] for part in range(4)], axis=1)
    by_z = dot3(modes, zi)
    by_z = jnp.concatenate([by_z[:, :256], by_z[:, 256:]], axis=0)
    high, low = halves(by_z)
    stacked = jnp.concatenate([high, low, high], axis=0)
    for j in range(8):
        block = dot(stacked, yi[:, 128 * j : 128 * j + 128], ((0,), (0,)))
        out[j] = block.astype(BF16)


def finish(got, direct, out, rows):
    for x in range(8):
        rows[256 * x : 256 * x + 256, :] = got[x].astype(F32)

    def body(z, carry):
        for o in range(C):
            spectral = rows[pl.ds(C * z + o, 8, stride=256), :]
            total = direct[z, 8 * o : 8 * o + 8, :] + spectral
            out[z, o] = gelu(total).astype(BF16)
        return carry

    lax.fori_loop(0, ZL, body, 0)


def turn_weights(weights, after, out, wide):
    for chunk in range(16):
        turned = weights[128 * chunk : 128 * chunk + 128, :].T
        for ri in range(2):
            wide[:, 16 * ri + chunk, :] = turned[64 * ri : 64 * ri + 64]
    out[...] = wide[...].astype(BF16)


def shards(fields, stiffness, lift_weight, lift_bias, mix_weight, spectral_weight, output_bias):
    table = {name: jnp.asarray(value) for name, value in tables().items()}
    everyone = ("gx", "gy", "ga")

    def exchange(value, axis):
        return lax.all_to_all(value, axis, split_axis=0, concat_axis=0, tiled=True)

    def shift(value, axis, by):
        return lax.ppermute(value, axis, [(i, (i + by) % 8) for i in range(8)])

    anywhere = pl.BlockSpec(memory_space=pl.ANY)
    f = fields.reshape(5, 128, 256)
    s = stiffness.reshape(128, 256)
    swap = [(0, 1), (1, 0)]
    fp, sp = lax.ppermute(f, "ga", swap), lax.ppermute(s, "ga", swap)
    copied = [pltpu.VMEM((2, 6, 2, 128, 128), F32)]
    [message] = call(pack_x, [((6, 2, 48, 128), F32)], [VMEM] * 4, copied)(f, s, fp, sp)
    across = [(2 * i, 2 * ((i - 1) % 8) + 1) for i in range(8)]
    across += [(2 * i + 1, 2 * ((i + 1) % 8)) for i in range(8)]
    got = lax.ppermute(message, ("gx", "ga"), across)

    turned = [pltpu.VMEM((64, 32, 128), F32)]
    [turned] = call(turn_weights, [((64, 32, 128), BF16)], [VMEM, anywhere], turned)(
        spectral_weight.reshape(2048, 128), message
    )
    weights = exchange(turned, ("gx", "gy"))

    message = ((3, 16, 128), F32)
    outer, low, high = call(pack_y, [((6, 2, 128, 128), F32), message, message], [VMEM] * 5)(
        f, s, fp, sp, got
    )
    ylow, yhigh = shift(low, "gy", -1), shift(high, "gy", 1)
    keep, send, narrow = call(
        stencil,
        [((160, 128), F32), ((160, 128), F32), ((8, 48, 128), BF16)],
        [VMEM] * 8 + [anywhere],
        [
            pltpu.VMEM((5, 16, 16, 384), F32),
            pltpu.VMEM((5, 16, 16, 384), F32),
            pltpu.VMEM((16, 16, 384), F32),
            pltpu.VMEM((5, 2, 128, 128), F32),
            pltpu.VMEM((320, 256), F32),
        ],
        mib=24,
    )(f, s, fp, sp, outer, ylow, yhigh, table["pairs"], weights)

    columns = exchange(narrow, "gy")
    spread = jnp.einsum("co,xy->oxcy", mix_weight, jnp.eye(8, dtype=BF16)).reshape(256, 256)
    obias = jnp.broadcast_to(jnp.repeat(output_bias, 8)[:, None], (256, 128))
    [direct] = call(
        pointwise,
        [((8, 256, 128), F32)],
        [VMEM, VMEM, SMEM, SMEM, VMEM, VMEM],
        [pltpu.VMEM((320, 128), F32)],
        flops=3 * 10**8,
    )(keep, lax.ppermute(send, "ga", swap), lift_weight, lift_bias, spread, obias)

    [modes] = call(
        forward,
        [((64, 4, 128), F32)],
        [VMEM, SMEM, SMEM, VMEM, VMEM],
        [pltpu.VMEM((256, 1024), BF16)],
    )(columns, lift_weight, lift_bias, table["yf"], table["zf"])
    modes = exchange(modes.reshape(128, 2, 128), everyone)
    [mixed] = call(mix_modes, [((64, 4, 128), F32)], [VMEM] * 3, mib=24)(
        modes.reshape(256, 128), weights, table["x"]
    )
    mixed = exchange(mixed.reshape(128, 2, 128), everyone)
    [spectral] = call(inverse, [((8, 256, 128), BF16)], [VMEM] * 3)(
        mixed.reshape(64, 4, 128), table["zi"], table["yi"]
    )
    spectral = exchange(spectral, "gy")
    [out] = call(
        finish, [((8, 32, 8, 128), BF16)], [VMEM] * 2, [pltpu.VMEM((2048, 128), F32)]
    )(spectral, direct)
    return out


def solution(mesh):
    placed = (
        P(None, "ga", "gx", "gy"),
        P("ga", "gx", "gy"),
        P(),
        P(),
        P(),
        P("ga", "gy", None, "gx", None),
        P(),
    )
    return jax.shard_map(
        shards, mesh=mesh, in_specs=placed, out_specs=P("ga", None, "gx", "gy"), check_vma=False
    )
```

```python
import functools
import math

import jax
import jax.numpy as jnp
import numpy as np
from jax import lax
from jax.experimental import pallas as pl
from jax.experimental.pallas import tpu as pltpu
from jax.sharding import PartitionSpec as P

NZ, C, MX, MY, MZ, GX, GY = 16, 32, 32, 64, 8, 64, 1024
ZL, XL, YL = 8, 16, 256
F32, BF16 = jnp.float32, jnp.bfloat16
ROOT = math.sqrt(2.0 / math.pi)
VMEM = pl.BlockSpec(memory_space=pltpu.VMEM)
SMEM = pl.BlockSpec(memory_space=pltpu.SMEM)


def cos_sin(freq, points, length):
    turn = np.mod(np.outer(freq, points), length) * (2.0 * np.pi / length)
    return np.cos(turn), np.sin(turn)


def split(table):
    table = np.asarray(table, np.float32)
    high = table.astype(jnp.bfloat16)
    low = (table - high.astype(np.float32)).astype(jnp.bfloat16)
    return high, low


@functools.cache
def tables():
    out = {}
    ky = np.arange(MY) - MY // 2
    cy, sy = cos_sin(ky, np.arange(GY), GY)
    rows = np.concatenate([cy, -sy]) / math.sqrt(GY)
    out["yf"] = np.concatenate(split(rows))
    rows = np.concatenate([cy, -sy]) / math.sqrt(GY)
    high, low = split(rows)
    out["yi"] = np.concatenate([high, high, low])
    kz = np.arange(MZ)
    cz, sz = (t / math.sqrt(NZ) for t in cos_sin(kz, np.arange(ZL), NZ))
    eye = np.eye(C)

    def kron_f(t):
        return np.einsum("kz,cd->czkd", t, eye).reshape(C * ZL, 2, 4 * C)

    zf = np.zeros((2, C * ZL, 2, 2, 4 * C))
    zf[0, :, :, 0], zf[1, :, :, 0] = kron_f(cz), kron_f(sz)
    zf[1, :, :, 1], zf[0, :, :, 1] = kron_f(cz), -kron_f(sz)
    out["zf"] = np.stack(split(zf.reshape(2 * C * ZL, 8 * 2 * C)))
    zi = np.zeros((2, 2, 4, C, 2, ZL, C))
    for half in range(2):
        for k in range(4):
            for z in range(ZL):
                c, s = cz[4 * half + k, z] * eye, sz[4 * half + k, z] * eye
                zi[half, 0, k, :, 0, z], zi[half, 1, k, :, 0, z] = c, -s
                zi[half, 1, k, :, 1, z], zi[half, 0, k, :, 1, z] = c, s
    out["zi"] = np.stack(split(zi.reshape(16 * C, 2 * ZL * C)))
    kx = np.arange(MX) - MX // 2
    cx, sx = cos_sin(kx, np.arange(GX), GX)
    cr = (cx / 8.0).astype(np.float32).astype(jnp.bfloat16).astype(np.float64)
    sr = (-sx / 8.0).astype(np.float32).astype(jnp.bfloat16).astype(np.float64)
    cr, sr = cr.reshape(8, 4, 8, 2, 4), sr.reshape(8, 4, 8, 2, 4)
    xf = np.zeros((4, 2, 8, 4, 4, 8, 4, 2, 2, 2))
    for k in range(4):
        for a in range(2):
            for h in range(2):
                sign = -1.0 if k * (h ^ a) % 2 else 1.0
                real, imag = sign * cr[:, :, :, a], sign * sr[:, :, :, a]
                xf[k, 0, :, k, :, :, :, h, a, 0] = real
                xf[k, 0, :, k, :, :, :, h, a, 1] = -imag
                xf[k, 1, :, k, :, :, :, h, a, 0] = imag
                xf[k, 1, :, k, :, :, :, h, a, 1] = real
    xf = xf.reshape(1024, 256).astype(np.float32).astype(jnp.bfloat16)
    ic, is_ = (cx / 8.0).T.reshape(GX, 8, 1, 4), (sx / 8.0).T.reshape(GX, 8, 1, 4)
    xi = np.zeros((2, GX, 2, 8, 4, 4))
    xi[0, :, 0], xi[0, :, 1] = ic, -is_
    xi[1, :, 0], xi[1, :, 1] = is_, ic
    out["x"] = np.concatenate([xf, *split(xi.reshape(128, 256))]).reshape(5, 256, 256)
    return out


def iotas(shape):
    return lax.broadcasted_iota(jnp.int32, shape, 0), lax.broadcasted_iota(jnp.int32, shape, 1)


def halves(value):
    high = value.astype(BF16)
    return high, (value - high.astype(F32)).astype(BF16)


def dot(a, b, contract=((1,), (0,))):
    return lax.dot_general(a, b, (contract, ((), ())), preferred_element_type=F32)


def dot3(a, b_ref):
    high, low = halves(a)
    return dot(high, b_ref[0]) + dot(low, b_ref[0]) + dot(high, b_ref[1])


def gelu(v):
    return 0.5 * v * (1.0 + jnp.tanh(ROOT * (v + 0.044715 * (v * v * v))))


def call(kernel, outs, in_specs, scratch=(), mib=16, flops=10**7, size=2**20):
    return pl.pallas_call(
        kernel,
        out_shape=[jax.ShapeDtypeStruct(s, d) for s, d in outs],
        in_specs=in_specs,
        out_specs=[VMEM] * len(outs),
        scratch_shapes=list(scratch),
        compiler_params=pltpu.CompilerParams(vmem_limit_bytes=mib << 20),
        cost_estimate=pl.CostEstimate(flops=flops, bytes_accessed=size, transcendentals=0),
    )


def rows_of(refs, field, slot, half):
    f, s, fp, sp = refs
    own, other = (s, sp) if field == 5 else (f.at[field], fp.at[field])
    start = 16 * (slot % 8) + 8 * half
    return (own if slot < 8 else other)[pl.ds(pl.multiple_of(start, 8), 8), :]


def edge_rows(f, s, out, rows):
    bottom = lax.axis_index("ga") == 0
    for field in range(6):
        for h in range(2):
            lanes = slice(128 * h, 128 * h + 128)
            rows[field, h] = s[:, lanes] if field == 5 else f[field, :, lanes]
            for d in range(3):
                first = rows[field, h, pl.ds(d, 8, stride=XL), :]
                last = rows[field, h, pl.ds(XL - 1 - d, 8, stride=XL), :]
                out[field, h, 8 * d : 8 * d + 8, :] = jnp.where(bottom, first, last)


def pack_own(f, s, own, rows):
    edge_rows(f, s, own, rows)


def pack_other(fp, sp, own, message, other, rows):
    edge_rows(fp, sp, other, rows)
    message[:, :, 0:24, :] = own[...]
    message[:, :, 24:48, :] = other[...]


def pack_y(f, s, fp, sp, message, outer, far, near):
    refs = (f, s, fp, sp)
    a = lax.axis_index("ga")
    row = lax.broadcasted_iota(jnp.int32, (8, 128), 0)
    beyond = jnp.where(a == 1, row, 7 - row) < 3
    lane = lax.broadcasted_iota(jnp.int32, (16, 128), 1) // 4
    lows, highs = jnp.zeros((16, 128), F32), jnp.zeros((16, 128), F32)
    for field in range(6):
        for h in range(2):
            for which in range(2):
                for d in range(3):
                    at = 24 * which + 8 * d
                    value = message[field, h, at : at + 8, :]
                    to = 64 * (1 - which)
                    outer[field, h, pl.ds(to + d, 8, stride=8), :] = value
                    outer[field, h, pl.ds(to + 7 - d, 8, stride=8), :] = value
        for slot in range(16):
            inner, block = rows_of(refs, field, slot, a), rows_of(refs, field, slot, 1 - a)
            edge = slice(8 * slot, 8 * slot + 8)
            for h in range(2):
                kept = block[:, 128 * h : 128 * h + 128]
                outer[field, h, edge, :] = jnp.where(beyond, outer[field, h, edge, :], kept)
            base = 64 * (field % 2) + 4 * slot
            here = lane == base // 4
            first = jnp.concatenate([inner[:, :128], outer[field, 0, edge, :]], axis=0)
            last = jnp.concatenate([inner[:, 128:], outer[field, 1, edge, :]], axis=0)
            lows = jnp.where(here, pltpu.roll(first, base, 1) if base else first, lows)
            highs = jnp.where(here, pltpu.roll(last, (base + 4) % 128, 1) if base != 124 else last, highs)
        if field % 2:
            even = lax.axis_index("gy") % 2 == 0
            far[field // 2] = jnp.where(even, lows, highs)
            near[field // 2] = jnp.where(even, highs, lows)


def stencil(f, s, fp, sp, outer, far, near, last, a, b, stiff):
    refs = (f, s, fp, sp)
    core = lax.axis_index("ga")
    even = lax.axis_index("gy") % 2 == 0
    first_lanes = lax.broadcasted_iota(jnp.int32, (16, 128), 1) < 64
    for field in range(6):
        for slot in range(16):
            to = stiff.at[slot] if field == 5 else a.at[field, slot]
            to[0:8, 0:256] = rows_of(refs, field, slot, core)
            for h in range(2):
                edge = outer[field, h, 8 * slot : 8 * slot + 8, :]
                to[8:16, 128 * h : 128 * h + 128] = edge
            base = 64 * (field % 2) + 4 * slot
            one, two = near[field // 2], far[field // 2]
            above, below = jnp.where(even, one, two), jnp.where(even, two, one)
            above = pltpu.roll(above, 128 - base, 1) if base else above
            below = pltpu.roll(below, 124 - base, 1) if base != 124 else below
            to[:, 256:384] = jnp.where(first_lanes, above, below)

    def advance(src, slot, crop):
        new, east, north, depth = [], [], [], []
        for field in range(5):
            mid = src[field, slot]
            up, down = src[field, (slot + 1) & 15], src[field, (slot + 15) & 15]
            xp, xm = pltpu.roll(mid, 15, 0), pltpu.roll(mid, 1, 0)
            yp, ym = pltpu.roll(mid, 383, 1), pltpu.roll(mid, 1, 1)
            if crop:
                mid, up, down, xp, xm, yp, ym = (
                    v[0:8, 0:256] for v in (mid, up, down, xp, xm, yp, ym)
                )
            total = 0.1 * mid + 0.12 * xp + 0.18 * xm + 0.17 * yp + 0.13 * ym
            new.append(total + 0.14 * up + 0.16 * down)
            east.append(xp - xm if field in (1, 4) else None)
            north.append(yp - ym if field in (2, 4) else None)
            depth.append(up - down if field in (3, 4) else None)
        div = 0.1 * (east[1] + north[2] + depth[3])
        new[0] = new[0] - div
        new[1] = new[1] - 0.1 * east[4]
        new[2] = new[2] - 0.1 * north[4]
        new[3] = new[3] - 0.1 * depth[4]
        new[4] = new[4] - (stiff[slot, 0:8, 0:256] if crop else stiff[slot]) * div
        return new

    for src, dst in ((a, b), (b, a), (a, None)):

        def body(slot, carry, src=src, dst=dst):
            new = advance(src, slot, dst is None)
            for field in range(5):
                if dst is None:
                    rows = pl.ds(pl.multiple_of(slot * 8, 8), 8)
                    for h in range(2):
                        last[field, h, rows, :] = new[field][:, 128 * h : 128 * h + 128]
                else:
                    dst[field, slot] = new[field]
            return carry

        lax.fori_loop(0, 16, body, 0)


def coarsen(last, after, keep, send, narrow, sums):
    for half in range(2):
        for x in range(4):
            for field in range(5):
                at = 160 * half + 40 * x + 8 * field
                for h in range(2):
                    even = last[field, h, pl.ds(64 * half + 2 * x, 8, stride=8), :]
                    odd = last[field, h, pl.ds(64 * half + 2 * x + 1, 8, stride=8), :]
                    sums[at : at + 8, 128 * h : 128 * h + 128] = even + odd
    value = sums[...]
    high = value.astype(BF16)
    rest = value - high.astype(F32)
    mid, low = halves(rest)
    row, lane = iotas((256, 128))
    table = jnp.where(row // 2 == lane, 0.25, 0.0).astype(BF16)
    mean = dot(high, table) + dot(mid, table) + dot(low, table)
    keep[...] = mean[:160]
    send[...] = mean[160:]
    for half in range(2):
        for x in range(4):
            at = 160 * half + 40 * x
            block = jnp.concatenate([mean[at : at + 40], jnp.zeros((8, 128), F32)], axis=0)
            narrow[2 * x + half] = block.astype(BF16)


def lift_rows(values, weight, bias):
    rows = []
    for c in range(C):
        v = bias[c] + values[0] * weight[0, c]
        for field in range(1, 5):
            v = v + values[field] * weight[field, c]
        rows.append(gelu(v))
    return jnp.concatenate(rows, axis=0).astype(BF16)


def pointwise(keep, got, weight, bias, mix, obias, out, wide):
    a = lax.axis_index("ga")
    wide[pl.ds(pl.multiple_of(160 * a, 8), 160), :] = keep[...]
    wide[pl.ds(pl.multiple_of(160 * (1 - a), 8), 160), :] = got[...]
    row, lane = iotas((256, 32))
    pick = (row // 8 == lane).astype(BF16)
    bias_o = jnp.sum(jnp.where(row // 8 == lane, obias[...], 0.0), axis=1, keepdims=True)
    by_row = dot(pick, mix[...], ((1,), (1,))).astype(BF16)
    row, lane = iotas((256, 256))
    spread = jnp.where(row % 8 == lane % 8, dot(by_row, pick, ((1,), (1,))), 0.0).astype(BF16)

    def body(z, carry):
        values = [wide[pl.ds(8 * field + z, 8, stride=40), :] for field in range(5)]
        out[z] = dot(spread, lift_rows(values, weight, bias)) + bias_o
        return carry

    lax.fori_loop(0, ZL, body, 0)


def forward(got, weight, bias, yf, zf, out, lifted):
    for j in range(8):
        block = got[j].astype(F32)
        values = [block[8 * field : 8 * field + 8] for field in range(5)]
        lifted[:, 128 * j : 128 * j + 128] = lift_rows(values, weight, bias)
    modes = dot(yf[...], lifted[...], ((1,), (1,)))
    modes = modes[:128] + modes[128:]
    modes = jnp.concatenate([modes[:64], modes[64:]], axis=1)
    result = dot3(modes, zf)
    for part in range(4):
        out[:, part, :] = result[:, 128 * part : 128 * part + 128]


def mix_modes(got, weights, x_tables, after, out):
    high, low = halves(got[...])
    row, lane = iotas((128, 128))
    modes = jnp.zeros((256, 128), F32)
    for k in range(4):
        spread = (row == 32 * k + lane // 4).astype(BF16)
        modes = modes + dot(x_tables[k], dot(high, spread).astype(BF16))
        modes = modes + dot(x_tables[k], dot(low, spread).astype(BF16))
    real, imag = modes[:128], modes[128:]
    total = jnp.zeros((256, 128), F32)
    for i in range(8):
        wr = weights[:, i, 0:16, :].astype(F32).reshape(128, 128)
        wi = weights[:, i, 16:32, :].astype(F32).reshape(128, 128)
        part = jnp.concatenate([wr * real - wi * imag, wr * imag + wi * real], axis=0)
        p_high, p_low = halves(part)
        gather = (lane % 32 == 4 * i + row % 4).astype(BF16)
        total = total + dot(p_high, gather) + dot(p_low, gather)
    row, lane = iotas((256, 128))
    total = jnp.where((row // 4) % 4 == lane // 32, total, 0.0)
    t_high, t_low = halves(total)
    back_high, back_low = x_tables[4, :128], x_tables[4, 128:]
    back = dot(back_high, t_high) + dot(back_high, t_low) + dot(back_low, t_high)
    odd = (lax.broadcasted_iota(jnp.int32, (64, 128), 1) // 32) % 2 == 1
    for ri in range(2):
        value = back[64 * ri : 64 * ri + 64]
        out[:, ri, :] = value
        out[:, 2 + ri, :] = jnp.where(odd, -value, value)


def inverse(got, zi, yi, out):
    modes = jnp.concatenate([got[:, part, :] for part in range(4)], axis=1)
    by_z = dot3(modes, zi)
    by_z = jnp.concatenate([by_z[:, :256], by_z[:, 256:]], axis=0)
    high, low = halves(by_z)
    stacked = jnp.concatenate([high, low, high], axis=0)
    for j in range(8):
        block = dot(stacked, yi[:, 128 * j : 128 * j + 128], ((0,), (0,)))
        out[j] = block.astype(BF16)


def finish(got, direct, out, rows):
    for x in range(8):
        rows[256 * x : 256 * x + 256, :] = got[x].astype(F32)

    def body(z, carry):
        for o in range(C):
            spectral = rows[pl.ds(C * z + o, 8, stride=256), :]
            total = direct[z, 8 * o : 8 * o + 8, :] + spectral
            out[z, o] = gelu(total).astype(BF16)
        return carry

    lax.fori_loop(0, ZL, body, 0)


def turn_weights(weights, after, out, wide):
    for chunk in range(16):
        turned = weights[128 * chunk : 128 * chunk + 128, :].T
        for ri in range(2):
            wide[:, 16 * ri + chunk, :] = turned[64 * ri : 64 * ri + 64]
    out[...] = wide[...].astype(BF16)


def shards(fields, stiffness, lift_weight, lift_bias, mix_weight, spectral_weight, output_bias):
    table = {name: jnp.asarray(value) for name, value in tables().items()}
    everyone = ("gx", "gy", "ga")

    def exchange(value, axis):
        return lax.all_to_all(value, axis, split_axis=0, concat_axis=0, tiled=True)

    anywhere = pl.BlockSpec(memory_space=pl.ANY)
    f = fields.reshape(5, 128, 256)
    s = stiffness.reshape(128, 256)
    swap = [(0, 1), (1, 0)]
    fp, sp = lax.ppermute(f, "ga", swap), lax.ppermute(s, "ga", swap)
    rows = pltpu.VMEM((6, 2, 128, 128), F32)
    edges = ((6, 2, 24, 128), F32)
    [own] = call(pack_own, [edges], [VMEM] * 2, [rows])(f, s)
    [message] = call(
        pack_other, [((6, 2, 48, 128), F32)], [VMEM] * 3, [pltpu.VMEM(*edges), rows]
    )(fp, sp, own)
    across = [(2 * i, 2 * ((i - 1) % 8) + 1) for i in range(8)]
    across += [(2 * i + 1, 2 * ((i + 1) % 8)) for i in range(8)]
    got = lax.ppermute(message, ("gx", "ga"), across)

    [turned] = call(
        turn_weights,
        [((64, 32, 128), BF16)],
        [VMEM, anywhere],
        [pltpu.VMEM((64, 32, 128), F32)],
        size=2 * 10**7,
    )(spectral_weight.reshape(2048, 128), message)
    hop = exchange(turned.reshape(8, 8, 32, 128), "gx")
    weights = exchange(jnp.transpose(hop, (1, 0, 2, 3)), "gy")

    message = ((3, 16, 128), F32)
    outer, far, near = call(
        pack_y, [((6, 2, 128, 128), F32), message, message], [VMEM] * 5, flops=10**12
    )(f, s, fp, sp, got)
    far = lax.ppermute(far, "gy", [(j, (j - 1 + 2 * (j % 2)) % 8) for j in range(8)])
    near = lax.ppermute(near, "gy", [(j, j + 1 - 2 * (j % 2)) for j in range(8)])
    [last] = call(
        stencil,
        [((5, 2, 128, 128), F32)],
        [VMEM] * 7,
        [
            pltpu.VMEM((5, 16, 16, 384), F32),
            pltpu.VMEM((5, 16, 16, 384), F32),
            pltpu.VMEM((16, 16, 384), F32),
        ],
        flops=10**12,
    )(f, s, fp, sp, outer, far, near)
    keep, send, narrow = call(
        coarsen,
        [((160, 128), F32), ((160, 128), F32), ((8, 48, 128), BF16)],
        [VMEM, anywhere],
        [pltpu.VMEM((320, 256), F32)],
    )(last, weights)

    columns = exchange(narrow, "gy")
    [direct] = call(
        pointwise,
        [((8, 256, 128), F32)],
        [VMEM, VMEM, SMEM, SMEM, VMEM, VMEM],
        [pltpu.VMEM((320, 128), F32)],
        flops=3 * 10**8,
    )(keep, lax.ppermute(send, "ga", swap), lift_weight, lift_bias, mix_weight, output_bias.reshape(1, C))

    [modes] = call(
        forward,
        [((64, 4, 128), F32)],
        [VMEM, SMEM, SMEM, VMEM, VMEM],
        [pltpu.VMEM((256, 1024), BF16)],
    )(columns, lift_weight, lift_bias, table["yf"], table["zf"])
    modes = exchange(modes.reshape(128, 2, 128), everyone)
    [mixed] = call(mix_modes, [((64, 4, 128), F32)], [VMEM] * 3 + [anywhere])(
        modes.reshape(256, 128), weights, table["x"], direct
    )
    mixed = exchange(mixed.reshape(128, 2, 128), everyone)
    [spectral] = call(inverse, [((8, 256, 128), BF16)], [VMEM] * 3)(
        mixed.reshape(64, 4, 128), table["zi"], table["yi"]
    )
    spectral = exchange(spectral, "gy")
    [out] = call(
        finish, [((8, 32, 8, 128), BF16)], [VMEM] * 2, [pltpu.VMEM((2048, 128), F32)]
    )(spectral, direct)
    return out


def solution(mesh):
    placed = (
        P(None, "ga", "gx", "gy"),
        P("ga", "gx", "gy"),
        P(),
        P(),
        P(),
        P("ga", "gy", None, "gx", None),
        P(),
    )
    return jax.shard_map(
        shards, mesh=mesh, in_specs=placed, out_specs=P("ga", None, "gx", "gy"), check_vma=False
    )
```

```python
import functools
import math

import jax
import jax.numpy as jnp
import numpy as np
from jax import lax
from jax.experimental import pallas as pl
from jax.experimental.pallas import tpu as pltpu
from jax.sharding import PartitionSpec as P

NZ, C, MX, MY, MZ, GX, GY = 16, 32, 32, 64, 8, 64, 1024
ZL, XL, YL = 8, 16, 256
F32, BF16 = jnp.float32, jnp.bfloat16
ROOT = math.sqrt(2.0 / math.pi)
VMEM = pl.BlockSpec(memory_space=pltpu.VMEM)
SMEM = pl.BlockSpec(memory_space=pltpu.SMEM)


def cos_sin(freq, points, length):
    turn = np.mod(np.outer(freq, points), length) * (2.0 * np.pi / length)
    return np.cos(turn), np.sin(turn)


def split(table):
    table = np.asarray(table, np.float32)
    high = table.astype(jnp.bfloat16)
    low = (table - high.astype(np.float32)).astype(jnp.bfloat16)
    return high, low


@functools.cache
def tables():
    out = {}
    ky = np.arange(MY) - MY // 2
    cy, sy = cos_sin(ky, np.arange(GY), GY)
    rows = np.concatenate([cy, -sy]) / math.sqrt(GY)
    out["yf"] = np.concatenate(split(rows))
    rows = np.concatenate([cy, -sy]) / math.sqrt(GY)
    high, low = split(rows)
    out["yi"] = np.concatenate([high, high, low])
    kz = np.arange(MZ)
    cz, sz = (t / math.sqrt(NZ) for t in cos_sin(kz, np.arange(ZL), NZ))
    eye = np.eye(C)

    def kron_f(t):
        return np.einsum("kz,cd->czkd", t, eye).reshape(C * ZL, 2, 4 * C)

    zf = np.zeros((2, C * ZL, 2, 2, 4 * C))
    zf[0, :, :, 0], zf[1, :, :, 0] = kron_f(cz), kron_f(sz)
    zf[1, :, :, 1], zf[0, :, :, 1] = kron_f(cz), -kron_f(sz)
    out["zf"] = np.stack(split(zf.reshape(2 * C * ZL, 8 * 2 * C)))
    zi = np.zeros((2, 2, 4, C, 2, ZL, C))
    for half in range(2):
        for k in range(4):
            for z in range(ZL):
                c, s = cz[4 * half + k, z] * eye, sz[4 * half + k, z] * eye
                zi[half, 0, k, :, 0, z], zi[half, 1, k, :, 0, z] = c, -s
                zi[half, 1, k, :, 1, z], zi[half, 0, k, :, 1, z] = c, s
    out["zi"] = np.stack(split(zi.reshape(16 * C, 2 * ZL * C)))
    kx = np.arange(MX) - MX // 2
    cx, sx = cos_sin(kx, np.arange(GX), GX)
    cr = (cx / 8.0).astype(np.float32).astype(jnp.bfloat16).astype(np.float64)
    sr = (-sx / 8.0).astype(np.float32).astype(jnp.bfloat16).astype(np.float64)
    cr, sr = cr.reshape(8, 4, 8, 2, 4), sr.reshape(8, 4, 8, 2, 4)
    xf = np.zeros((4, 2, 8, 4, 4, 8, 4, 2, 2, 2))
    for k in range(4):
        for a in range(2):
            for h in range(2):
                sign = -1.0 if k * (h ^ a) % 2 else 1.0
                real, imag = sign * cr[:, :, :, a], sign * sr[:, :, :, a]
                xf[k, 0, :, k, :, :, :, h, a, 0] = real
                xf[k, 0, :, k, :, :, :, h, a, 1] = -imag
                xf[k, 1, :, k, :, :, :, h, a, 0] = imag
                xf[k, 1, :, k, :, :, :, h, a, 1] = real
    xf = xf.reshape(1024, 256).astype(np.float32).astype(jnp.bfloat16)
    ic, is_ = (cx / 8.0).T.reshape(GX, 8, 1, 4), (sx / 8.0).T.reshape(GX, 8, 1, 4)
    xi = np.zeros((2, GX, 2, 8, 4, 4))
    xi[0, :, 0], xi[0, :, 1] = ic, -is_
    xi[1, :, 0], xi[1, :, 1] = is_, ic
    out["x"] = np.concatenate([xf, *split(xi.reshape(128, 256))]).reshape(5, 256, 256)
    return out


def iotas(shape):
    return lax.broadcasted_iota(jnp.int32, shape, 0), lax.broadcasted_iota(jnp.int32, shape, 1)


def halves(value):
    high = value.astype(BF16)
    return high, (value - high.astype(F32)).astype(BF16)


def dot(a, b, contract=((1,), (0,))):
    return lax.dot_general(a, b, (contract, ((), ())), preferred_element_type=F32)


def dot3(a, b_ref):
    high, low = halves(a)
    return dot(high, b_ref[0]) + dot(low, b_ref[0]) + dot(high, b_ref[1])


def gelu(v):
    return 0.5 * v * (1.0 + jnp.tanh(ROOT * (v + 0.044715 * (v * v * v))))


def call(kernel, outs, in_specs, scratch=(), mib=16, flops=10**7, size=2**20):
    return pl.pallas_call(
        kernel,
        out_shape=[jax.ShapeDtypeStruct(s, d) for s, d in outs],
        in_specs=in_specs,
        out_specs=[VMEM] * len(outs),
        scratch_shapes=list(scratch),
        compiler_params=pltpu.CompilerParams(vmem_limit_bytes=mib << 20),
        cost_estimate=pl.CostEstimate(flops=flops, bytes_accessed=size, transcendentals=0),
    )


def rows_of(refs, field, slot, half):
    f, s, fp, sp = refs
    own, other = (s, sp) if field == 5 else (f.at[field], fp.at[field])
    start = 16 * (slot % 8) + 8 * half
    return (own if slot < 8 else other)[pl.ds(pl.multiple_of(start, 8), 8), :]


def edge_rows(f, s, out, rows):
    bottom = lax.axis_index("ga") == 0
    for field in range(6):
        for h in range(2):
            lanes = slice(128 * h, 128 * h + 128)
            rows[field, h] = s[:, lanes] if field == 5 else f[field, :, lanes]
            for d in range(3):
                first = rows[field, h, pl.ds(d, 8, stride=XL), :]
                last = rows[field, h, pl.ds(XL - 1 - d, 8, stride=XL), :]
                out[field, h, 8 * d : 8 * d + 8, :] = jnp.where(bottom, first, last)


def pack_own(f, s, own, rows):
    edge_rows(f, s, own, rows)


def pack_other(fp, sp, own, message, other, rows):
    edge_rows(fp, sp, other, rows)
    message[:, :, 0:24, :] = own[...]
    message[:, :, 24:48, :] = other[...]


def pack_y(f, s, fp, sp, message, outer, far, near):
    refs = (f, s, fp, sp)
    a = lax.axis_index("ga")
    row = lax.broadcasted_iota(jnp.int32, (8, 128), 0)
    beyond = jnp.where(a == 1, row, 7 - row) < 3
    lane = lax.broadcasted_iota(jnp.int32, (16, 128), 1) // 4
    lows, highs = jnp.zeros((16, 128), F32), jnp.zeros((16, 128), F32)
    for field in range(6):
        for h in range(2):
            for which in range(2):
                for d in range(3):
                    at = 24 * which + 8 * d
                    value = message[field, h, at : at + 8, :]
                    to = 64 * (1 - which)
                    outer[field, h, pl.ds(to + d, 8, stride=8), :] = value
                    outer[field, h, pl.ds(to + 7 - d, 8, stride=8), :] = value
        for slot in range(16):
            inner, block = rows_of(refs, field, slot, a), rows_of(refs, field, slot, 1 - a)
            edge = slice(8 * slot, 8 * slot + 8)
            for h in range(2):
                kept = block[:, 128 * h : 128 * h + 128]
                outer[field, h, edge, :] = jnp.where(beyond, outer[field, h, edge, :], kept)
            base = 64 * (field % 2) + 4 * slot
            here = lane == base // 4
            first = jnp.concatenate([inner[:, :128], outer[field, 0, edge, :]], axis=0)
            last = jnp.concatenate([inner[:, 128:], outer[field, 1, edge, :]], axis=0)
            lows = jnp.where(here, pltpu.roll(first, base, 1) if base else first, lows)
            highs = jnp.where(here, pltpu.roll(last, (base + 4) % 128, 1) if base != 124 else last, highs)
        if field % 2:
            even = lax.axis_index("gy") % 2 == 0
            far[field // 2] = jnp.where(even, lows, highs)
            near[field // 2] = jnp.where(even, highs, lows)


def stencil(f, s, fp, sp, outer, far, near, last, a, b, stiff):
    refs = (f, s, fp, sp)
    core = lax.axis_index("ga")
    even = lax.axis_index("gy") % 2 == 0
    first_lanes = lax.broadcasted_iota(jnp.int32, (16, 128), 1) < 64
    for field in range(6):
        for slot in range(16):
            to = stiff.at[slot] if field == 5 else a.at[field, slot]
            to[0:8, 0:256] = rows_of(refs, field, slot, core)
            for h in range(2):
                edge = outer[field, h, 8 * slot : 8 * slot + 8, :]
                to[8:16, 128 * h : 128 * h + 128] = edge
            base = 64 * (field % 2) + 4 * slot
            one, two = near[field // 2], far[field // 2]
            above, below = jnp.where(even, one, two), jnp.where(even, two, one)
            above = pltpu.roll(above, 128 - base, 1) if base else above
            below = pltpu.roll(below, 124 - base, 1) if base != 124 else below
            to[:, 256:384] = jnp.where(first_lanes, above, below)

    def advance(src, slot, crop):
        new, east, north, depth = [], [], [], []
        for field in range(5):
            mid = src[field, slot]
            up, down = src[field, (slot + 1) & 15], src[field, (slot + 15) & 15]
            xp, xm = pltpu.roll(mid, 15, 0), pltpu.roll(mid, 1, 0)
            yp, ym = pltpu.roll(mid, 383, 1), pltpu.roll(mid, 1, 1)
            if crop:
                mid, up, down, xp, xm, yp, ym = (
                    v[0:8, 0:256] for v in (mid, up, down, xp, xm, yp, ym)
                )
            total = 0.1 * mid + 0.12 * xp + 0.18 * xm + 0.17 * yp + 0.13 * ym
            new.append(total + 0.14 * up + 0.16 * down)
            east.append(xp - xm if field in (1, 4) else None)
            north.append(yp - ym if field in (2, 4) else None)
            depth.append(up - down if field in (3, 4) else None)
        div = 0.1 * (east[1] + north[2] + depth[3])
        new[0] = new[0] - div
        new[1] = new[1] - 0.1 * east[4]
        new[2] = new[2] - 0.1 * north[4]
        new[3] = new[3] - 0.1 * depth[4]
        new[4] = new[4] - (stiff[slot, 0:8, 0:256] if crop else stiff[slot]) * div
        return new

    for src, dst in ((a, b), (b, a), (a, None)):

        def body(slot, carry, src=src, dst=dst):
            new = advance(src, slot, dst is None)
            for field in range(5):
                if dst is None:
                    rows = pl.ds(pl.multiple_of(slot * 8, 8), 8)
                    for h in range(2):
                        last[field, h, rows, :] = new[field][:, 128 * h : 128 * h + 128]
                else:
                    dst[field, slot] = new[field]
            return carry

        lax.fori_loop(0, 16, body, 0)


def coarsen(last, weights, keep, send, narrow, sums):
    for half in range(2):
        for x in range(4):
            for field in range(5):
                at = 160 * half + 40 * x + 8 * field
                for h in range(2):
                    even = last[field, h, pl.ds(64 * half + 2 * x, 8, stride=8), :]
                    odd = last[field, h, pl.ds(64 * half + 2 * x + 1, 8, stride=8), :]
                    sums[at : at + 8, 128 * h : 128 * h + 128] = even + odd
    value = sums[...]
    high = value.astype(BF16)
    rest = value - high.astype(F32)
    mid, low = halves(rest)
    row, lane = iotas((256, 128))
    table = jnp.where(row // 2 == lane, 0.25, 0.0).astype(BF16)
    mean = dot(high, table) + dot(mid, table) + dot(low, table)
    keep[...] = mean[:160]
    send[...] = mean[160:]
    for half in range(2):
        for x in range(4):
            at = 160 * half + 40 * x
            block = jnp.concatenate([mean[at : at + 40], jnp.zeros((8, 128), F32)], axis=0)
            narrow[2 * x + half, 0:48, :] = block.astype(BF16)
    for i in range(8):
        narrow[:, 48 + 32 * i : 80 + 32 * i, :] = weights[i]


def lift_rows(values, weight, bias):
    rows = []
    for c in range(C):
        v = bias[c] + values[0] * weight[0, c]
        for field in range(1, 5):
            v = v + values[field] * weight[field, c]
        rows.append(gelu(v))
    return jnp.concatenate(rows, axis=0).astype(BF16)


def pointwise(keep, got, weight, bias, mix, obias, out, wide):
    a = lax.axis_index("ga")
    wide[pl.ds(pl.multiple_of(160 * a, 8), 160), :] = keep[...]
    wide[pl.ds(pl.multiple_of(160 * (1 - a), 8), 160), :] = got[...]
    row, lane = iotas((256, 32))
    pick = (row // 8 == lane).astype(BF16)
    bias_o = jnp.sum(jnp.where(row // 8 == lane, obias[...], 0.0), axis=1, keepdims=True)
    by_row = dot(pick, mix[...], ((1,), (1,))).astype(BF16)
    row, lane = iotas((256, 256))
    spread = jnp.where(row % 8 == lane % 8, dot(by_row, pick, ((1,), (1,))), 0.0).astype(BF16)

    def body(z, carry):
        values = [wide[pl.ds(8 * field + z, 8, stride=40), :] for field in range(5)]
        out[z] = dot(spread, lift_rows(values, weight, bias)) + bias_o
        return carry

    lax.fori_loop(0, ZL, body, 0)


def forward(got, weight, bias, yf_far, zf_far, out, lifted, yf, zf, sems):
    copies = [
        pltpu.make_async_copy(yf_far, yf, sems.at[0]),
        pltpu.make_async_copy(zf_far, zf, sems.at[1]),
    ]
    for copy in copies:
        copy.start()
    for j in range(8):
        block = got[j, 0:48, :].astype(F32)
        values = [block[8 * field : 8 * field + 8] for field in range(5)]
        lifted[:, 128 * j : 128 * j + 128] = lift_rows(values, weight, bias)
    copies[0].wait()
    modes = dot(yf[...], lifted[...], ((1,), (1,)))
    modes = modes[:128] + modes[128:]
    modes = jnp.concatenate([modes[:64], modes[64:]], axis=1)
    copies[1].wait()
    result = dot3(modes, zf)
    for part in range(4):
        out[:, part, :] = result[:, 128 * part : 128 * part + 128]


def mix_modes(got, weights, x_tables, after, out):
    high, low = halves(got[...])
    row, lane = iotas((128, 128))
    modes = jnp.zeros((256, 128), F32)
    for k in range(4):
        spread = (row == 32 * k + lane // 4).astype(BF16)
        modes = modes + dot(x_tables[k], dot(high, spread).astype(BF16))
        modes = modes + dot(x_tables[k], dot(low, spread).astype(BF16))
    real, imag = modes[:128], modes[128:]
    total = jnp.zeros((256, 128), F32)
    for i in range(8):
        at = 48 + 32 * i
        wr = weights[:, at : at + 16, :].astype(F32).reshape(128, 128)
        wi = weights[:, at + 16 : at + 32, :].astype(F32).reshape(128, 128)
        part = jnp.concatenate([wr * real - wi * imag, wr * imag + wi * real], axis=0)
        p_high, p_low = halves(part)
        gather = (lane % 32 == 4 * i + row % 4).astype(BF16)
        total = total + dot(p_high, gather) + dot(p_low, gather)
    row, lane = iotas((256, 128))
    total = jnp.where((row // 4) % 4 == lane // 32, total, 0.0)
    t_high, t_low = halves(total)
    back_high, back_low = x_tables[4, :128], x_tables[4, 128:]
    back = dot(back_high, t_high) + dot(back_high, t_low) + dot(back_low, t_high)
    odd = (lax.broadcasted_iota(jnp.int32, (64, 128), 1) // 32) % 2 == 1
    for ri in range(2):
        value = back[64 * ri : 64 * ri + 64]
        out[:, ri, :] = value
        out[:, 2 + ri, :] = jnp.where(odd, -value, value)


def inverse(got, zi, yi, out):
    modes = jnp.concatenate([got[:, part, :] for part in range(4)], axis=1)
    by_z = dot3(modes, zi)
    by_z = jnp.concatenate([by_z[:, :256], by_z[:, 256:]], axis=0)
    high, low = halves(by_z)
    stacked = jnp.concatenate([high, low, high], axis=0)
    for j in range(8):
        block = dot(stacked, yi[:, 128 * j : 128 * j + 128], ((0,), (0,)))
        out[j] = block.astype(BF16)


def finish(got, direct, out, rows):
    for x in range(8):
        rows[256 * x : 256 * x + 256, :] = got[x].astype(F32)

    def body(z, carry):
        for o in range(C):
            spectral = rows[pl.ds(C * z + o, 8, stride=256), :]
            total = direct[z, 8 * o : 8 * o + 8, :] + spectral
            out[z, o] = gelu(total).astype(BF16)
        return carry

    lax.fori_loop(0, ZL, body, 0)


def turn_weights(weights, after, out, wide):
    for chunk in range(16):
        turned = weights[128 * chunk : 128 * chunk + 128, :].T
        for ri in range(2):
            wide[:, 16 * ri + chunk, :] = turned[64 * ri : 64 * ri + 64]
    out[...] = wide[...].astype(BF16)


def shards(fields, stiffness, lift_weight, lift_bias, mix_weight, spectral_weight, output_bias):
    table = {name: jnp.asarray(value) for name, value in tables().items()}
    everyone = ("gx", "gy", "ga")

    def exchange(value, axis):
        return lax.all_to_all(value, axis, split_axis=0, concat_axis=0, tiled=True)

    anywhere = pl.BlockSpec(memory_space=pl.ANY)
    f = fields.reshape(5, 128, 256)
    s = stiffness.reshape(128, 256)
    swap = [(0, 1), (1, 0)]
    fp, sp = lax.ppermute(f, "ga", swap), lax.ppermute(s, "ga", swap)
    rows = pltpu.VMEM((6, 2, 128, 128), F32)
    edges = ((6, 2, 24, 128), F32)
    [own] = call(pack_own, [edges], [VMEM] * 2, [rows])(f, s)
    [message] = call(
        pack_other, [((6, 2, 48, 128), F32)], [VMEM] * 3, [pltpu.VMEM(*edges), rows]
    )(fp, sp, own)
    across = [(2 * i, 2 * ((i - 1) % 8) + 1) for i in range(8)]
    across += [(2 * i + 1, 2 * ((i + 1) % 8)) for i in range(8)]
    got = lax.ppermute(message, ("gx", "ga"), across)

    [turned] = call(
        turn_weights,
        [((64, 32, 128), BF16)],
        [VMEM, anywhere],
        [pltpu.VMEM((64, 32, 128), F32)],
        size=2 * 10**7,
    )(spectral_weight.reshape(2048, 128), message)
    hop = exchange(turned.reshape(8, 8, 32, 128), "gx")

    message = ((3, 16, 128), F32)
    outer, far, near = call(
        pack_y, [((6, 2, 128, 128), F32), message, message], [VMEM] * 5, flops=10**12
    )(f, s, fp, sp, got)
    far = lax.ppermute(far, "gy", [(j, (j - 1 + 2 * (j % 2)) % 8) for j in range(8)])
    near = lax.ppermute(near, "gy", [(j, j + 1 - 2 * (j % 2)) for j in range(8)])
    [last] = call(
        stencil,
        [((5, 2, 128, 128), F32)],
        [VMEM] * 7,
        [
            pltpu.VMEM((5, 16, 16, 384), F32),
            pltpu.VMEM((5, 16, 16, 384), F32),
            pltpu.VMEM((16, 16, 384), F32),
        ],
        flops=10**12,
    )(f, s, fp, sp, outer, far, near)
    keep, send, narrow = call(
        coarsen,
        [((160, 128), F32), ((160, 128), F32), ((8, 304, 128), BF16)],
        [VMEM] * 2,
        [pltpu.VMEM((320, 256), F32)],
    )(last, hop)

    columns = exchange(narrow, "gy")
    [direct] = call(
        pointwise,
        [((8, 256, 128), F32)],
        [VMEM, VMEM, SMEM, SMEM, VMEM, VMEM],
        [pltpu.VMEM((320, 128), F32)],
        flops=3 * 10**8,
    )(keep, lax.ppermute(send, "ga", swap), lift_weight, lift_bias, mix_weight, output_bias.reshape(1, C))

    [modes] = call(
        forward,
        [((64, 4, 128), F32)],
        [VMEM, SMEM, SMEM, anywhere, anywhere],
        [
            pltpu.VMEM((256, 1024), BF16),
            pltpu.VMEM((256, 1024), BF16),
            pltpu.VMEM((2, 512, 512), BF16),
            pltpu.SemaphoreType.DMA((2,)),
        ],
    )(columns, lift_weight, lift_bias, table["yf"], table["zf"])
    modes = exchange(modes.reshape(128, 2, 128), everyone)
    [mixed] = call(mix_modes, [((64, 4, 128), F32)], [VMEM] * 3 + [anywhere])(
        modes.reshape(256, 128), columns, table["x"], direct
    )
    mixed = exchange(mixed.reshape(128, 2, 128), everyone)
    [spectral] = call(inverse, [((8, 256, 128), BF16)], [VMEM] * 3)(
        mixed.reshape(64, 4, 128), table["zi"], table["yi"]
    )
    spectral = exchange(spectral, "gy")
    [out] = call(
        finish, [((8, 32, 8, 128), BF16)], [VMEM] * 2, [pltpu.VMEM((2048, 128), F32)]
    )(spectral, direct)
    return out


def solution(mesh):
    placed = (
        P(None, "ga", "gx", "gy"),
        P("ga", "gx", "gy"),
        P(),
        P(),
        P(),
        P("ga", "gy", None, "gx", None),
        P(),
    )
    return jax.shard_map(
        shards, mesh=mesh, in_specs=placed, out_specs=P("ga", None, "gx", "gy"), check_vma=False
    )
```

```python
import functools
import math

import jax
import jax.numpy as jnp
import numpy as np
from jax import lax
from jax.experimental import pallas as pl
from jax.experimental.pallas import tpu as pltpu
from jax.sharding import PartitionSpec as P

NZ, C, MX, MY, MZ, GX, GY = 16, 32, 32, 64, 8, 64, 1024
ZL, XL, YL = 8, 16, 256
F32, BF16 = jnp.float32, jnp.bfloat16
ROOT = math.sqrt(2.0 / math.pi)
VMEM = pl.BlockSpec(memory_space=pltpu.VMEM)
SMEM = pl.BlockSpec(memory_space=pltpu.SMEM)


def cos_sin(freq, points, length):
    turn = np.mod(np.outer(freq, points), length) * (2.0 * np.pi / length)
    return np.cos(turn), np.sin(turn)


def split(table):
    table = np.asarray(table, np.float32)
    high = table.astype(jnp.bfloat16)
    low = (table - high.astype(np.float32)).astype(jnp.bfloat16)
    return high, low


@functools.cache
def tables():
    out = {}
    ky = np.arange(MY) - MY // 2
    cy, sy = cos_sin(ky, np.arange(GY), GY)
    rows = np.concatenate([cy, -sy]) / math.sqrt(GY)
    out["yf"] = np.concatenate(split(rows)).reshape(256, 8, 128).transpose(1, 0, 2)
    rows = np.concatenate([cy, -sy]) / math.sqrt(GY)
    high, low = split(rows)
    out["yi"] = np.concatenate([high, high, low])
    cf, sf = (
        np.einsum("kz,cd->czkd", w / math.sqrt(NZ), np.eye(8)).reshape(128, 2, 32)
        for w in cos_sin(np.arange(MZ), np.arange(NZ), NZ)
    )
    zf = np.zeros((2, 128, 2, 2, 32))
    zf[0, :, :, 0], zf[1, :, :, 0], zf[1, :, :, 1], zf[0, :, :, 1] = cf, sf, cf, -sf
    out["zf"] = np.concatenate(split(zf.reshape(256, 128)), axis=1)
    cz, sz = (w / math.sqrt(NZ) for w in cos_sin(np.arange(MZ), np.arange(ZL), NZ))
    eye = np.eye(C)
    zi = np.zeros((2, 2, 4, C, 2, ZL, C))
    for half in range(2):
        for k in range(4):
            for z in range(ZL):
                c, s = cz[4 * half + k, z] * eye, sz[4 * half + k, z] * eye
                zi[half, 0, k, :, 0, z], zi[half, 1, k, :, 0, z] = c, -s
                zi[half, 1, k, :, 1, z], zi[half, 0, k, :, 1, z] = c, s
    out["zi"] = np.stack(split(zi.reshape(16 * C, 2 * ZL * C)))
    kx = np.arange(MX) - MX // 2
    cx, sx = cos_sin(kx, np.arange(GX), GX)
    cr = (cx / 8.0).astype(np.float32).astype(jnp.bfloat16).astype(np.float64)
    sr = (-sx / 8.0).astype(np.float32).astype(jnp.bfloat16).astype(np.float64)
    cr, sr = cr.reshape(8, 4, 8, 2, 4), sr.reshape(8, 4, 8, 2, 4)
    xf = np.zeros((4, 2, 8, 4, 4, 8, 2, 4, 2))
    for k in range(4):
        for a in range(2):
            sign = -1.0 if k * a % 2 else 1.0
            real, imag = sign * cr[:, :, :, a], sign * sr[:, :, :, a]
            xf[k, 0, :, k, :, :, a, :, 0], xf[k, 0, :, k, :, :, a, :, 1] = real, -imag
            xf[k, 1, :, k, :, :, a, :, 0], xf[k, 1, :, k, :, :, a, :, 1] = imag, real
    out["xf"] = xf.reshape(4, 256, 128).astype(np.float32).astype(jnp.bfloat16)
    ic, is_ = (cx / 8.0).T.reshape(GX, 8, 1, 4), (sx / 8.0).T.reshape(GX, 8, 1, 4)
    xi = np.zeros((2, GX, 2, 8, 4, 4))
    xi[0, :, 0], xi[0, :, 1] = ic, -is_
    xi[1, :, 0], xi[1, :, 1] = is_, ic
    out["xi"] = np.stack(split(xi.reshape(128, 256)))
    return out


def iotas(shape):
    return lax.broadcasted_iota(jnp.int32, shape, 0), lax.broadcasted_iota(jnp.int32, shape, 1)


def halves(value):
    high = value.astype(BF16)
    return high, (value - high.astype(F32)).astype(BF16)


def dot(a, b, contract=((1,), (0,))):
    return lax.dot_general(a, b, (contract, ((), ())), preferred_element_type=F32)


def dot3(a, b_ref):
    high, low = halves(a)
    return dot(high, b_ref[0]) + dot(low, b_ref[0]) + dot(high, b_ref[1])


def gelu(v):
    return 0.5 * v * (1.0 + jnp.tanh(ROOT * (v + 0.044715 * (v * v * v))))


def call(kernel, outs, in_specs, scratch=(), mib=16, flops=10**7, size=2**20):
    return pl.pallas_call(
        kernel,
        out_shape=[jax.ShapeDtypeStruct(s, d) for s, d in outs],
        in_specs=in_specs,
        out_specs=[VMEM] * len(outs),
        scratch_shapes=list(scratch),
        compiler_params=pltpu.CompilerParams(vmem_limit_bytes=mib << 20),
        cost_estimate=pl.CostEstimate(flops=flops, bytes_accessed=size, transcendentals=0),
    )


def rows_of(refs, field, slot, half):
    f, s, fp, sp = refs
    own, other = (s, sp) if field == 5 else (f.at[field], fp.at[field])
    start = 16 * (slot % 8) + 8 * half
    return (own if slot < 8 else other)[pl.ds(pl.multiple_of(start, 8), 8), :]


def edge_rows(f, s, out, rows):
    bottom = lax.axis_index("ga") == 0
    for field in range(6):
        for h in range(2):
            lanes = slice(128 * h, 128 * h + 128)
            rows[field, h] = s[:, lanes] if field == 5 else f[field, :, lanes]
            for d in range(3):
                first = rows[field, h, pl.ds(d, 8, stride=XL), :]
                last = rows[field, h, pl.ds(XL - 1 - d, 8, stride=XL), :]
                out[field, h, 8 * d : 8 * d + 8, :] = jnp.where(bottom, first, last)


def pack_own(f, s, own, rows):
    edge_rows(f, s, own, rows)


def pack_other(fp, sp, own, message, other, rows):
    edge_rows(fp, sp, other, rows)
    message[:, :, 0:24, :] = own[...]
    message[:, :, 24:48, :] = other[...]


def pack_y(f, s, fp, sp, message, outer, far, near):
    refs = (f, s, fp, sp)
    a = lax.axis_index("ga")
    row = lax.broadcasted_iota(jnp.int32, (8, 128), 0)
    beyond = jnp.where(a == 1, row, 7 - row) < 3
    lane = lax.broadcasted_iota(jnp.int32, (16, 128), 1) // 4
    lows, highs = jnp.zeros((16, 128), F32), jnp.zeros((16, 128), F32)
    for field in range(6):
        for h in range(2):
            for which in range(2):
                for d in range(3):
                    at = 24 * which + 8 * d
                    value = message[field, h, at : at + 8, :]
                    to = 64 * (1 - which)
                    outer[field, h, pl.ds(to + d, 8, stride=8), :] = value
                    outer[field, h, pl.ds(to + 7 - d, 8, stride=8), :] = value
        for slot in range(16):
            inner, block = rows_of(refs, field, slot, a), rows_of(refs, field, slot, 1 - a)
            edge = slice(8 * slot, 8 * slot + 8)
            for h in range(2):
                kept = block[:, 128 * h : 128 * h + 128]
                outer[field, h, edge, :] = jnp.where(beyond, outer[field, h, edge, :], kept)
            base = 64 * (field % 2) + 4 * slot
            here = lane == base // 4
            first = jnp.concatenate([inner[:, :128], outer[field, 0, edge, :]], axis=0)
            last = jnp.concatenate([inner[:, 128:], outer[field, 1, edge, :]], axis=0)
            lows = jnp.where(here, pltpu.roll(first, base, 1) if base else first, lows)
            highs = jnp.where(here, pltpu.roll(last, (base + 4) % 128, 1) if base != 124 else last, highs)
        if field % 2:
            even = lax.axis_index("gy") % 2 == 0
            far[field // 2] = jnp.where(even, lows, highs)
            near[field // 2] = jnp.where(even, highs, lows)


def stencil(f, s, fp, sp, outer, far, near, after, last, a, b, stiff):
    refs = (f, s, fp, sp)
    core = lax.axis_index("ga")
    even = lax.axis_index("gy") % 2 == 0
    first_lanes = lax.broadcasted_iota(jnp.int32, (16, 128), 1) < 64
    for field in range(6):
        for slot in range(16):
            to = stiff.at[slot] if field == 5 else a.at[field, slot]
            to[0:8, 0:256] = rows_of(refs, field, slot, core)
            for h in range(2):
                edge = outer[field, h, 8 * slot : 8 * slot + 8, :]
                to[8:16, 128 * h : 128 * h + 128] = edge
            base = 64 * (field % 2) + 4 * slot
            one, two = near[field // 2], far[field // 2]
            above, below = jnp.where(even, one, two), jnp.where(even, two, one)
            above = pltpu.roll(above, 128 - base, 1) if base else above
            below = pltpu.roll(below, 124 - base, 1) if base != 124 else below
            to[:, 256:384] = jnp.where(first_lanes, above, below)

    def advance(src, slot, crop):
        new, east, north, depth = [], [], [], []
        for field in range(5):
            mid = src[field, slot]
            up, down = src[field, (slot + 1) & 15], src[field, (slot + 15) & 15]
            xp, xm = pltpu.roll(mid, 15, 0), pltpu.roll(mid, 1, 0)
            yp, ym = pltpu.roll(mid, 383, 1), pltpu.roll(mid, 1, 1)
            if crop:
                mid, up, down, xp, xm, yp, ym = (
                    v[0:8, 0:256] for v in (mid, up, down, xp, xm, yp, ym)
                )
            total = 0.1 * mid + 0.12 * xp + 0.18 * xm + 0.17 * yp + 0.13 * ym
            new.append(total + 0.14 * up + 0.16 * down)
            east.append(xp - xm if field in (1, 4) else None)
            north.append(yp - ym if field in (2, 4) else None)
            depth.append(up - down if field in (3, 4) else None)
        div = 0.1 * (east[1] + north[2] + depth[3])
        new[0] = new[0] - div
        new[1] = new[1] - 0.1 * east[4]
        new[2] = new[2] - 0.1 * north[4]
        new[3] = new[3] - 0.1 * depth[4]
        new[4] = new[4] - (stiff[slot, 0:8, 0:256] if crop else stiff[slot]) * div
        return new

    for src, dst in ((a, b), (b, a), (a, None)):

        def body(slot, carry, src=src, dst=dst):
            new = advance(src, slot, dst is None)
            for field in range(5):
                if dst is None:
                    rows = pl.ds(pl.multiple_of(slot * 8, 8), 8)
                    for h in range(2):
                        last[field, h, rows, :] = new[field][:, 128 * h : 128 * h + 128]
                else:
                    dst[field, slot] = new[field]
            return carry

        lax.fori_loop(0, 16, body, 0)


def lift_rows(values, weight, bias):
    rows = []
    for c in range(C):
        v = bias[c] + values[0] * weight[0, c]
        for field in range(1, 5):
            v = v + values[field] * weight[field, c]
        rows.append(gelu(v))
    return jnp.concatenate(rows, axis=0).astype(BF16)


def pointwise(keep, got, weight, bias, mix, obias, out, wide):
    a = lax.axis_index("ga")
    wide[pl.ds(pl.multiple_of(160 * a, 8), 160), :] = keep[...]
    wide[pl.ds(pl.multiple_of(160 * (1 - a), 8), 160), :] = got[...]
    row, lane = iotas((256, 32))
    pick = (row // 8 == lane).astype(BF16)
    bias_o = jnp.sum(jnp.where(row // 8 == lane, obias[...], 0.0), axis=1, keepdims=True)
    by_row = dot(pick, mix[...], ((1,), (1,))).astype(BF16)
    row, lane = iotas((256, 256))
    spread = jnp.where(row % 8 == lane % 8, dot(by_row, pick, ((1,), (1,))), 0.0).astype(BF16)

    def body(z, carry):
        values = [wide[pl.ds(8 * field + z, 8, stride=40), :] for field in range(5)]
        out[z] = dot(spread, lift_rows(values, weight, bias)) + bias_o
        return carry

    lax.fori_loop(0, ZL, body, 0)


def forward(
    last, weight, bias, yf_far, zf_far, keep, send, out, sums, lifted, modes, yf, zf, sems
):
    copies = [
        pltpu.make_async_copy(yf_far.at[lax.axis_index("gy")], yf, sems.at[0]),
        pltpu.make_async_copy(zf_far, zf, sems.at[1]),
    ]
    for copy in copies:
        copy.start()
    for half in range(2):
        for x in range(4):
            for field in range(5):
                at = 160 * half + 40 * x + 8 * field
                for h in range(2):
                    even = last[field, h, pl.ds(64 * half + 2 * x, 8, stride=8), :]
                    odd = last[field, h, pl.ds(64 * half + 2 * x + 1, 8, stride=8), :]
                    sums[at : at + 8, 128 * h : 128 * h + 128] = even + odd
    value = sums[...]
    high = value.astype(BF16)
    rest = value - high.astype(F32)
    mid, low = halves(rest)
    row, lane = iotas((256, 128))
    table = jnp.where(row // 2 == lane, 0.25, 0.0).astype(BF16)
    mean = dot(high, table) + dot(mid, table) + dot(low, table)
    keep[...] = mean[:160]
    send[...] = mean[160:]
    for x in range(4):
        at = [40 * x + 8 * field for field in range(5)]
        values = [jnp.concatenate([mean[r : r + 8], mean[r + 160 : r + 168]], axis=0) for r in at]
        lifted[x] = lift_rows(values, weight, bias)
    copies[0].wait()
    for x in range(4):
        both = dot(yf[...], lifted[x], ((1,), (1,)))
        modes[x] = both[:128] + both[128:]
    copies[1].wait()
    parts = []
    for group in range(4):
        lanes = slice(128 * group, 128 * group + 128)
        stack = [
            jnp.concatenate([modes[x, 0:64, lanes], modes[x, 64:128, lanes]], axis=1)
            for x in range(4)
        ]
        m_high, m_low = halves(jnp.concatenate(stack, axis=0))
        both = dot(m_high, zf[...])
        parts.append(both[:, :128] + both[:, 128:] + dot(m_low, zf[:, :128]))
    lane = lax.broadcasted_iota(jnp.int32, (256, 128), 1) // 32
    for part in range(4):
        total = parts[part]
        for group in range(4):
            if group != part:
                moved = pltpu.roll(parts[group], (32 * (group - part)) % 128, 1)
                total = jnp.where(lane == group, moved, total)
        for x in range(4):
            out[:, 8 * (part // 2) + 2 * x + part % 2, :] = total[64 * x : 64 * x + 64]


def mix_modes(got, weights, xf, xi, after, out):
    total = got[:, 0]
    for j in range(1, 8):
        total = total + got[:, j]
    high, low = halves(total.reshape(128, 128))
    row, lane = iotas((128, 128))
    modes = jnp.zeros((256, 128), F32)
    for k in range(4):
        spread = (row // 8 % 4 == k) & (row // 32 * 8 + row % 8 == lane // 4)
        spread = spread.astype(BF16)
        modes = modes + dot(xf[k], dot(high, spread).astype(BF16))
        modes = modes + dot(xf[k], dot(low, spread).astype(BF16))
    real, imag = modes[:128], modes[128:]
    total = jnp.zeros((256, 128), F32)
    for i in range(8):
        wr = weights[8 * i : 8 * i + 8, 0:16, :].astype(F32).reshape(128, 128)
        wi = weights[8 * i : 8 * i + 8, 16:32, :].astype(F32).reshape(128, 128)
        part = jnp.concatenate([wr * real - wi * imag, wr * imag + wi * real], axis=0)
        p_high, p_low = halves(part)
        gather = (lane % 32 == 4 * i + row % 4).astype(BF16)
        total = total + dot(p_high, gather) + dot(p_low, gather)
    row, lane = iotas((256, 128))
    total = jnp.where((row // 4) % 4 == lane // 32, total, 0.0)
    t_high, t_low = halves(total)
    back = dot(xi[0], t_high) + dot(xi[0], t_low) + dot(xi[1], t_high)
    odd = (lax.broadcasted_iota(jnp.int32, (64, 128), 1) // 32) % 2 == 1
    for ri in range(2):
        value = back[64 * ri : 64 * ri + 64]
        out[:, ri, :] = value
        out[:, 2 + ri, :] = jnp.where(odd, -value, value)


def inverse(got, zi, yi, out):
    modes = jnp.concatenate([got[:, part, :] for part in range(4)], axis=1)
    by_z = dot3(modes, zi)
    by_z = jnp.concatenate([by_z[:, :256], by_z[:, 256:]], axis=0)
    high, low = halves(by_z)
    stacked = jnp.concatenate([high, low, high], axis=0)
    for j in range(8):
        block = dot(stacked, yi[:, 128 * j : 128 * j + 128], ((0,), (0,)))
        out[j] = block.astype(BF16)


def finish(got, direct, out, rows):
    for x in range(8):
        rows[256 * x : 256 * x + 256, :] = got[x].astype(F32)

    def body(z, carry):
        for o in range(C):
            spectral = rows[pl.ds(C * z + o, 8, stride=256), :]
            total = direct[z, 8 * o : 8 * o + 8, :] + spectral
            out[z, o] = gelu(total).astype(BF16)
        return carry

    lax.fori_loop(0, ZL, body, 0)


def turn_weights(weights, after, out, wide):
    for chunk in range(16):
        turned = weights[128 * chunk : 128 * chunk + 128, :].T
        for ri in range(2):
            wide[:, 16 * ri + chunk, :] = turned[64 * ri : 64 * ri + 64]
    out[...] = wide[...].astype(BF16)


def shards(fields, stiffness, lift_weight, lift_bias, mix_weight, spectral_weight, output_bias):
    table = {name: jnp.asarray(value) for name, value in tables().items()}
    everyone = ("gx", "gy", "ga")

    def exchange(value, axis):
        return lax.all_to_all(value, axis, split_axis=0, concat_axis=0, tiled=True)

    anywhere = pl.BlockSpec(memory_space=pl.ANY)
    f = fields.reshape(5, 128, 256)
    s = stiffness.reshape(128, 256)
    swap = [(0, 1), (1, 0)]
    fp, sp = lax.ppermute(f, "ga", swap), lax.ppermute(s, "ga", swap)
    rows = pltpu.VMEM((6, 2, 128, 128), F32)
    edges = ((6, 2, 24, 128), F32)
    [own] = call(pack_own, [edges], [VMEM] * 2, [rows])(f, s)
    [message] = call(
        pack_other, [((6, 2, 48, 128), F32)], [VMEM] * 3, [pltpu.VMEM(*edges), rows]
    )(fp, sp, own)
    across = [(2 * i, 2 * ((i - 1) % 8) + 1) for i in range(8)]
    across += [(2 * i + 1, 2 * ((i + 1) % 8)) for i in range(8)]
    got = lax.ppermute(message, ("gx", "ga"), across)

    [turned] = call(
        turn_weights,
        [((64, 32, 128), BF16)],
        [VMEM, anywhere],
        [pltpu.VMEM((64, 32, 128), F32)],
        size=2 * 10**7,
    )(spectral_weight.reshape(2048, 128), message)
    weights = exchange(turned, ("gx", "gy"))

    message = ((3, 16, 128), F32)
    outer, far, near = call(
        pack_y, [((6, 2, 128, 128), F32), message, message], [VMEM] * 5, flops=10**12
    )(f, s, fp, sp, got)
    far = lax.ppermute(far, "gy", [(j, (j - 1 + 2 * (j % 2)) % 8) for j in range(8)])
    near = lax.ppermute(near, "gy", [(j, j + 1 - 2 * (j % 2)) for j in range(8)])
    [last] = call(
        stencil,
        [((5, 2, 128, 128), F32)],
        [VMEM] * 7 + [anywhere],
        [
            pltpu.VMEM((5, 16, 16, 384), F32),
            pltpu.VMEM((5, 16, 16, 384), F32),
            pltpu.VMEM((16, 16, 384), F32),
        ],
        flops=10**12,
    )(f, s, fp, sp, outer, far, near, weights)
    keep, send, modes = call(
        forward,
        [((160, 128), F32), ((160, 128), F32), ((64, 16, 128), F32)],
        [VMEM, SMEM, SMEM, anywhere, anywhere],
        [
            pltpu.VMEM((320, 256), F32),
            pltpu.VMEM((4, 512, 128), BF16),
            pltpu.VMEM((4, 128, 512), F32),
            pltpu.VMEM((256, 128), BF16),
            pltpu.VMEM((256, 256), BF16),
            pltpu.SemaphoreType.DMA((2,)),
        ],
    )(last, lift_weight, lift_bias, table["yf"], table["zf"])
    modes = exchange(modes.reshape(128, 8, 128), everyone)
    [direct] = call(
        pointwise,
        [((8, 256, 128), F32)],
        [VMEM, VMEM, SMEM, SMEM, VMEM, VMEM],
        [pltpu.VMEM((320, 128), F32)],
        flops=3 * 10**8,
    )(keep, lax.ppermute(send, "ga", swap), lift_weight, lift_bias, mix_weight, output_bias.reshape(1, C))

    [mixed] = call(mix_modes, [((64, 4, 128), F32)], [VMEM] * 4 + [anywhere])(
        modes.reshape(8, 8, 16, 128), weights, table["xf"], table["xi"], direct
    )
    mixed = exchange(mixed.reshape(128, 2, 128), everyone)
    [spectral] = call(inverse, [((8, 256, 128), BF16)], [VMEM] * 3)(
        mixed.reshape(64, 4, 128), table["zi"], table["yi"]
    )
    spectral = exchange(spectral, "gy")
    [out] = call(
        finish, [((8, 32, 8, 128), BF16)], [VMEM] * 2, [pltpu.VMEM((2048, 128), F32)]
    )(spectral, direct)
    return out


def solution(mesh):
    placed = (
        P(None, "ga", "gx", "gy"),
        P("ga", "gx", "gy"),
        P(),
        P(),
        P(),
        P("ga", "gy", None, "gx", None),
        P(),
    )
    return jax.shard_map(
        shards, mesh=mesh, in_specs=placed, out_specs=P("ga", None, "gx", "gy"), check_vma=False
    )
```

```python
import functools
import math

import jax
import jax.numpy as jnp
import numpy as np
from jax import lax
from jax.experimental import pallas as pl
from jax.experimental.pallas import tpu as pltpu
from jax.sharding import PartitionSpec as P

NZ, C, MX, MY, MZ, GX, GY = 16, 32, 32, 64, 8, 64, 1024
ZL, XL, YL = 8, 16, 256
F32, BF16 = jnp.float32, jnp.bfloat16
ROOT = math.sqrt(2.0 / math.pi)
VMEM = pl.BlockSpec(memory_space=pltpu.VMEM)
SMEM = pl.BlockSpec(memory_space=pltpu.SMEM)


def cos_sin(freq, points, length):
    turn = np.mod(np.outer(freq, points), length) * (2.0 * np.pi / length)
    return np.cos(turn), np.sin(turn)


def split(table):
    table = np.asarray(table, np.float32)
    high = table.astype(jnp.bfloat16)
    low = (table - high.astype(np.float32)).astype(jnp.bfloat16)
    return high, low


@functools.cache
def tables():
    out = {}
    ky = np.arange(MY) - MY // 2
    cy, sy = cos_sin(ky, np.arange(GY), GY)
    rows = np.concatenate([cy, -sy]) / math.sqrt(GY)
    out["yf"] = np.concatenate(split(rows)).reshape(256, 8, 128).transpose(1, 0, 2)
    high, low = (half.reshape(128, 8, 128).transpose(1, 0, 2) for half in split(rows))
    out["yi"] = np.concatenate([high, low], axis=2)
    cf, sf = (
        np.einsum("kz,cd->czkd", w / math.sqrt(NZ), np.eye(8)).reshape(128, 2, 32)
        for w in cos_sin(np.arange(MZ), np.arange(NZ), NZ)
    )
    zf = np.zeros((2, 128, 2, 2, 32))
    zf[0, :, :, 0], zf[1, :, :, 0], zf[1, :, :, 1], zf[0, :, :, 1] = cf, sf, cf, -sf
    out["zf"] = np.concatenate(split(zf.reshape(256, 128)), axis=1)
    ci, si = (
        np.einsum("kz,op->zokp", w / math.sqrt(NZ), np.eye(16)).reshape(128, 2, 64)
        for w in cos_sin(np.arange(MZ), np.arange(ZL), NZ)
    )
    zi = np.zeros((2, 128, 2, 2, 64))
    zi[0, :, :, 0], zi[0, :, :, 1], zi[1, :, :, 0], zi[1, :, :, 1] = ci, -si, si, ci
    out["zi"] = np.concatenate(split(zi.reshape(256, 256)))
    kx = np.arange(MX) - MX // 2
    cx, sx = cos_sin(kx, np.arange(GX), GX)
    cr = (cx / 8.0).astype(np.float32).astype(jnp.bfloat16).astype(np.float64)
    sr = (-sx / 8.0).astype(np.float32).astype(jnp.bfloat16).astype(np.float64)
    cr, sr = cr.reshape(8, 4, 8, 2, 4), sr.reshape(8, 4, 8, 2, 4)
    xf = np.zeros((4, 2, 8, 4, 4, 8, 2, 4, 2))
    for k in range(4):
        for a in range(2):
            sign = -1.0 if k * a % 2 else 1.0
            real, imag = sign * cr[:, :, :, a], sign * sr[:, :, :, a]
            xf[k, 0, :, k, :, :, a, :, 0], xf[k, 0, :, k, :, :, a, :, 1] = real, -imag
            xf[k, 1, :, k, :, :, a, :, 0], xf[k, 1, :, k, :, :, a, :, 1] = imag, real
    out["xf"] = xf.reshape(4, 256, 128).astype(np.float32).astype(jnp.bfloat16)
    ic, is_ = (cx / 8.0).T.reshape(GX, 8, 1, 4), (sx / 8.0).T.reshape(GX, 8, 1, 4)
    xi = np.zeros((2, GX, 2, 8, 4, 4))
    xi[0, :, 0], xi[0, :, 1] = ic, -is_
    xi[1, :, 0], xi[1, :, 1] = is_, ic
    out["xi"] = np.stack(split(xi.reshape(128, 256)))
    return out


def iotas(shape):
    return lax.broadcasted_iota(jnp.int32, shape, 0), lax.broadcasted_iota(jnp.int32, shape, 1)


def halves(value):
    high = value.astype(BF16)
    return high, (value - high.astype(F32)).astype(BF16)


def dot(a, b, contract=((1,), (0,))):
    return lax.dot_general(a, b, (contract, ((), ())), preferred_element_type=F32)


def gelu(v):
    return 0.5 * v * (1.0 + jnp.tanh(ROOT * (v + 0.044715 * (v * v * v))))


def call(kernel, outs, in_specs, scratch=(), mib=16, flops=10**7, size=2**20):
    return pl.pallas_call(
        kernel,
        out_shape=[jax.ShapeDtypeStruct(s, d) for s, d in outs],
        in_specs=in_specs,
        out_specs=[VMEM] * len(outs),
        scratch_shapes=list(scratch),
        compiler_params=pltpu.CompilerParams(vmem_limit_bytes=mib << 20),
        cost_estimate=pl.CostEstimate(flops=flops, bytes_accessed=size, transcendentals=0),
    )


def rows_of(refs, field, slot, half):
    f, s, fp, sp = refs
    own, other = (s, sp) if field == 5 else (f.at[field], fp.at[field])
    start = 16 * (slot % 8) + 8 * half
    return (own if slot < 8 else other)[pl.ds(pl.multiple_of(start, 8), 8), :]


def edge_rows(f, s, out, rows):
    bottom = lax.axis_index("ga") == 0
    for field in range(6):
        for h in range(2):
            lanes = slice(128 * h, 128 * h + 128)
            rows[field, h] = s[:, lanes] if field == 5 else f[field, :, lanes]
            for d in range(3):
                first = rows[field, h, pl.ds(d, 8, stride=XL), :]
                last = rows[field, h, pl.ds(XL - 1 - d, 8, stride=XL), :]
                out[field, h, 8 * d : 8 * d + 8, :] = jnp.where(bottom, first, last)


def pack_own(f, s, own, rows):
    edge_rows(f, s, own, rows)


def pack_other(fp, sp, own, message, other, rows):
    edge_rows(fp, sp, other, rows)
    message[:, :, 0:24, :] = own[...]
    message[:, :, 24:48, :] = other[...]


def pack_y(f, s, fp, sp, message, outer, far, near):
    refs = (f, s, fp, sp)
    a = lax.axis_index("ga")
    row = lax.broadcasted_iota(jnp.int32, (8, 128), 0)
    beyond = jnp.where(a == 1, row, 7 - row) < 3
    lane = lax.broadcasted_iota(jnp.int32, (16, 128), 1) // 4
    lows, highs = jnp.zeros((16, 128), F32), jnp.zeros((16, 128), F32)
    for field in range(6):
        for h in range(2):
            for which in range(2):
                for d in range(3):
                    at = 24 * which + 8 * d
                    value = message[field, h, at : at + 8, :]
                    to = 64 * (1 - which)
                    outer[field, h, pl.ds(to + d, 8, stride=8), :] = value
                    outer[field, h, pl.ds(to + 7 - d, 8, stride=8), :] = value
        for slot in range(16):
            inner, block = rows_of(refs, field, slot, a), rows_of(refs, field, slot, 1 - a)
            edge = slice(8 * slot, 8 * slot + 8)
            for h in range(2):
                kept = block[:, 128 * h : 128 * h + 128]
                outer[field, h, edge, :] = jnp.where(beyond, outer[field, h, edge, :], kept)
            base = 64 * (field % 2) + 4 * slot
            here = lane == base // 4
            first = jnp.concatenate([inner[:, :128], outer[field, 0, edge, :]], axis=0)
            last = jnp.concatenate([inner[:, 128:], outer[field, 1, edge, :]], axis=0)
            lows = jnp.where(here, pltpu.roll(first, base, 1) if base else first, lows)
            highs = jnp.where(here, pltpu.roll(last, (base + 4) % 128, 1) if base != 124 else last, highs)
        if field % 2:
            even = lax.axis_index("gy") % 2 == 0
            far[field // 2] = jnp.where(even, lows, highs)
            near[field // 2] = jnp.where(even, highs, lows)


def stencil(f, s, fp, sp, outer, far, near, after, last, a, b, stiff):
    refs = (f, s, fp, sp)
    core = lax.axis_index("ga")
    even = lax.axis_index("gy") % 2 == 0
    first_lanes = lax.broadcasted_iota(jnp.int32, (16, 128), 1) < 64
    for field in range(6):
        for slot in range(16):
            to = stiff.at[slot] if field == 5 else a.at[field, slot]
            to[0:8, 0:256] = rows_of(refs, field, slot, core)
            for h in range(2):
                edge = outer[field, h, 8 * slot : 8 * slot + 8, :]
                to[8:16, 128 * h : 128 * h + 128] = edge
            base = 64 * (field % 2) + 4 * slot
            one, two = near[field // 2], far[field // 2]
            above, below = jnp.where(even, one, two), jnp.where(even, two, one)
            above = pltpu.roll(above, 128 - base, 1) if base else above
            below = pltpu.roll(below, 124 - base, 1) if base != 124 else below
            to[:, 256:384] = jnp.where(first_lanes, above, below)

    def advance(src, slot, crop):
        new, east, north, depth = [], [], [], []
        for field in range(5):
            mid = src[field, slot]
            up, down = src[field, (slot + 1) & 15], src[field, (slot + 15) & 15]
            xp, xm = pltpu.roll(mid, 15, 0), pltpu.roll(mid, 1, 0)
            yp, ym = pltpu.roll(mid, 383, 1), pltpu.roll(mid, 1, 1)
            if crop:
                mid, up, down, xp, xm, yp, ym = (
                    v[0:8, 0:256] for v in (mid, up, down, xp, xm, yp, ym)
                )
            total = 0.1 * mid + 0.12 * xp + 0.18 * xm + 0.17 * yp + 0.13 * ym
            new.append(total + 0.14 * up + 0.16 * down)
            east.append(xp - xm if field in (1, 4) else None)
            north.append(yp - ym if field in (2, 4) else None)
            depth.append(up - down if field in (3, 4) else None)
        div = 0.1 * (east[1] + north[2] + depth[3])
        new[0] = new[0] - div
        new[1] = new[1] - 0.1 * east[4]
        new[2] = new[2] - 0.1 * north[4]
        new[3] = new[3] - 0.1 * depth[4]
        new[4] = new[4] - (stiff[slot, 0:8, 0:256] if crop else stiff[slot]) * div
        return new

    for src, dst in ((a, b), (b, a), (a, None)):

        def body(slot, carry, src=src, dst=dst):
            new = advance(src, slot, dst is None)
            for field in range(5):
                if dst is None:
                    rows = pl.ds(pl.multiple_of(slot * 8, 8), 8)
                    for h in range(2):
                        last[field, h, rows, :] = new[field][:, 128 * h : 128 * h + 128]
                else:
                    dst[field, slot] = new[field]
            return carry

        lax.fori_loop(0, 16, body, 0)


def lift_rows(values, weight, bias):
    rows = []
    for c in range(C):
        v = bias[c] + values[0] * weight[0, c]
        for field in range(1, 5):
            v = v + values[field] * weight[field, c]
        rows.append(gelu(v))
    return jnp.concatenate(rows, axis=0).astype(BF16)


def pointwise(keep, got, weight, bias, mix, obias, out, wide):
    a = lax.axis_index("ga")
    wide[pl.ds(pl.multiple_of(160 * a, 8), 160), :] = keep[...]
    wide[pl.ds(pl.multiple_of(160 * (1 - a), 8), 160), :] = got[...]
    row, lane = iotas((256, 32))
    pick = (row // 8 == lane).astype(BF16)
    bias_o = jnp.sum(jnp.where(row // 8 == lane, obias[...], 0.0), axis=1, keepdims=True)
    by_row = dot(pick, mix[...], ((1,), (1,))).astype(BF16)
    row, lane = iotas((256, 256))
    spread = jnp.where(row % 8 == lane % 8, dot(by_row, pick, ((1,), (1,))), 0.0).astype(BF16)

    def body(z, carry):
        values = [wide[pl.ds(8 * field + z, 8, stride=40), :] for field in range(5)]
        out[z] = dot(spread, lift_rows(values, weight, bias)) + bias_o
        return carry

    lax.fori_loop(0, ZL, body, 0)


def forward(
    last, weight, bias, yf_far, zf_far, keep, send, out, sums, lifted, modes, yf, zf, sems
):
    copies = [
        pltpu.make_async_copy(yf_far.at[lax.axis_index("gy")], yf, sems.at[0]),
        pltpu.make_async_copy(zf_far, zf, sems.at[1]),
    ]
    for copy in copies:
        copy.start()
    for half in range(2):
        for x in range(4):
            for field in range(5):
                at = 160 * half + 40 * x + 8 * field
                for h in range(2):
                    even = last[field, h, pl.ds(64 * half + 2 * x, 8, stride=8), :]
                    odd = last[field, h, pl.ds(64 * half + 2 * x + 1, 8, stride=8), :]
                    sums[at : at + 8, 128 * h : 128 * h + 128] = even + odd
    value = sums[...]
    high = value.astype(BF16)
    rest = value - high.astype(F32)
    mid, low = halves(rest)
    row, lane = iotas((256, 128))
    table = jnp.where(row // 2 == lane, 0.25, 0.0).astype(BF16)
    mean = dot(high, table) + dot(mid, table) + dot(low, table)
    keep[...] = mean[:160]
    send[...] = mean[160:]
    for x in range(4):
        at = [40 * x + 8 * field for field in range(5)]
        values = [jnp.concatenate([mean[r : r + 8], mean[r + 160 : r + 168]], axis=0) for r in at]
        lifted[x] = lift_rows(values, weight, bias)
    copies[0].wait()
    for x in range(4):
        both = dot(yf[...], lifted[x], ((1,), (1,)))
        modes[x] = both[:128] + both[128:]
    copies[1].wait()
    parts = []
    for group in range(4):
        lanes = slice(128 * group, 128 * group + 128)
        stack = [
            jnp.concatenate([modes[x, 0:64, lanes], modes[x, 64:128, lanes]], axis=1)
            for x in range(4)
        ]
        m_high, m_low = halves(jnp.concatenate(stack, axis=0))
        both = dot(m_high, zf[...])
        parts.append(both[:, :128] + both[:, 128:] + dot(m_low, zf[:, :128]))
    lane = lax.broadcasted_iota(jnp.int32, (256, 128), 1) // 32
    for part in range(4):
        total = parts[part]
        for group in range(4):
            if group != part:
                moved = pltpu.roll(parts[group], (32 * (group - part)) % 128, 1)
                total = jnp.where(lane == group, moved, total)
        for x in range(4):
            out[:, 8 * (part // 2) + 2 * x + part % 2, :] = total[64 * x : 64 * x + 64]


def mix_modes(got, weights, xf, xi, after, out):
    total = got[:, 0]
    for j in range(1, 8):
        total = total + got[:, j]
    high, low = halves(total.reshape(128, 128))
    row, lane = iotas((128, 128))
    modes = jnp.zeros((256, 128), F32)
    for k in range(4):
        spread = (row // 8 % 4 == k) & (row // 32 * 8 + row % 8 == lane // 4)
        spread = spread.astype(BF16)
        modes = modes + dot(xf[k], dot(high, spread).astype(BF16))
        modes = modes + dot(xf[k], dot(low, spread).astype(BF16))
    real, imag = modes[:128], modes[128:]
    total = jnp.zeros((256, 128), F32)
    for i in range(8):
        wr = weights[8 * i : 8 * i + 8, 0:16, :].astype(F32).reshape(128, 128)
        wi = weights[8 * i : 8 * i + 8, 16:32, :].astype(F32).reshape(128, 128)
        part = jnp.concatenate([wr * real - wi * imag, wr * imag + wi * real], axis=0)
        p_high, p_low = halves(part)
        gather = (lane // 64 * 16 + lane % 16 == 4 * i + row % 4).astype(BF16)
        total = total + dot(p_high, gather) + dot(p_low, gather)
    row, lane = iotas((256, 128))
    total = jnp.where((row // 4) % 4 == (lane // 16) % 4, total, 0.0)
    t_high, t_low = halves(total)
    back = dot(xi[0], t_high) + dot(xi[0], t_low) + dot(xi[1], t_high)
    real, imag = back[:64], back[64:]
    lane = lax.broadcasted_iota(jnp.int32, (64, 128), 1)
    parts = [
        jnp.where(lane < 64, real, pltpu.roll(imag, 64, 1)),
        jnp.where(lane < 64, pltpu.roll(real, 64, 1), imag),
    ]
    odd = (lane // 16) % 2 == 1
    for a in range(2):
        signed = [jnp.where(odd, -part, part) for part in parts] if a else parts
        for i in range(8):
            rows = slice(8 * i, 8 * i + 8)
            tile = jnp.concatenate([part[rows] for part in signed], axis=0).astype(BF16)
            for j in range(8):
                out[i, j, a] = tile


def finish(got, direct, yi_far, zi_far, out, rows, spectral, yi, zi, sems):
    copies = [
        pltpu.make_async_copy(yi_far.at[lax.axis_index("gy")], yi, sems.at[0]),
        pltpu.make_async_copy(zi_far, zi, sems.at[1]),
    ]
    for copy in copies:
        copy.start()
    rows[...] = got[...].astype(F32)
    for copy in copies:
        copy.wait()
    by_z = []
    for part in range(2):
        stack = []
        for x in range(8):
            pair = [rows[pl.ds(16 * a + 8 * part + x, 64, stride=32), :] for a in range(2)]
            stack.append(jnp.concatenate(pair, axis=1).astype(BF16))
        both = dot(zi[...], jnp.concatenate(stack, axis=0), ((1,), (1,)))
        by_z.append(both[:256] + both[256:])
    blank = jnp.zeros((64, 128), BF16)

    def twice(lanes):
        real, imag = yi[0:64, lanes], yi[64:128, lanes]
        pieces = [[real, blank], [blank, real], [imag, blank], [blank, imag]]
        return jnp.concatenate([jnp.concatenate(row, axis=1) for row in pieces], axis=0)

    t_high, t_low = twice(slice(0, 128)), twice(slice(128, 256))
    for pair in range(4):
        lanes = slice(128 * pair, 128 * pair + 128)
        value = jnp.concatenate(
            [jnp.concatenate([v[:128, lanes], v[128:, lanes]], axis=1) for v in by_z], axis=0
        )
        high, low = halves(value)
        both = dot(high, t_high) + dot(low, t_high) + dot(high, t_low)
        for x in range(2):
            spectral[pl.ds(2 * pair + x, 256, stride=8), :] = both[:, 128 * x : 128 * x + 128]
    for part in range(2):
        for z in range(ZL):
            at = 128 * (8 * part + z)
            branch = spectral[at : at + 128, :].astype(BF16).astype(F32)
            total = gelu(direct[z, 128 * part : 128 * part + 128, :] + branch)
            out[z, 16 * part : 16 * part + 16] = total.reshape(16, 8, 128).astype(BF16)


def turn_weights(weights, after, out, wide):
    for chunk in range(16):
        turned = weights[128 * chunk : 128 * chunk + 128, :].T
        for ri in range(2):
            wide[:, 16 * ri + chunk, :] = turned[64 * ri : 64 * ri + 64]
    out[...] = wide[...].astype(BF16)


def shards(fields, stiffness, lift_weight, lift_bias, mix_weight, spectral_weight, output_bias):
    table = {name: jnp.asarray(value) for name, value in tables().items()}
    everyone = ("gx", "gy", "ga")

    def exchange(value, axis):
        return lax.all_to_all(value, axis, split_axis=0, concat_axis=0, tiled=True)

    anywhere = pl.BlockSpec(memory_space=pl.ANY)
    f = fields.reshape(5, 128, 256)
    s = stiffness.reshape(128, 256)
    swap = [(0, 1), (1, 0)]
    fp, sp = lax.ppermute(f, "ga", swap), lax.ppermute(s, "ga", swap)
    rows = pltpu.VMEM((6, 2, 128, 128), F32)
    edges = ((6, 2, 24, 128), F32)
    [own] = call(pack_own, [edges], [VMEM] * 2, [rows])(f, s)
    [message] = call(
        pack_other, [((6, 2, 48, 128), F32)], [VMEM] * 3, [pltpu.VMEM(*edges), rows]
    )(fp, sp, own)
    across = [(2 * i, 2 * ((i - 1) % 8) + 1) for i in range(8)]
    across += [(2 * i + 1, 2 * ((i + 1) % 8)) for i in range(8)]
    got = lax.ppermute(message, ("gx", "ga"), across)

    [turned] = call(
        turn_weights,
        [((64, 32, 128), BF16)],
        [VMEM, anywhere],
        [pltpu.VMEM((64, 32, 128), F32)],
        size=2 * 10**7,
    )(spectral_weight.reshape(2048, 128), message)
    weights = exchange(turned, ("gx", "gy"))

    message = ((3, 16, 128), F32)
    outer, far, near = call(
        pack_y, [((6, 2, 128, 128), F32), message, message], [VMEM] * 5, flops=10**12
    )(f, s, fp, sp, got)
    far = lax.ppermute(far, "gy", [(j, (j - 1 + 2 * (j % 2)) % 8) for j in range(8)])
    near = lax.ppermute(near, "gy", [(j, j + 1 - 2 * (j % 2)) for j in range(8)])
    [last] = call(
        stencil,
        [((5, 2, 128, 128), F32)],
        [VMEM] * 7 + [anywhere],
        [
            pltpu.VMEM((5, 16, 16, 384), F32),
            pltpu.VMEM((5, 16, 16, 384), F32),
            pltpu.VMEM((16, 16, 384), F32),
        ],
        flops=10**12,
    )(f, s, fp, sp, outer, far, near, weights)
    keep, send, modes = call(
        forward,
        [((160, 128), F32), ((160, 128), F32), ((64, 16, 128), F32)],
        [VMEM, SMEM, SMEM, anywhere, anywhere],
        [
            pltpu.VMEM((320, 256), F32),
            pltpu.VMEM((4, 512, 128), BF16),
            pltpu.VMEM((4, 128, 512), F32),
            pltpu.VMEM((256, 128), BF16),
            pltpu.VMEM((256, 256), BF16),
            pltpu.SemaphoreType.DMA((2,)),
        ],
    )(last, lift_weight, lift_bias, table["yf"], table["zf"])
    modes = exchange(modes.reshape(128, 8, 128), everyone)
    [direct] = call(
        pointwise,
        [((8, 256, 128), F32)],
        [VMEM, VMEM, SMEM, SMEM, VMEM, VMEM],
        [pltpu.VMEM((320, 128), F32)],
        flops=3 * 10**8,
    )(keep, lax.ppermute(send, "ga", swap), lift_weight, lift_bias, mix_weight, output_bias.reshape(1, C))

    [mixed] = call(mix_modes, [((8, 8, 2, 16, 128), BF16)], [VMEM] * 4 + [anywhere])(
        modes.reshape(8, 8, 16, 128), weights, table["xf"], table["xi"], direct
    )
    mixed = exchange(mixed.reshape(128, 16, 128), everyone)
    [out] = call(
        finish,
        [((8, 32, 8, 128), BF16)],
        [VMEM, VMEM, anywhere, anywhere],
        [
            pltpu.VMEM((2048, 128), F32),
            pltpu.VMEM((2048, 128), F32),
            pltpu.VMEM((128, 256), BF16),
            pltpu.VMEM((512, 256), BF16),
            pltpu.SemaphoreType.DMA((2,)),
        ],
    )(mixed.reshape(2048, 128), direct, table["yi"], table["zi"])
    return out


def solution(mesh):
    placed = (
        P(None, "ga", "gx", "gy"),
        P("ga", "gx", "gy"),
        P(),
        P(),
        P(),
        P("ga", "gy", None, "gx", None),
        P(),
    )
    return jax.shard_map(
        shards, mesh=mesh, in_specs=placed, out_specs=P("ga", None, "gx", "gy"), check_vma=False
    )
```

```python
import functools
import math

import jax
import jax.numpy as jnp
import numpy as np
from jax import lax
from jax.experimental import pallas as pl
from jax.experimental.pallas import tpu as pltpu
from jax.sharding import PartitionSpec as P

NZ, C, MX, MY, MZ, GX, GY = 16, 32, 32, 64, 8, 64, 1024
ZL, XL, YL = 8, 16, 256
F32, BF16 = jnp.float32, jnp.bfloat16
ROOT = math.sqrt(2.0 / math.pi)
VMEM = pl.BlockSpec(memory_space=pltpu.VMEM)
SMEM = pl.BlockSpec(memory_space=pltpu.SMEM)
HBM = pl.BlockSpec(memory_space=pltpu.HBM)


def cos_sin(freq, points, length):
    turn = np.mod(np.outer(freq, points), length) * (2.0 * np.pi / length)
    return np.cos(turn), np.sin(turn)


def split(table):
    table = np.asarray(table, np.float32)
    high = table.astype(jnp.bfloat16)
    low = (table - high.astype(np.float32)).astype(jnp.bfloat16)
    return high, low


@functools.cache
def tables():
    out = {}
    ky = np.arange(MY) - MY // 2
    cy, sy = cos_sin(ky, np.arange(GY), GY)
    rows = np.concatenate([cy, -sy]) / math.sqrt(GY)
    out["yf"] = np.concatenate(split(rows)).reshape(256, 8, 128).transpose(1, 0, 2)
    high, low = (half.reshape(128, 8, 128).transpose(1, 0, 2) for half in split(rows))
    out["yi"] = np.concatenate([high, low], axis=2)
    cf, sf = (
        np.einsum("kz,cd->czkd", w / math.sqrt(NZ), np.eye(8)).reshape(128, 2, 32)
        for w in cos_sin(np.arange(MZ), np.arange(NZ), NZ)
    )
    zf = np.zeros((2, 128, 2, 2, 32))
    zf[0, :, :, 0], zf[1, :, :, 0], zf[1, :, :, 1], zf[0, :, :, 1] = cf, sf, cf, -sf
    out["zf"] = np.concatenate(split(zf.reshape(256, 128)), axis=1)
    ci, si = (
        np.einsum("kz,op->zokp", w / math.sqrt(NZ), np.eye(16)).reshape(128, 2, 64)
        for w in cos_sin(np.arange(MZ), np.arange(ZL), NZ)
    )
    zi = np.zeros((2, 128, 2, 2, 64))
    zi[0, :, :, 0], zi[0, :, :, 1], zi[1, :, :, 0], zi[1, :, :, 1] = ci, -si, si, ci
    out["zi"] = np.concatenate(split(zi.reshape(256, 256)))
    kx = np.arange(MX) - MX // 2
    cx, sx = cos_sin(kx, np.arange(GX), GX)
    cr = (cx / 8.0).astype(np.float32).astype(jnp.bfloat16).astype(np.float64)
    sr = (-sx / 8.0).astype(np.float32).astype(jnp.bfloat16).astype(np.float64)
    cr, sr = cr.reshape(8, 4, 8, 2, 4), sr.reshape(8, 4, 8, 2, 4)
    xf = np.zeros((4, 2, 8, 4, 4, 8, 2, 4, 2))
    for k in range(4):
        for a in range(2):
            sign = -1.0 if k * a % 2 else 1.0
            real, imag = sign * cr[:, :, :, a], sign * sr[:, :, :, a]
            xf[k, 0, :, k, :, :, a, :, 0], xf[k, 0, :, k, :, :, a, :, 1] = real, -imag
            xf[k, 1, :, k, :, :, a, :, 0], xf[k, 1, :, k, :, :, a, :, 1] = imag, real
    out["xf"] = xf.reshape(4, 256, 128).astype(np.float32).astype(jnp.bfloat16)
    ic, is_ = (cx / 8.0).T.reshape(GX, 8, 1, 4), (sx / 8.0).T.reshape(GX, 8, 1, 4)
    xi = np.zeros((2, GX, 2, 8, 4, 4))
    xi[0, :, 0], xi[0, :, 1] = ic, -is_
    xi[1, :, 0], xi[1, :, 1] = is_, ic
    out["xi"] = np.stack(split(xi.reshape(128, 256)))
    return out


def iotas(shape):
    return lax.broadcasted_iota(jnp.int32, shape, 0), lax.broadcasted_iota(jnp.int32, shape, 1)


def halves(value):
    high = value.astype(BF16)
    return high, (value - high.astype(F32)).astype(BF16)


def dot(a, b, contract=((1,), (0,))):
    return lax.dot_general(a, b, (contract, ((), ())), preferred_element_type=F32)


def gelu(v):
    return 0.5 * v * (1.0 + jnp.tanh(ROOT * (v + 0.044715 * (v * v * v))))


def call(kernel, outs, in_specs, scratch=(), mib=16, flops=10**7, size=2**20):
    return pl.pallas_call(
        kernel,
        out_shape=[jax.ShapeDtypeStruct(s, d) for s, d in outs],
        in_specs=in_specs,
        out_specs=[VMEM] * len(outs),
        scratch_shapes=list(scratch),
        compiler_params=pltpu.CompilerParams(vmem_limit_bytes=mib << 20),
        cost_estimate=pl.CostEstimate(flops=flops, bytes_accessed=size, transcendentals=0),
    )


def rows_of(refs, field, slot, half):
    f, s, fp, sp = refs
    own, other = (s, sp) if field == 5 else (f.at[field], fp.at[field])
    start = 16 * (slot % 8) + 8 * half
    return (own if slot < 8 else other)[pl.ds(pl.multiple_of(start, 8), 8), :]


def edge_rows(f, s, out, rows):
    bottom = lax.axis_index("ga") == 0
    for field in range(6):
        for h in range(2):
            lanes = slice(128 * h, 128 * h + 128)
            rows[field, h] = s[:, lanes] if field == 5 else f[field, :, lanes]
            for d in range(3):
                first = rows[field, h, pl.ds(d, 8, stride=XL), :]
                last = rows[field, h, pl.ds(XL - 1 - d, 8, stride=XL), :]
                out[field, h, 8 * d : 8 * d + 8, :] = jnp.where(bottom, first, last)


def edge_lanes(f, s, first_slot, lows, highs):
    a = lax.axis_index("ga")
    lane = lax.broadcasted_iota(jnp.int32, (16, 128), 1) // 4
    for field in range(6):
        ref = s if field == 5 else f.at[field]
        low, high = lows[field // 2], highs[field // 2]
        for plane in range(8):
            base = 64 * (field % 2) + 4 * (first_slot + plane)
            both = [
                ref[pl.ds(pl.multiple_of(16 * plane + 8 * half, 8), 8), :] for half in (a, 1 - a)
            ]
            block = jnp.concatenate(both, axis=0)
            here = lane == base // 4
            low = jnp.where(here, turn(block[:, :128], base), low)
            high = jnp.where(here, turn(block[:, 128:], base + 4), high)
        lows[field // 2], highs[field // 2] = low, high


def turn(value, shift):
    return pltpu.roll(value, shift % 128, 1) if shift % 128 else value


def pack_own(f_far, s_far, own, lows, highs, rows, f, s, sems):
    copies = [
        pltpu.make_async_copy(f_far, f, sems.at[0]),
        pltpu.make_async_copy(s_far, s, sems.at[1]),
    ]
    for copy in copies:
        copy.start()
    for copy in copies:
        copy.wait()
    edge_rows(f, s, own, rows)
    low, high = ([jnp.zeros((16, 128), F32)] * 3 for _ in range(2))
    edge_lanes(f, s, 0, low, high)
    for pair in range(3):
        lows[pair], highs[pair] = low[pair], high[pair]


def pack_other(fp, sp, own, lows, highs, message, far, near, corner_far, corner_near, other, rows):
    edge_rows(fp, sp, other, rows)
    message[:, :, 0:24, :] = own[...]
    message[:, :, 24:48, :] = other[...]
    low, high = [lows[pair] for pair in range(3)], [highs[pair] for pair in range(3)]
    edge_lanes(fp, sp, 8, low, high)
    even = lax.axis_index("gy") % 2 == 0
    for pair in range(3):
        one = jnp.where(even, low[pair], high[pair])
        two = jnp.where(even, high[pair], low[pair])
        far[pair], near[pair] = one, two
        corner_far[pair], corner_near[pair] = one[:8], two[:8]


def stencil(f, s, fp, sp, got, far, near, corner_far, corner_near, last, a, b, stiff, outer):
    refs = (f, s, fp, sp)
    core = lax.axis_index("ga")
    even = lax.axis_index("gy") % 2 == 0
    row = lax.broadcasted_iota(jnp.int32, (8, 128), 0)
    beyond = jnp.where(core == 1, row, 7 - row) < 3
    first_lanes = lax.broadcasted_iota(jnp.int32, (16, 128), 1) < 64
    for field in range(6):
        for h in range(2):
            for which in range(2):
                for d in range(3):
                    at = 24 * which + 8 * d
                    value = got[field, h, at : at + 8, :]
                    to = 64 * (1 - which)
                    outer[h, pl.ds(to + d, 8, stride=8), :] = value
                    outer[h, pl.ds(to + 7 - d, 8, stride=8), :] = value
        pair = field // 2
        above = jnp.where(even, near[pair], far[pair])
        below = jnp.where(even, far[pair], near[pair])
        corner_above = jnp.where(even, corner_near[pair], corner_far[pair])
        corner_below = jnp.where(even, corner_far[pair], corner_near[pair])
        for slot in range(16):
            to = stiff.at[slot] if field == 5 else a.at[field, slot]
            to[0:8, 0:256] = rows_of(refs, field, slot, core)
            block = rows_of(refs, field, slot, 1 - core)
            for h in range(2):
                lanes = slice(128 * h, 128 * h + 128)
                edge = outer[h, 8 * slot : 8 * slot + 8, :]
                to[8:16, lanes] = jnp.where(beyond, edge, block[:, lanes])
            base = 64 * (field % 2) + 4 * slot
            side = jnp.where(first_lanes, turn(above, -base), turn(below, 124 - base))
            base = 64 * (field % 2) + 4 * (slot ^ 8)
            corner = jnp.where(
                first_lanes[:8], turn(corner_above, -base), turn(corner_below, 124 - base)
            )
            to[0:8, 256:384] = side[:8]
            to[8:16, 256:384] = jnp.where(beyond, corner, side[8:])

    def terms(src, field, slot, crop):
        mid = src[field, slot]
        up, down = src[field, (slot + 1) & 15], src[field, (slot + 15) & 15]
        xp, xm = pltpu.roll(mid, 15, 0), pltpu.roll(mid, 1, 0)
        yp, ym = pltpu.roll(mid, 383, 1), pltpu.roll(mid, 1, 1)
        if crop:
            mid, up, down, xp, xm, yp, ym = (v[0:8, 0:256] for v in (mid, up, down, xp, xm, yp, ym))
        total = 0.1 * mid + 0.12 * xp + 0.18 * xm + 0.17 * yp + 0.13 * ym
        return total + 0.14 * up + 0.16 * down, xp - xm, yp - ym, up - down

    def advance(src, slot, crop, store):
        vx, east, _, _ = terms(src, 1, slot, crop)
        vy, _, north, _ = terms(src, 2, slot, crop)
        vz, _, _, depth = terms(src, 3, slot, crop)
        div = 0.1 * (east + north + depth)
        store(0, terms(src, 0, slot, crop)[0] - div)
        pressure, east, north, depth = terms(src, 4, slot, crop)
        store(1, vx - 0.1 * east)
        store(2, vy - 0.1 * north)
        store(3, vz - 0.1 * depth)
        store(4, pressure - (stiff[slot, 0:8, 0:256] if crop else stiff[slot]) * div)

    for src, dst in ((a, b), (b, a), (a, None)):

        def body(slot, carry, src=src, dst=dst):
            def store(field, new):
                if dst is None:
                    rows = pl.ds(pl.multiple_of(slot * 8, 8), 8)
                    for h in range(2):
                        last[field, h, rows, :] = new[:, 128 * h : 128 * h + 128]
                else:
                    dst[field, slot] = new

            advance(src, slot, dst is None, store)
            return carry

        lax.fori_loop(0, 16, body, 0)


def lift_rows(values, weight, bias):
    rows = []
    for c in range(C):
        v = bias[c] + values[0] * weight[0, c]
        for field in range(1, 5):
            v = v + values[field] * weight[field, c]
        rows.append(gelu(v))
    return jnp.concatenate(rows, axis=0).astype(BF16)


def pointwise(keep, got, weight, bias, mix, obias, out, wide):
    a = lax.axis_index("ga")
    wide[pl.ds(pl.multiple_of(160 * a, 8), 160), :] = keep[...]
    wide[pl.ds(pl.multiple_of(160 * (1 - a), 8), 160), :] = got[...]
    row, lane = iotas((256, 32))
    pick = (row // 8 == lane).astype(BF16)
    bias_o = jnp.sum(jnp.where(row // 8 == lane, obias[...], 0.0), axis=1, keepdims=True)
    by_row = dot(pick, mix[...], ((1,), (1,))).astype(BF16)
    row, lane = iotas((256, 256))
    spread = jnp.where(row % 8 == lane % 8, dot(by_row, pick, ((1,), (1,))), 0.0).astype(BF16)

    def body(z, carry):
        values = [wide[pl.ds(8 * field + z, 8, stride=40), :] for field in range(5)]
        out[z] = dot(spread, lift_rows(values, weight, bias)) + bias_o
        return carry

    lax.fori_loop(0, ZL, body, 0)


def forward(
    last, after, weight, bias, yf_far, zf_far, keep, send, out, sums, lifted, modes, yf, zf, sems
):
    copies = [
        pltpu.make_async_copy(yf_far.at[lax.axis_index("gy")], yf, sems.at[0]),
        pltpu.make_async_copy(zf_far, zf, sems.at[1]),
    ]
    for copy in copies:
        copy.start()
    for half in range(2):
        for x in range(4):
            for field in range(5):
                at = 160 * half + 40 * x + 8 * field
                for h in range(2):
                    even = last[field, h, pl.ds(64 * half + 2 * x, 8, stride=8), :]
                    odd = last[field, h, pl.ds(64 * half + 2 * x + 1, 8, stride=8), :]
                    sums[at : at + 8, 128 * h : 128 * h + 128] = even + odd
    value = sums[...]
    high = value.astype(BF16)
    rest = value - high.astype(F32)
    mid, low = halves(rest)
    row, lane = iotas((256, 128))
    table = jnp.where(row // 2 == lane, 0.25, 0.0).astype(BF16)
    mean = dot(high, table) + dot(mid, table) + dot(low, table)
    keep[...] = mean[:160]
    send[...] = mean[160:]
    for x in range(4):
        at = [40 * x + 8 * field for field in range(5)]
        values = [jnp.concatenate([mean[r : r + 8], mean[r + 160 : r + 168]], axis=0) for r in at]
        lifted[x] = lift_rows(values, weight, bias)
    copies[0].wait()
    for x in range(4):
        both = dot(yf[...], lifted[x], ((1,), (1,)))
        modes[x] = both[:128] + both[128:]
    copies[1].wait()
    parts = []
    for group in range(4):
        lanes = slice(128 * group, 128 * group + 128)
        stack = [
            jnp.concatenate([modes[x, 0:64, lanes], modes[x, 64:128, lanes]], axis=1)
            for x in range(4)
        ]
        m_high, m_low = halves(jnp.concatenate(stack, axis=0))
        both = dot(m_high, zf[...])
        parts.append(both[:, :128] + both[:, 128:] + dot(m_low, zf[:, :128]))
    lane = lax.broadcasted_iota(jnp.int32, (256, 128), 1) // 32
    for part in range(4):
        total = parts[part]
        for group in range(4):
            if group != part:
                moved = pltpu.roll(parts[group], (32 * (group - part)) % 128, 1)
                total = jnp.where(lane == group, moved, total)
        for x in range(4):
            out[:, 8 * (part // 2) + 2 * x + part % 2, :] = total[64 * x : 64 * x + 64]


def mix_modes(got, weights, xf, xi, after, out):
    total = got[:, 0]
    for j in range(1, 8):
        total = total + got[:, j]
    high, low = halves(total.reshape(128, 128))
    row, lane = iotas((128, 128))
    modes = jnp.zeros((256, 128), F32)
    for k in range(4):
        spread = (row // 8 % 4 == k) & (row // 32 * 8 + row % 8 == lane // 4)
        spread = spread.astype(BF16)
        modes = modes + dot(xf[k], dot(high, spread).astype(BF16))
        modes = modes + dot(xf[k], dot(low, spread).astype(BF16))
    real, imag = modes[:128], modes[128:]
    total = jnp.zeros((256, 128), F32)
    for i in range(8):
        wr = weights[8 * i : 8 * i + 8, 0:16, :].astype(F32).reshape(128, 128)
        wi = weights[8 * i : 8 * i + 8, 16:32, :].astype(F32).reshape(128, 128)
        part = jnp.concatenate([wr * real - wi * imag, wr * imag + wi * real], axis=0)
        p_high, p_low = halves(part)
        gather = (lane // 64 * 16 + lane % 16 == 4 * i + row % 4).astype(BF16)
        total = total + dot(p_high, gather) + dot(p_low, gather)
    row, lane = iotas((256, 128))
    total = jnp.where((row // 4) % 4 == (lane // 16) % 4, total, 0.0)
    t_high, t_low = halves(total)
    back = dot(xi[0], t_high) + dot(xi[0], t_low) + dot(xi[1], t_high)
    real, imag = back[:64], back[64:]
    lane = lax.broadcasted_iota(jnp.int32, (64, 128), 1)
    parts = [
        jnp.where(lane < 64, real, pltpu.roll(imag, 64, 1)),
        jnp.where(lane < 64, pltpu.roll(real, 64, 1), imag),
    ]
    odd = (lane // 16) % 2 == 1
    for a in range(2):
        signed = [jnp.where(odd, -part, part) for part in parts] if a else parts
        for i in range(8):
            rows = slice(8 * i, 8 * i + 8)
            tile = jnp.concatenate([part[rows] for part in signed], axis=0).astype(BF16)
            for j in range(8):
                out[i, j, a] = tile


def finish(got, direct, yi_far, zi_far, out, rows, spectral, yi, zi, sems):
    copies = [
        pltpu.make_async_copy(yi_far.at[lax.axis_index("gy")], yi, sems.at[0]),
        pltpu.make_async_copy(zi_far, zi, sems.at[1]),
    ]
    for copy in copies:
        copy.start()
    rows[...] = got[...].astype(F32)
    for copy in copies:
        copy.wait()
    by_z = []
    for part in range(2):
        stack = []
        for x in range(8):
            pair = [rows[pl.ds(16 * a + 8 * part + x, 64, stride=32), :] for a in range(2)]
            stack.append(jnp.concatenate(pair, axis=1).astype(BF16))
        both = dot(zi[...], jnp.concatenate(stack, axis=0), ((1,), (1,)))
        by_z.append(both[:256] + both[256:])
    blank = jnp.zeros((64, 128), BF16)

    def twice(lanes):
        real, imag = yi[0:64, lanes], yi[64:128, lanes]
        pieces = [[real, blank], [blank, real], [imag, blank], [blank, imag]]
        return jnp.concatenate([jnp.concatenate(row, axis=1) for row in pieces], axis=0)

    t_high, t_low = twice(slice(0, 128)), twice(slice(128, 256))
    for pair in range(4):
        lanes = slice(128 * pair, 128 * pair + 128)
        value = jnp.concatenate(
            [jnp.concatenate([v[:128, lanes], v[128:, lanes]], axis=1) for v in by_z], axis=0
        )
        high, low = halves(value)
        both = dot(high, t_high) + dot(low, t_high) + dot(high, t_low)
        for x in range(2):
            spectral[pl.ds(2 * pair + x, 256, stride=8), :] = both[:, 128 * x : 128 * x + 128]
    for part in range(2):
        for z in range(ZL):
            at = 128 * (8 * part + z)
            branch = spectral[at : at + 128, :].astype(BF16).astype(F32)
            total = gelu(direct[z, 128 * part : 128 * part + 128, :] + branch)
            out[z, 16 * part : 16 * part + 16] = total.reshape(16, 8, 128).astype(BF16)


def turn_weights(weights, after, out, wide):
    for chunk in range(16):
        turned = weights[128 * chunk : 128 * chunk + 128, :].T
        for ri in range(2):
            wide[:, 16 * ri + chunk, :] = turned[64 * ri : 64 * ri + 64]
    out[...] = wide[...].astype(BF16)


def shards(fields, stiffness, lift_weight, lift_bias, mix_weight, spectral_weight, output_bias):
    table = {name: jnp.asarray(value) for name, value in tables().items()}
    everyone = ("gx", "gy", "ga")

    def exchange(value, axis):
        return lax.all_to_all(value, axis, split_axis=0, concat_axis=0, tiled=True)

    anywhere = pl.BlockSpec(memory_space=pl.ANY)
    f = fields.reshape(5, 128, 256)
    s = stiffness.reshape(128, 256)
    swap = [(0, 1), (1, 0)]
    fp, sp = lax.ppermute(f, "ga", swap), lax.ppermute(s, "ga", swap)
    rows = pltpu.VMEM((6, 2, 128, 128), F32)
    edges, lanes = ((6, 2, 24, 128), F32), ((3, 16, 128), F32)
    own, lows, highs = call(
        pack_own,
        [edges, lanes, lanes],
        [HBM] * 2,
        [
            rows,
            pltpu.VMEM((5, 128, 256), F32),
            pltpu.VMEM((128, 256), F32),
            pltpu.SemaphoreType.DMA((2,)),
        ],
    )(f, s)
    corners = ((3, 8, 128), F32)
    message, far, near, corner_far, corner_near = call(
        pack_other,
        [((6, 2, 48, 128), F32), lanes, lanes, corners, corners],
        [VMEM] * 5,
        [pltpu.VMEM(*edges), rows],
    )(fp, sp, own, lows, highs)
    meets = [(2 * i + a, 2 * ((i - 1 + 2 * a) % 8) + 1 - a) for i in range(8) for a in range(2)]
    far_pairs = [(j, (j - 1 + 2 * (j % 2)) % 8) for j in range(8)]
    near_pairs = [(j, j + 1 - 2 * (j % 2)) for j in range(8)]

    def diagonal(pairs):
        return [
            (16 * (u // 2) + 2 * j + u % 2, 16 * (v // 2) + 2 * k + v % 2)
            for u, v in meets
            for j, k in pairs
        ]

    got = lax.ppermute(message, ("gx", "ga"), meets)
    far = lax.ppermute(far, "gy", far_pairs)
    got_far = lax.ppermute(corner_far, everyone, diagonal(far_pairs))
    near = lax.ppermute(near, "gy", near_pairs)
    got_near = lax.ppermute(corner_near, everyone, diagonal(near_pairs))

    [turned] = call(
        turn_weights,
        [((64, 32, 128), BF16)],
        [VMEM, anywhere],
        [pltpu.VMEM((64, 32, 128), F32)],
    )(spectral_weight.reshape(2048, 128), corner_near)
    weights = exchange(turned, ("gx", "gy"))

    [last] = call(
        stencil,
        [((5, 2, 128, 128), F32)],
        [VMEM] * 9,
        [
            pltpu.VMEM((5, 16, 16, 384), F32),
            pltpu.VMEM((5, 16, 16, 384), F32),
            pltpu.VMEM((16, 16, 384), F32),
            pltpu.VMEM((2, 128, 128), F32),
        ],
        flops=10**12,
    )(f, s, fp, sp, got, far, near, got_far, got_near)
    keep, send, modes = call(
        forward,
        [((160, 128), F32), ((160, 128), F32), ((64, 16, 128), F32)],
        [VMEM, anywhere, SMEM, SMEM, HBM, HBM],
        [
            pltpu.VMEM((320, 256), F32),
            pltpu.VMEM((4, 512, 128), BF16),
            pltpu.VMEM((4, 128, 512), F32),
            pltpu.VMEM((256, 128), BF16),
            pltpu.VMEM((256, 256), BF16),
            pltpu.SemaphoreType.DMA((2,)),
        ],
    )(last, weights, lift_weight, lift_bias, table["yf"], table["zf"])
    modes = exchange(modes.reshape(128, 8, 128), everyone)
    [direct] = call(
        pointwise,
        [((8, 256, 128), F32)],
        [VMEM, VMEM, SMEM, SMEM, VMEM, VMEM],
        [pltpu.VMEM((320, 128), F32)],
        flops=3 * 10**8,
    )(keep, lax.ppermute(send, "ga", swap), lift_weight, lift_bias, mix_weight, output_bias.reshape(1, C))

    [mixed] = call(mix_modes, [((8, 8, 2, 16, 128), BF16)], [VMEM] * 4 + [anywhere])(
        modes.reshape(8, 8, 16, 128), weights, table["xf"], table["xi"], direct
    )
    mixed = exchange(mixed.reshape(128, 16, 128), everyone)
    [out] = call(
        finish,
        [((8, 32, 8, 128), BF16)],
        [VMEM, VMEM, HBM, HBM],
        [
            pltpu.VMEM((2048, 128), F32),
            pltpu.VMEM((2048, 128), F32),
            pltpu.VMEM((128, 256), BF16),
            pltpu.VMEM((512, 256), BF16),
            pltpu.SemaphoreType.DMA((2,)),
        ],
    )(mixed.reshape(2048, 128), direct, table["yi"], table["zi"])
    return out


def solution(mesh):
    placed = (
        P(None, "ga", "gx", "gy"),
        P("ga", "gx", "gy"),
        P(),
        P(),
        P(),
        P("ga", "gy", None, "gx", None),
        P(),
    )
    return jax.shard_map(
        shards, mesh=mesh, in_specs=placed, out_specs=P("ga", None, "gx", "gy"), check_vma=False
    )
```

```python
import functools
import math

import jax
import jax.numpy as jnp
import numpy as np
from jax import lax
from jax.experimental import pallas as pl
from jax.experimental.pallas import tpu as pltpu
from jax.sharding import PartitionSpec as P

NZ, C, MX, MY, MZ, GX, GY = 16, 32, 32, 64, 8, 64, 1024
ZL, XL, YL = 8, 16, 256
F32, BF16 = jnp.float32, jnp.bfloat16
ROOT = math.sqrt(2.0 / math.pi)
VMEM = pl.BlockSpec(memory_space=pltpu.VMEM)
SMEM = pl.BlockSpec(memory_space=pltpu.SMEM)


def cos_sin(freq, points, length):
    turn = np.mod(np.outer(freq, points), length) * (2.0 * np.pi / length)
    return np.cos(turn), np.sin(turn)


def split(table):
    table = np.asarray(table, np.float32)
    high = table.astype(jnp.bfloat16)
    low = (table - high.astype(np.float32)).astype(jnp.bfloat16)
    return high, low


@functools.cache
def tables():
    out = {}
    ky = np.arange(MY) - MY // 2
    cy, sy = cos_sin(ky, np.arange(GY), GY)
    rows = np.concatenate([cy, -sy]) / math.sqrt(GY)
    out["yf"] = np.concatenate(split(rows)).reshape(256, 8, 128).transpose(1, 0, 2)
    high, low = (half.reshape(128, 8, 128).transpose(1, 0, 2) for half in split(rows))
    out["yi"] = np.concatenate([high, low], axis=2)
    cf, sf = (
        np.einsum("kz,cd->czkd", w / math.sqrt(NZ), np.eye(8)).reshape(128, 2, 32)
        for w in cos_sin(np.arange(MZ), np.arange(NZ), NZ)
    )
    zf = np.zeros((2, 128, 2, 2, 32))
    zf[0, :, :, 0], zf[1, :, :, 0], zf[1, :, :, 1], zf[0, :, :, 1] = cf, sf, cf, -sf
    out["zf"] = np.concatenate(split(zf.reshape(256, 128)), axis=1)
    ci, si = (
        np.einsum("kz,op->zokp", w / math.sqrt(NZ), np.eye(16)).reshape(128, 2, 64)
        for w in cos_sin(np.arange(MZ), np.arange(ZL), NZ)
    )
    zi = np.zeros((2, 128, 2, 2, 64))
    zi[0, :, :, 0], zi[0, :, :, 1], zi[1, :, :, 0], zi[1, :, :, 1] = ci, -si, si, ci
    out["zi"] = np.concatenate(split(zi.reshape(256, 256)))
    kx = np.arange(MX) - MX // 2
    cx, sx = cos_sin(kx, np.arange(GX), GX)
    cr = (cx / 8.0).astype(np.float32).astype(jnp.bfloat16).astype(np.float64)
    sr = (-sx / 8.0).astype(np.float32).astype(jnp.bfloat16).astype(np.float64)
    cr, sr = cr.reshape(8, 4, 8, 2, 4), sr.reshape(8, 4, 8, 2, 4)
    xf = np.zeros((4, 2, 8, 4, 4, 8, 2, 4, 2))
    for k in range(4):
        for a in range(2):
            sign = -1.0 if k * a % 2 else 1.0
            real, imag = sign * cr[:, :, :, a], sign * sr[:, :, :, a]
            xf[k, 0, :, k, :, :, a, :, 0], xf[k, 0, :, k, :, :, a, :, 1] = real, -imag
            xf[k, 1, :, k, :, :, a, :, 0], xf[k, 1, :, k, :, :, a, :, 1] = imag, real
    xf = xf.reshape(4, 256, 128).transpose(1, 0, 2).reshape(256, 512)
    out["xf"] = xf.astype(np.float32).astype(jnp.bfloat16)
    ic, is_ = (cx / 8.0).T.reshape(GX, 8, 1, 4), (sx / 8.0).T.reshape(GX, 8, 1, 4)
    xi = np.zeros((2, GX, 2, 8, 4, 4))
    xi[0, :, 0], xi[0, :, 1] = ic, -is_
    xi[1, :, 0], xi[1, :, 1] = is_, ic
    out["xi"] = np.concatenate(split(xi.reshape(128, 256)))
    return out


def iotas(shape):
    return lax.broadcasted_iota(jnp.int32, shape, 0), lax.broadcasted_iota(jnp.int32, shape, 1)


def halves(value):
    high = value.astype(BF16)
    return high, (value - high.astype(F32)).astype(BF16)


def dot(a, b, contract=((1,), (0,))):
    return lax.dot_general(a, b, (contract, ((), ())), preferred_element_type=F32)


def gelu(v):
    return 0.5 * v * (1.0 + jnp.tanh(ROOT * (v + 0.044715 * (v * v * v))))


def call(kernel, outs, in_specs, scratch=(), mib=16, flops=10**7, size=2**20):
    return pl.pallas_call(
        kernel,
        out_shape=[jax.ShapeDtypeStruct(s, d) for s, d in outs],
        in_specs=in_specs,
        out_specs=[VMEM] * len(outs),
        scratch_shapes=list(scratch),
        compiler_params=pltpu.CompilerParams(vmem_limit_bytes=mib << 20),
        cost_estimate=pl.CostEstimate(flops=flops, bytes_accessed=size, transcendentals=0),
    )


def rows_of(refs, field, slot, half):
    f, s, fp, sp = refs
    own, other = (s, sp) if field == 5 else (f.at[field], fp.at[field])
    start = 16 * (slot % 8) + 8 * half
    return (own if slot < 8 else other)[pl.ds(pl.multiple_of(start, 8), 8), :]


def edge_rows(f, s, out, rows):
    bottom = lax.axis_index("ga") == 0
    for field in range(6):
        for h in range(2):
            lanes = slice(128 * h, 128 * h + 128)
            rows[field, h] = s[:, lanes] if field == 5 else f[field, :, lanes]
            for d in range(3):
                first = rows[field, h, pl.ds(d, 8, stride=XL), :]
                last = rows[field, h, pl.ds(XL - 1 - d, 8, stride=XL), :]
                out[field, h, 8 * d : 8 * d + 8, :] = jnp.where(bottom, first, last)


def pack_own(f, s, own, rows):
    edge_rows(f, s, own, rows)


def pack_other(fp, sp, own, message, other, rows):
    edge_rows(fp, sp, other, rows)
    message[:, :, 0:24, :] = own[...]
    message[:, :, 24:48, :] = other[...]


def pack_y(f, s, fp, sp, message, after, far, near, outer):
    refs = (f, s, fp, sp)
    a = lax.axis_index("ga")
    row = lax.broadcasted_iota(jnp.int32, (8, 128), 0)
    beyond = jnp.where(a == 1, row, 7 - row) < 3
    lane = lax.broadcasted_iota(jnp.int32, (16, 128), 1) // 4
    lows, highs = jnp.zeros((16, 128), F32), jnp.zeros((16, 128), F32)
    for field in range(6):
        for h in range(2):
            for which in range(2):
                for d in range(3):
                    at = 24 * which + 8 * d
                    value = message[field, h, at : at + 8, :]
                    to = 64 * (1 - which)
                    outer[field, h, pl.ds(to + d, 8, stride=8), :] = value
                    outer[field, h, pl.ds(to + 7 - d, 8, stride=8), :] = value
        for slot in range(16):
            inner, block = rows_of(refs, field, slot, a), rows_of(refs, field, slot, 1 - a)
            edge = slice(8 * slot, 8 * slot + 8)
            for h in range(2):
                kept = block[:, 128 * h : 128 * h + 128]
                outer[field, h, edge, :] = jnp.where(beyond, outer[field, h, edge, :], kept)
            base = 64 * (field % 2) + 4 * slot
            here = lane == base // 4
            first = jnp.concatenate([inner[:, :128], outer[field, 0, edge, :]], axis=0)
            last = jnp.concatenate([inner[:, 128:], outer[field, 1, edge, :]], axis=0)
            lows = jnp.where(here, pltpu.roll(first, base, 1) if base else first, lows)
            highs = jnp.where(here, pltpu.roll(last, (base + 4) % 128, 1) if base != 124 else last, highs)
        if field % 2:
            even = lax.axis_index("gy") % 2 == 0
            far[field // 2] = jnp.where(even, lows, highs)
            near[field // 2] = jnp.where(even, highs, lows)


def stencil(f, s, fp, sp, got, far, near, last, a, b, stiff, outer):
    refs = (f, s, fp, sp)
    core = lax.axis_index("ga")
    even = lax.axis_index("gy") % 2 == 0
    first_lanes = lax.broadcasted_iota(jnp.int32, (16, 128), 1) < 64
    row = lax.broadcasted_iota(jnp.int32, (8, 128), 0)
    beyond = jnp.where(core == 1, row, 7 - row) < 3
    for field in range(6):
        for h in range(2):
            for which in range(2):
                for d in range(3):
                    at = 24 * which + 8 * d
                    value = got[field, h, at : at + 8, :]
                    to = 64 * (1 - which)
                    outer[h, pl.ds(to + d, 8, stride=8), :] = value
                    outer[h, pl.ds(to + 7 - d, 8, stride=8), :] = value
        one, two = near[field // 2], far[field // 2]
        above, below = jnp.where(even, one, two), jnp.where(even, two, one)
        for slot in range(16):
            to = stiff.at[slot] if field == 5 else a.at[field, slot]
            to[0:8, 0:256] = rows_of(refs, field, slot, core)
            block = rows_of(refs, field, slot, 1 - core)
            for h in range(2):
                lanes = slice(128 * h, 128 * h + 128)
                edge = outer[h, 8 * slot : 8 * slot + 8, :]
                to[8:16, lanes] = jnp.where(beyond, edge, block[:, lanes])
            base = 64 * (field % 2) + 4 * slot
            up = pltpu.roll(above, 128 - base, 1) if base else above
            down = pltpu.roll(below, 124 - base, 1) if base != 124 else below
            to[:, 256:384] = jnp.where(first_lanes, up, down)

    def terms(src, field, slot, crop):
        mid = src[field, slot]
        up, down = src[field, (slot + 1) & 15], src[field, (slot + 15) & 15]
        xp, xm = pltpu.roll(mid, 15, 0), pltpu.roll(mid, 1, 0)
        yp, ym = pltpu.roll(mid, 383, 1), pltpu.roll(mid, 1, 1)
        if crop:
            mid, up, down, xp, xm, yp, ym = (v[0:8, 0:256] for v in (mid, up, down, xp, xm, yp, ym))
        total = 0.1 * mid + 0.12 * xp + 0.18 * xm + 0.17 * yp + 0.13 * ym
        return total + 0.14 * up + 0.16 * down, xp - xm, yp - ym, up - down

    def advance(src, slot, crop, store):
        vx, east, _, _ = terms(src, 1, slot, crop)
        vy, _, north, _ = terms(src, 2, slot, crop)
        vz, _, _, depth = terms(src, 3, slot, crop)
        div = 0.1 * (east + north + depth)
        store(0, terms(src, 0, slot, crop)[0] - div)
        pressure, east, north, depth = terms(src, 4, slot, crop)
        store(1, vx - 0.1 * east)
        store(2, vy - 0.1 * north)
        store(3, vz - 0.1 * depth)
        store(4, pressure - (stiff[slot, 0:8, 0:256] if crop else stiff[slot]) * div)

    for src, dst in ((a, b), (b, a), (a, None)):

        def body(slot, carry, src=src, dst=dst):
            def store(field, new):
                if dst is None:
                    rows = pl.ds(pl.multiple_of(slot * 8, 8), 8)
                    for h in range(2):
                        last[field, h, rows, :] = new[:, 128 * h : 128 * h + 128]
                else:
                    dst[field, slot] = new

            advance(src, slot, dst is None, store)
            return carry

        lax.fori_loop(0, 16, body, 0, unroll=True)


def lift_rows(values, weight, bias):
    rows = []
    for c in range(C):
        v = bias[c] + values[0] * weight[0, c]
        for field in range(1, 5):
            v = v + values[field] * weight[field, c]
        rows.append(gelu(v))
    return jnp.concatenate(rows, axis=0).astype(BF16)


def pointwise(keep, got, weight, bias, mix, obias, out, wide):
    a = lax.axis_index("ga")
    wide[pl.ds(pl.multiple_of(160 * a, 8), 160), :] = keep[...]
    wide[pl.ds(pl.multiple_of(160 * (1 - a), 8), 160), :] = got[...]
    row, lane = iotas((256, 32))
    pick = (row // 8 == lane).astype(BF16)
    bias_o = jnp.sum(jnp.where(row // 8 == lane, obias[...], 0.0), axis=1, keepdims=True)
    by_row = dot(pick, mix[...], ((1,), (1,))).astype(BF16)
    row, lane = iotas((256, 256))
    spread = jnp.where(row % 8 == lane % 8, dot(by_row, pick, ((1,), (1,))), 0.0).astype(BF16)

    def body(z, carry):
        values = [wide[pl.ds(8 * field + z, 8, stride=40), :] for field in range(5)]
        out[z] = dot(spread, lift_rows(values, weight, bias)) + bias_o
        return carry

    lax.fori_loop(0, ZL, body, 0)


def forward(
    last, after, weight, bias, yf_far, zf_far, keep, send, out, sums, lifted, modes, yf, zf, sems
):
    copies = [
        pltpu.make_async_copy(yf_far.at[lax.axis_index("gy")], yf, sems.at[0]),
        pltpu.make_async_copy(zf_far, zf, sems.at[1]),
    ]
    for copy in copies:
        copy.start()
    for half in range(2):
        for x in range(4):
            for field in range(5):
                at = 160 * half + 40 * x + 8 * field
                for h in range(2):
                    even = last[field, h, pl.ds(64 * half + 2 * x, 8, stride=8), :]
                    odd = last[field, h, pl.ds(64 * half + 2 * x + 1, 8, stride=8), :]
                    sums[at : at + 8, 128 * h : 128 * h + 128] = even + odd
    value = sums[...]
    high = value.astype(BF16)
    rest = value - high.astype(F32)
    mid, low = halves(rest)
    row, lane = iotas((256, 128))
    table = jnp.where(row // 2 == lane, 0.25, 0.0).astype(BF16)
    mean = dot(high, table) + dot(mid, table) + dot(low, table)
    keep[...] = mean[:160]
    send[...] = mean[160:]
    for x in range(4):
        at = [40 * x + 8 * field for field in range(5)]
        values = [jnp.concatenate([mean[r : r + 8], mean[r + 160 : r + 168]], axis=0) for r in at]
        lifted[x] = lift_rows(values, weight, bias)
    copies[0].wait()
    for x in range(4):
        both = dot(yf[...], lifted[x], ((1,), (1,)))
        modes[x] = both[:128] + both[128:]
    copies[1].wait()
    parts = []
    for group in range(4):
        lanes = slice(128 * group, 128 * group + 128)
        stack = [
            jnp.concatenate([modes[x, 0:64, lanes], modes[x, 64:128, lanes]], axis=1)
            for x in range(4)
        ]
        m_high, m_low = halves(jnp.concatenate(stack, axis=0))
        both = dot(m_high, zf[...])
        parts.append(both[:, :128] + both[:, 128:] + dot(m_low, zf[:, :128]))
    lane = lax.broadcasted_iota(jnp.int32, (256, 128), 1) // 32
    for part in range(4):
        total = parts[part]
        for group in range(4):
            if group != part:
                moved = pltpu.roll(parts[group], (32 * (group - part)) % 128, 1)
                total = jnp.where(lane == group, moved, total)
        for x in range(4):
            rows = pl.ds(8 * (part // 2) + 2 * x + part % 2, 64, stride=16)
            out[rows, :] = total[64 * x : 64 * x + 64]


def mix_modes(got, weights, xf, xi, after, out):
    total = got[:, 0]
    for j in range(1, 8):
        total = total + got[:, j]
    both = jnp.concatenate(halves(total.reshape(128, 128)), axis=0)
    row, lane = iotas((128, 512))
    spread = (row // 8 % 4 == lane // 128) & (row // 32 * 8 + row % 8 == lane % 128 // 4)
    wide = dot(both, spread.astype(BF16)).astype(BF16)
    pieces = [
        jnp.concatenate([wide[:128, 128 * k : 128 * k + 128], wide[128:, 128 * k : 128 * k + 128]], axis=1)
        for k in range(4)
    ]
    modes = dot(xf[...], jnp.concatenate(pieces, axis=0))
    modes = modes[:, :128] + modes[:, 128:]
    real, imag = modes[:128], modes[128:]
    highs, lows = [], []
    for i in range(8):
        wr = weights[8 * i : 8 * i + 8, 0:16, :].astype(F32).reshape(128, 128)
        wi = weights[8 * i : 8 * i + 8, 16:32, :].astype(F32).reshape(128, 128)
        high, low = halves(
            jnp.concatenate([wr * real - wi * imag, wr * imag + wi * real], axis=0)
        )
        highs.append(high)
        lows.append(low)
    row, lane = iotas((1024, 128))
    gather = (lane // 64 * 16 + lane % 16 == 4 * (row // 128) + row % 4).astype(BF16)
    parts = [jnp.concatenate(part, axis=1) for part in (highs, lows)]
    total = dot(jnp.concatenate(parts, axis=0), gather)
    total = total[:256] + total[256:]
    row, lane = iotas((256, 128))
    total = jnp.where((row // 4) % 4 == (lane // 16) % 4, total, 0.0)
    back = dot(xi[...], jnp.concatenate(halves(total), axis=1))
    back = back[:128, :128] + back[:128, 128:] + back[128:, :128]
    real, imag = back[:64], back[64:]
    lane = lax.broadcasted_iota(jnp.int32, (64, 128), 1)
    parts = [
        jnp.where(lane < 64, real, pltpu.roll(imag, 64, 1)),
        jnp.where(lane < 64, pltpu.roll(real, 64, 1), imag),
    ]
    odd = (lane // 16) % 2 == 1
    for a in range(2):
        signed = [jnp.where(odd, -part, part) for part in parts] if a else parts
        for i in range(8):
            rows = slice(8 * i, 8 * i + 8)
            tile = jnp.concatenate([part[rows] for part in signed], axis=0).astype(BF16)
            for j in range(8):
                out[i, j, a] = tile


def finish(got, direct, yi_far, zi_far, out, rows, spectral, yi, zi, sems):
    copies = [
        pltpu.make_async_copy(yi_far.at[lax.axis_index("gy")], yi, sems.at[0]),
        pltpu.make_async_copy(zi_far, zi, sems.at[1]),
    ]
    for copy in copies:
        copy.start()
    rows[...] = got[...].astype(F32)
    for copy in copies:
        copy.wait()
    by_z = []
    for part in range(2):
        stack = []
        for x in range(8):
            pair = [rows[pl.ds(16 * a + 8 * part + x, 64, stride=32), :] for a in range(2)]
            stack.append(jnp.concatenate(pair, axis=1).astype(BF16))
        both = dot(zi[...], jnp.concatenate(stack, axis=0), ((1,), (1,)))
        by_z.append(both[:256] + both[256:])
    blank = jnp.zeros((64, 128), BF16)

    def twice(lanes):
        real, imag = yi[0:64, lanes], yi[64:128, lanes]
        pieces = [[real, blank], [blank, real], [imag, blank], [blank, imag]]
        return jnp.concatenate([jnp.concatenate(row, axis=1) for row in pieces], axis=0)

    t_high, t_low = twice(slice(0, 128)), twice(slice(128, 256))
    for pair in range(4):
        lanes = slice(128 * pair, 128 * pair + 128)
        value = jnp.concatenate(
            [jnp.concatenate([v[:128, lanes], v[128:, lanes]], axis=1) for v in by_z], axis=0
        )
        high, low = halves(value)
        both = dot(high, t_high) + dot(low, t_high) + dot(high, t_low)
        for x in range(2):
            spectral[pl.ds(2 * pair + x, 256, stride=8), :] = both[:, 128 * x : 128 * x + 128]
    for part in range(2):
        for z in range(ZL):
            at = 128 * (8 * part + z)
            branch = spectral[at : at + 128, :].astype(BF16).astype(F32)
            total = gelu(direct[z, 128 * part : 128 * part + 128, :] + branch)
            out[z, 16 * part : 16 * part + 16] = total.reshape(16, 8, 128).astype(BF16)


def turn_weights(weights, after, out, wide):
    for chunk in range(16):
        turned = weights[128 * chunk : 128 * chunk + 128, :].T
        for ri in range(2):
            wide[:, 16 * ri + chunk, :] = turned[64 * ri : 64 * ri + 64]
    out[...] = wide[...].astype(BF16)


def shards(fields, stiffness, lift_weight, lift_bias, mix_weight, spectral_weight, output_bias):
    table = {name: jnp.asarray(value) for name, value in tables().items()}
    everyone = ("gx", "gy", "ga")

    def exchange(value, axis):
        return lax.all_to_all(value, axis, split_axis=0, concat_axis=0, tiled=True)

    anywhere = pl.BlockSpec(memory_space=pl.ANY)
    f = fields.reshape(5, 128, 256)
    s = stiffness.reshape(128, 256)
    swap = [(0, 1), (1, 0)]
    fp, sp = lax.ppermute(f, "ga", swap), lax.ppermute(s, "ga", swap)
    rows = pltpu.VMEM((6, 2, 128, 128), F32)
    edges = ((6, 2, 24, 128), F32)
    [own] = call(pack_own, [edges], [VMEM] * 2, [rows])(f, s)
    [message] = call(
        pack_other, [((6, 2, 48, 128), F32)], [VMEM] * 3, [pltpu.VMEM(*edges), rows]
    )(fp, sp, own)
    across = [(2 * i, 2 * ((i - 1) % 8) + 1) for i in range(8)]
    across += [(2 * i + 1, 2 * ((i + 1) % 8)) for i in range(8)]
    got = lax.ppermute(message, ("gx", "ga"), across)

    [turned] = call(
        turn_weights,
        [((64, 32, 128), BF16)],
        [VMEM, anywhere],
        [pltpu.VMEM((64, 32, 128), F32)],
        size=2 * 10**7,
    )(spectral_weight.reshape(2048, 128), message)
    weights = exchange(turned, ("gx", "gy"))

    message = ((3, 16, 128), F32)
    far, near = call(
        pack_y, [message, message], [VMEM] * 5 + [anywhere], [pltpu.VMEM((6, 2, 128, 128), F32)]
    )(f, s, fp, sp, got, turned)
    far = lax.ppermute(far, "gy", [(j, (j - 1 + 2 * (j % 2)) % 8) for j in range(8)])
    near = lax.ppermute(near, "gy", [(j, j + 1 - 2 * (j % 2)) for j in range(8)])
    [last] = call(
        stencil,
        [((5, 2, 128, 128), F32)],
        [VMEM] * 7,
        [
            pltpu.VMEM((5, 16, 16, 384), F32),
            pltpu.VMEM((5, 16, 16, 384), F32),
            pltpu.VMEM((16, 16, 384), F32),
            pltpu.VMEM((2, 128, 128), F32),
        ],
        flops=10**12,
    )(f, s, fp, sp, got, far, near)
    keep, send, modes = call(
        forward,
        [((160, 128), F32), ((160, 128), F32), ((1024, 128), F32)],
        [VMEM, anywhere, SMEM, SMEM, anywhere, anywhere],
        [
            pltpu.VMEM((320, 256), F32),
            pltpu.VMEM((4, 512, 128), BF16),
            pltpu.VMEM((4, 128, 512), F32),
            pltpu.VMEM((256, 128), BF16),
            pltpu.VMEM((256, 256), BF16),
            pltpu.SemaphoreType.DMA((2,)),
        ],
    )(last, weights, lift_weight, lift_bias, table["yf"], table["zf"])
    modes = exchange(modes.reshape(128, 8, 128), everyone)
    [direct] = call(
        pointwise,
        [((8, 256, 128), F32)],
        [VMEM, VMEM, SMEM, SMEM, VMEM, VMEM],
        [pltpu.VMEM((320, 128), F32)],
        flops=3 * 10**8,
    )(keep, lax.ppermute(send, "ga", swap), lift_weight, lift_bias, mix_weight, output_bias.reshape(1, C))

    [mixed] = call(mix_modes, [((8, 8, 2, 16, 128), BF16)], [VMEM] * 4 + [anywhere])(
        modes.reshape(8, 8, 16, 128), weights, table["xf"], table["xi"], direct
    )
    mixed = exchange(mixed.reshape(128, 16, 128), everyone)
    [out] = call(
        finish,
        [((8, 32, 8, 128), BF16)],
        [VMEM, VMEM, anywhere, anywhere],
        [
            pltpu.VMEM((2048, 128), F32),
            pltpu.VMEM((2048, 128), F32),
            pltpu.VMEM((128, 256), BF16),
            pltpu.VMEM((512, 256), BF16),
            pltpu.SemaphoreType.DMA((2,)),
        ],
    )(mixed.reshape(2048, 128), direct, table["yi"], table["zi"])
    return out


def solution(mesh):
    placed = (
        P(None, "ga", "gx", "gy"),
        P("ga", "gx", "gy"),
        P(),
        P(),
        P(),
        P("ga", "gy", None, "gx", None),
        P(),
    )
    return jax.shard_map(
        shards, mesh=mesh, in_specs=placed, out_specs=P("ga", None, "gx", "gy"), check_vma=False
    )
```

```python
import functools
import math

import jax
import jax.numpy as jnp
import numpy as np
from jax import lax
from jax.experimental import pallas as pl
from jax.experimental.pallas import tpu as pltpu
from jax.sharding import PartitionSpec as P

NZ, C, MX, MY, MZ, GX, GY = 16, 32, 32, 64, 8, 64, 1024
ZL, XL, YL = 8, 16, 256
F32, BF16 = jnp.float32, jnp.bfloat16
ROOT = math.sqrt(2.0 / math.pi)
VMEM = pl.BlockSpec(memory_space=pltpu.VMEM)
SMEM = pl.BlockSpec(memory_space=pltpu.SMEM)


def cos_sin(freq, points, length):
    turn = np.mod(np.outer(freq, points), length) * (2.0 * np.pi / length)
    return np.cos(turn), np.sin(turn)


def split(table):
    table = np.asarray(table, np.float32)
    high = table.astype(jnp.bfloat16)
    low = (table - high.astype(np.float32)).astype(jnp.bfloat16)
    return high, low


@functools.cache
def tables():
    out = {}
    ky = np.arange(MY) - MY // 2
    cy, sy = cos_sin(ky, np.arange(GY), GY)
    rows = np.concatenate([cy, -sy]) / math.sqrt(GY)
    out["yf"] = np.concatenate(split(rows)).reshape(256, 8, 128).transpose(1, 0, 2)
    high, low = (half.reshape(128, 8, 128).transpose(1, 0, 2) for half in split(rows))
    out["yi"] = np.concatenate([high, low], axis=2)
    cf, sf = (
        np.einsum("kz,cd->czkd", w / math.sqrt(NZ), np.eye(8)).reshape(128, 2, 32)
        for w in cos_sin(np.arange(MZ), np.arange(NZ), NZ)
    )
    zf = np.zeros((2, 128, 2, 2, 32))
    zf[0, :, :, 0], zf[1, :, :, 0], zf[1, :, :, 1], zf[0, :, :, 1] = cf, sf, cf, -sf
    out["zf"] = np.concatenate(split(zf.reshape(256, 128)), axis=1)
    ci, si = (
        np.einsum("kz,op->zokp", w / math.sqrt(NZ), np.eye(16)).reshape(128, 2, 64)
        for w in cos_sin(np.arange(MZ), np.arange(ZL), NZ)
    )
    zi = np.zeros((2, 128, 2, 2, 64))
    zi[0, :, :, 0], zi[0, :, :, 1], zi[1, :, :, 0], zi[1, :, :, 1] = ci, -si, si, ci
    out["zi"] = np.concatenate(split(zi.reshape(256, 256)))
    kx = np.arange(MX) - MX // 2
    cx, sx = cos_sin(kx, np.arange(GX), GX)
    cr = (cx / 8.0).astype(np.float32).astype(jnp.bfloat16).astype(np.float64)
    sr = (-sx / 8.0).astype(np.float32).astype(jnp.bfloat16).astype(np.float64)
    cr, sr = cr.reshape(8, 4, 8, 2, 4), sr.reshape(8, 4, 8, 2, 4)
    xf = np.zeros((4, 2, 8, 4, 4, 8, 2, 4, 2))
    for k in range(4):
        for a in range(2):
            sign = -1.0 if k * a % 2 else 1.0
            real, imag = sign * cr[:, :, :, a], sign * sr[:, :, :, a]
            xf[k, 0, :, k, :, :, a, :, 0], xf[k, 0, :, k, :, :, a, :, 1] = real, -imag
            xf[k, 1, :, k, :, :, a, :, 0], xf[k, 1, :, k, :, :, a, :, 1] = imag, real
    xf = xf.reshape(4, 256, 128).transpose(1, 0, 2).reshape(256, 512)
    out["xf"] = xf.astype(np.float32).astype(jnp.bfloat16)
    ic, is_ = (cx / 8.0).T.reshape(GX, 8, 1, 4), (sx / 8.0).T.reshape(GX, 8, 1, 4)
    xi = np.zeros((2, GX, 2, 8, 4, 4))
    xi[0, :, 0], xi[0, :, 1] = ic, -is_
    xi[1, :, 0], xi[1, :, 1] = is_, ic
    out["xi"] = np.concatenate(split(xi.reshape(128, 256)))
    return out


def iotas(shape):
    return lax.broadcasted_iota(jnp.int32, shape, 0), lax.broadcasted_iota(jnp.int32, shape, 1)


def halves(value):
    high = value.astype(BF16)
    return high, (value - high.astype(F32)).astype(BF16)


def dot(a, b, contract=((1,), (0,))):
    return lax.dot_general(a, b, (contract, ((), ())), preferred_element_type=F32)


def gelu(v):
    return 0.5 * v * (1.0 + jnp.tanh(ROOT * (v + 0.044715 * (v * v * v))))


def call(kernel, outs, in_specs, scratch=(), mib=16, flops=10**7, size=2**20):
    return pl.pallas_call(
        kernel,
        out_shape=[jax.ShapeDtypeStruct(s, d) for s, d in outs],
        in_specs=in_specs,
        out_specs=[VMEM] * len(outs),
        scratch_shapes=list(scratch),
        compiler_params=pltpu.CompilerParams(vmem_limit_bytes=mib << 20),
        cost_estimate=pl.CostEstimate(flops=flops, bytes_accessed=size, transcendentals=0),
    )


def rows_of(refs, field, slot, half):
    f, s, fp, sp = refs
    own, other = (s, sp) if field == 5 else (f.at[field], fp.at[field])
    start = 16 * (slot % 8) + 8 * half
    return (own if slot < 8 else other)[pl.ds(pl.multiple_of(start, 8), 8), :]


def edge_rows(f, s, out, rows):
    bottom = lax.axis_index("ga") == 0
    for field in range(6):
        for h in range(2):
            lanes = slice(128 * h, 128 * h + 128)
            rows[field, h] = s[:, lanes] if field == 5 else f[field, :, lanes]
            for d in range(3):
                first = rows[field, h, pl.ds(d, 8, stride=XL), :]
                last = rows[field, h, pl.ds(XL - 1 - d, 8, stride=XL), :]
                out[field, h, 8 * d : 8 * d + 8, :] = jnp.where(bottom, first, last)


def pack_own(f, s, own, rows):
    edge_rows(f, s, own, rows)


def pack_other(fp, sp, own, message, other, rows):
    edge_rows(fp, sp, other, rows)
    message[:, :, 0:24, :] = own[...]
    message[:, :, 24:48, :] = other[...]


def pack_y(f, s, fp, sp, message, far, near, outer):
    refs = (f, s, fp, sp)
    a = lax.axis_index("ga")
    row = lax.broadcasted_iota(jnp.int32, (8, 128), 0)
    beyond = jnp.where(a == 1, row, 7 - row) < 3
    lane = lax.broadcasted_iota(jnp.int32, (16, 128), 1) // 4
    lows, highs = jnp.zeros((16, 128), F32), jnp.zeros((16, 128), F32)
    for field in range(6):
        for h in range(2):
            for which in range(2):
                for d in range(3):
                    at = 24 * which + 8 * d
                    value = message[field, h, at : at + 8, :]
                    to = 64 * (1 - which)
                    outer[field, h, pl.ds(to + d, 8, stride=8), :] = value
                    outer[field, h, pl.ds(to + 7 - d, 8, stride=8), :] = value
        for slot in range(16):
            inner, block = rows_of(refs, field, slot, a), rows_of(refs, field, slot, 1 - a)
            edge = slice(8 * slot, 8 * slot + 8)
            for h in range(2):
                kept = block[:, 128 * h : 128 * h + 128]
                outer[field, h, edge, :] = jnp.where(beyond, outer[field, h, edge, :], kept)
            base = 64 * (field % 2) + 4 * slot
            here = lane == base // 4
            first = jnp.concatenate([inner[:, :128], outer[field, 0, edge, :]], axis=0)
            last = jnp.concatenate([inner[:, 128:], outer[field, 1, edge, :]], axis=0)
            lows = jnp.where(here, pltpu.roll(first, base, 1) if base else first, lows)
            highs = jnp.where(here, pltpu.roll(last, (base + 4) % 128, 1) if base != 124 else last, highs)
        if field % 2:
            even = lax.axis_index("gy") % 2 == 0
            far[field // 2] = jnp.where(even, lows, highs)
            near[field // 2] = jnp.where(even, highs, lows)


def stencil(f, s, fp, sp, got, far, near, last, a, b, stiff, outer):
    refs = (f, s, fp, sp)
    core = lax.axis_index("ga")
    even = lax.axis_index("gy") % 2 == 0
    first_lanes = lax.broadcasted_iota(jnp.int32, (16, 128), 1) < 64
    row = lax.broadcasted_iota(jnp.int32, (8, 128), 0)
    beyond = jnp.where(core == 1, row, 7 - row) < 3
    for field in range(6):
        for h in range(2):
            for which in range(2):
                for d in range(3):
                    at = 24 * which + 8 * d
                    value = got[field, h, at : at + 8, :]
                    to = 64 * (1 - which)
                    outer[h, pl.ds(to + d, 8, stride=8), :] = value
                    outer[h, pl.ds(to + 7 - d, 8, stride=8), :] = value
        one, two = near[field // 2], far[field // 2]
        above, below = jnp.where(even, one, two), jnp.where(even, two, one)
        for slot in range(16):
            to = stiff.at[slot] if field == 5 else a.at[field, slot]
            to[0:8, 0:256] = rows_of(refs, field, slot, core)
            block = rows_of(refs, field, slot, 1 - core)
            for h in range(2):
                lanes = slice(128 * h, 128 * h + 128)
                edge = outer[h, 8 * slot : 8 * slot + 8, :]
                to[8:16, lanes] = jnp.where(beyond, edge, block[:, lanes])
            base = 64 * (field % 2) + 4 * slot
            up = pltpu.roll(above, 128 - base, 1) if base else above
            down = pltpu.roll(below, 124 - base, 1) if base != 124 else below
            to[:, 256:384] = jnp.where(first_lanes, up, down)

    def terms(src, field, slot, crop):
        mid = src[field, slot]
        up, down = src[field, (slot + 1) & 15], src[field, (slot + 15) & 15]
        xp, xm = pltpu.roll(mid, 15, 0), pltpu.roll(mid, 1, 0)
        yp, ym = pltpu.roll(mid, 383, 1), pltpu.roll(mid, 1, 1)
        if crop:
            mid, up, down, xp, xm, yp, ym = (v[0:8, 0:256] for v in (mid, up, down, xp, xm, yp, ym))
        total = 0.1 * mid + 0.12 * xp + 0.18 * xm + 0.17 * yp + 0.13 * ym
        return total + 0.14 * up + 0.16 * down, xp - xm, yp - ym, up - down

    def advance(src, slot, crop, store):
        vx, east, _, _ = terms(src, 1, slot, crop)
        vy, _, north, _ = terms(src, 2, slot, crop)
        vz, _, _, depth = terms(src, 3, slot, crop)
        div = 0.1 * (east + north + depth)
        store(0, terms(src, 0, slot, crop)[0] - div)
        pressure, east, north, depth = terms(src, 4, slot, crop)
        store(1, vx - 0.1 * east)
        store(2, vy - 0.1 * north)
        store(3, vz - 0.1 * depth)
        store(4, pressure - (stiff[slot, 0:8, 0:256] if crop else stiff[slot]) * div)

    for src, dst in ((a, b), (b, a), (a, None)):

        def body(slot, carry, src=src, dst=dst):
            def store(field, new):
                if dst is None:
                    rows = pl.ds(pl.multiple_of(slot * 8, 8), 8)
                    for h in range(2):
                        last[field, h, rows, :] = new[:, 128 * h : 128 * h + 128]
                else:
                    dst[field, slot] = new

            advance(src, slot, dst is None, store)
            return carry

        lax.fori_loop(0, 16, body, 0, unroll=True)


def lift_rows(values, weight, bias):
    rows = []
    for c in range(C):
        v = bias[c] + values[0] * weight[0, c]
        for field in range(1, 5):
            v = v + values[field] * weight[field, c]
        rows.append(gelu(v))
    return jnp.concatenate(rows, axis=0).astype(BF16)


def pointwise(keep, got, weight, bias, mix, obias, out, wide):
    a = lax.axis_index("ga")
    wide[pl.ds(pl.multiple_of(160 * a, 8), 160), :] = keep[...]
    wide[pl.ds(pl.multiple_of(160 * (1 - a), 8), 160), :] = got[...]
    row, lane = iotas((256, 32))
    pick = (row // 8 == lane).astype(BF16)
    bias_o = jnp.sum(jnp.where(row // 8 == lane, obias[...], 0.0), axis=1, keepdims=True)
    by_row = dot(pick, mix[...], ((1,), (1,))).astype(BF16)
    row, lane = iotas((256, 256))
    spread = jnp.where(row % 8 == lane % 8, dot(by_row, pick, ((1,), (1,))), 0.0).astype(BF16)

    def body(z, carry):
        values = [wide[pl.ds(8 * field + z, 8, stride=40), :] for field in range(5)]
        out[z] = dot(spread, lift_rows(values, weight, bias)) + bias_o
        return carry

    lax.fori_loop(0, ZL, body, 0)


def forward(
    last, after, weight, bias, yf_far, zf_far, keep, send, out, sums, lifted, modes, yf, zf, sems
):
    copies = [
        pltpu.make_async_copy(yf_far.at[lax.axis_index("gy")], yf, sems.at[0]),
        pltpu.make_async_copy(zf_far, zf, sems.at[1]),
    ]
    for copy in copies:
        copy.start()
    for half in range(2):
        for x in range(4):
            for field in range(5):
                at = 160 * half + 40 * x + 8 * field
                for h in range(2):
                    even = last[field, h, pl.ds(64 * half + 2 * x, 8, stride=8), :]
                    odd = last[field, h, pl.ds(64 * half + 2 * x + 1, 8, stride=8), :]
                    sums[at : at + 8, 128 * h : 128 * h + 128] = even + odd
    value = sums[...]
    high = value.astype(BF16)
    rest = value - high.astype(F32)
    mid, low = halves(rest)
    row, lane = iotas((256, 128))
    table = jnp.where(row // 2 == lane, 0.25, 0.0).astype(BF16)
    mean = dot(high, table) + dot(mid, table) + dot(low, table)
    keep[...] = mean[:160]
    send[...] = mean[160:]
    for x in range(4):
        at = [40 * x + 8 * field for field in range(5)]
        values = [jnp.concatenate([mean[r : r + 8], mean[r + 160 : r + 168]], axis=0) for r in at]
        lifted[x] = lift_rows(values, weight, bias)
    copies[0].wait()
    for x in range(4):
        both = dot(yf[...], lifted[x], ((1,), (1,)))
        modes[x] = both[:128] + both[128:]
    copies[1].wait()
    parts = []
    for group in range(4):
        lanes = slice(128 * group, 128 * group + 128)
        stack = [
            jnp.concatenate([modes[x, 0:64, lanes], modes[x, 64:128, lanes]], axis=1)
            for x in range(4)
        ]
        m_high, m_low = halves(jnp.concatenate(stack, axis=0))
        both = dot(m_high, zf[...])
        parts.append(both[:, :128] + both[:, 128:] + dot(m_low, zf[:, :128]))
    lane = lax.broadcasted_iota(jnp.int32, (256, 128), 1) // 32
    for part in range(4):
        total = parts[part]
        for group in range(4):
            if group != part:
                moved = pltpu.roll(parts[group], (32 * (group - part)) % 128, 1)
                total = jnp.where(lane == group, moved, total)
        for x in range(4):
            rows = pl.ds(8 * (part // 2) + 2 * x + part % 2, 64, stride=16)
            out[rows, :] = total[64 * x : 64 * x + 64]


def mix_modes(got, weights, xf, xi, after, out):
    total = got[:, 0]
    for j in range(1, 8):
        total = total + got[:, j]
    both = jnp.concatenate(halves(total.reshape(128, 128)), axis=0)
    row, lane = iotas((128, 512))
    spread = (row // 8 % 4 == lane // 128) & (row // 32 * 8 + row % 8 == lane % 128 // 4)
    wide = dot(both, spread.astype(BF16)).astype(BF16)
    pieces = [
        jnp.concatenate([wide[:128, 128 * k : 128 * k + 128], wide[128:, 128 * k : 128 * k + 128]], axis=1)
        for k in range(4)
    ]
    modes = dot(xf[...], jnp.concatenate(pieces, axis=0))
    modes = modes[:, :128] + modes[:, 128:]
    real, imag = modes[:128], modes[128:]
    highs, lows = [], []
    for i in range(8):
        wr = weights[8 * i : 8 * i + 8, 0:16, :].astype(F32).reshape(128, 128)
        wi = weights[8 * i : 8 * i + 8, 16:32, :].astype(F32).reshape(128, 128)
        high, low = halves(
            jnp.concatenate([wr * real - wi * imag, wr * imag + wi * real], axis=0)
        )
        highs.append(high)
        lows.append(low)
    row, lane = iotas((1024, 128))
    gather = (lane // 64 * 16 + lane % 16 == 4 * (row // 128) + row % 4).astype(BF16)
    parts = [jnp.concatenate(part, axis=1) for part in (highs, lows)]
    total = dot(jnp.concatenate(parts, axis=0), gather)
    total = total[:256] + total[256:]
    row, lane = iotas((256, 128))
    total = jnp.where((row // 4) % 4 == (lane // 16) % 4, total, 0.0)
    back = dot(xi[...], jnp.concatenate(halves(total), axis=1))
    back = back[:128, :128] + back[:128, 128:] + back[128:, :128]
    real, imag = back[:64], back[64:]
    lane = lax.broadcasted_iota(jnp.int32, (64, 128), 1)
    parts = [
        jnp.where(lane < 64, real, pltpu.roll(imag, 64, 1)),
        jnp.where(lane < 64, pltpu.roll(real, 64, 1), imag),
    ]
    odd = (lane // 16) % 2 == 1
    for a in range(2):
        signed = [jnp.where(odd, -part, part) for part in parts] if a else parts
        for i in range(8):
            rows = slice(8 * i, 8 * i + 8)
            tile = jnp.concatenate([part[rows] for part in signed], axis=0).astype(BF16)
            for j in range(8):
                out[i, j, a] = tile


def finish(got, direct, yi_far, zi_far, out, rows, spectral, yi, zi, sems):
    copies = [
        pltpu.make_async_copy(yi_far.at[lax.axis_index("gy")], yi, sems.at[0]),
        pltpu.make_async_copy(zi_far, zi, sems.at[1]),
    ]
    for copy in copies:
        copy.start()
    rows[...] = got[...].astype(F32)
    for copy in copies:
        copy.wait()
    by_z = []
    for part in range(2):
        stack = []
        for x in range(8):
            pair = [rows[pl.ds(16 * a + 8 * part + x, 64, stride=32), :] for a in range(2)]
            stack.append(jnp.concatenate(pair, axis=1).astype(BF16))
        both = dot(zi[...], jnp.concatenate(stack, axis=0), ((1,), (1,)))
        by_z.append(both[:256] + both[256:])
    blank = jnp.zeros((64, 128), BF16)

    def twice(lanes):
        real, imag = yi[0:64, lanes], yi[64:128, lanes]
        pieces = [[real, blank], [blank, real], [imag, blank], [blank, imag]]
        return jnp.concatenate([jnp.concatenate(row, axis=1) for row in pieces], axis=0)

    t_high, t_low = twice(slice(0, 128)), twice(slice(128, 256))
    for pair in range(4):
        lanes = slice(128 * pair, 128 * pair + 128)
        value = jnp.concatenate(
            [jnp.concatenate([v[:128, lanes], v[128:, lanes]], axis=1) for v in by_z], axis=0
        )
        high, low = halves(value)
        both = dot(high, t_high) + dot(low, t_high) + dot(high, t_low)
        for x in range(2):
            spectral[pl.ds(2 * pair + x, 256, stride=8), :] = both[:, 128 * x : 128 * x + 128]
    for part in range(2):
        for z in range(ZL):
            at = 128 * (8 * part + z)
            branch = spectral[at : at + 128, :].astype(BF16).astype(F32)
            total = gelu(direct[z, 128 * part : 128 * part + 128, :] + branch)
            out[z, 16 * part : 16 * part + 16] = total.reshape(16, 8, 128).astype(BF16)


def turn_weights(weights, after, out, wide):
    for chunk in range(16):
        turned = weights[128 * chunk : 128 * chunk + 128, :].T
        for ri in range(2):
            wide[:, 16 * ri + chunk, :] = turned[64 * ri : 64 * ri + 64]
    out[...] = wide[...].astype(BF16)


def shards(fields, stiffness, lift_weight, lift_bias, mix_weight, spectral_weight, output_bias):
    table = {name: jnp.asarray(value) for name, value in tables().items()}
    everyone = ("gx", "gy", "ga")

    def exchange(value, axis):
        return lax.all_to_all(value, axis, split_axis=0, concat_axis=0, tiled=True)

    anywhere = pl.BlockSpec(memory_space=pl.ANY)
    f = fields.reshape(5, 128, 256)
    s = stiffness.reshape(128, 256)
    swap = [(0, 1), (1, 0)]
    fp, sp = lax.ppermute(f, "ga", swap), lax.ppermute(s, "ga", swap)
    rows = pltpu.VMEM((6, 2, 128, 128), F32)
    edges = ((6, 2, 24, 128), F32)
    [own] = call(pack_own, [edges], [VMEM] * 2, [rows])(f, s)
    [message] = call(
        pack_other, [((6, 2, 48, 128), F32)], [VMEM] * 3, [pltpu.VMEM(*edges), rows]
    )(fp, sp, own)
    across = [(2 * i, 2 * ((i - 1) % 8) + 1) for i in range(8)]
    across += [(2 * i + 1, 2 * ((i + 1) % 8)) for i in range(8)]
    got = lax.ppermute(message, ("gx", "ga"), across)

    [turned] = call(
        turn_weights,
        [((64, 32, 128), BF16)],
        [VMEM, anywhere],
        [pltpu.VMEM((64, 32, 128), F32)],
        size=2 * 10**7,
    )(spectral_weight.reshape(2048, 128), message)
    weights = exchange(turned, ("gx", "gy"))

    message = ((3, 16, 128), F32)
    far, near = call(
        pack_y,
        [message, message],
        [VMEM] * 5,
        [pltpu.VMEM((6, 2, 128, 128), F32)],
        flops=10**12,
    )(f, s, fp, sp, got)
    far = lax.ppermute(far, "gy", [(j, (j - 1 + 2 * (j % 2)) % 8) for j in range(8)])
    near = lax.ppermute(near, "gy", [(j, j + 1 - 2 * (j % 2)) for j in range(8)])
    [last] = call(
        stencil,
        [((5, 2, 128, 128), F32)],
        [VMEM] * 7,
        [
            pltpu.VMEM((5, 16, 16, 384), F32),
            pltpu.VMEM((5, 16, 16, 384), F32),
            pltpu.VMEM((16, 16, 384), F32),
            pltpu.VMEM((2, 128, 128), F32),
        ],
    )(f, s, fp, sp, got, far, near)
    keep, send, modes = call(
        forward,
        [((160, 128), F32), ((160, 128), F32), ((1024, 128), F32)],
        [VMEM, anywhere, SMEM, SMEM, anywhere, anywhere],
        [
            pltpu.VMEM((320, 256), F32),
            pltpu.VMEM((4, 512, 128), BF16),
            pltpu.VMEM((4, 128, 512), F32),
            pltpu.VMEM((256, 128), BF16),
            pltpu.VMEM((256, 256), BF16),
            pltpu.SemaphoreType.DMA((2,)),
        ],
    )(last, weights, lift_weight, lift_bias, table["yf"], table["zf"])
    modes = exchange(modes.reshape(128, 8, 128), everyone)
    [direct] = call(
        pointwise,
        [((8, 256, 128), F32)],
        [VMEM, VMEM, SMEM, SMEM, VMEM, VMEM],
        [pltpu.VMEM((320, 128), F32)],
        flops=3 * 10**8,
    )(keep, lax.ppermute(send, "ga", swap), lift_weight, lift_bias, mix_weight, output_bias.reshape(1, C))

    [mixed] = call(mix_modes, [((8, 8, 2, 16, 128), BF16)], [VMEM] * 4 + [anywhere])(
        modes.reshape(8, 8, 16, 128), weights, table["xf"], table["xi"], direct
    )
    mixed = exchange(mixed.reshape(128, 16, 128), everyone)
    [out] = call(
        finish,
        [((8, 32, 8, 128), BF16)],
        [VMEM, VMEM, anywhere, anywhere],
        [
            pltpu.VMEM((2048, 128), F32),
            pltpu.VMEM((2048, 128), F32),
            pltpu.VMEM((128, 256), BF16),
            pltpu.VMEM((512, 256), BF16),
            pltpu.SemaphoreType.DMA((2,)),
        ],
    )(mixed.reshape(2048, 128), direct, table["yi"], table["zi"])
    return out


def solution(mesh):
    placed = (
        P(None, "ga", "gx", "gy"),
        P("ga", "gx", "gy"),
        P(),
        P(),
        P(),
        P("ga", "gy", None, "gx", None),
        P(),
    )
    return jax.shard_map(
        shards, mesh=mesh, in_specs=placed, out_specs=P("ga", None, "gx", "gy"), check_vma=False
    )
```

```python
import functools
import math

import jax
import jax.numpy as jnp
import numpy as np
from jax import lax
from jax.experimental import pallas as pl
from jax.experimental.pallas import tpu as pltpu
from jax.sharding import PartitionSpec as P

NZ, C, MX, MY, MZ, GX, GY = 16, 32, 32, 64, 8, 64, 1024
ZL, XL, YL = 8, 16, 256
F32, BF16 = jnp.float32, jnp.bfloat16
ROOT = math.sqrt(2.0 / math.pi)
VMEM = pl.BlockSpec(memory_space=pltpu.VMEM)
SMEM = pl.BlockSpec(memory_space=pltpu.SMEM)


def cos_sin(freq, points, length):
    turn = np.mod(np.outer(freq, points), length) * (2.0 * np.pi / length)
    return np.cos(turn), np.sin(turn)


def split(table):
    table = np.asarray(table, np.float32)
    high = table.astype(jnp.bfloat16)
    low = (table - high.astype(np.float32)).astype(jnp.bfloat16)
    return high, low


@functools.cache
def tables():
    out = {}
    ky = np.arange(MY) - MY // 2
    cy, sy = cos_sin(ky, np.arange(GY), GY)
    rows = np.concatenate([cy, -sy]) / math.sqrt(GY)
    out["yf"] = split(rows)[0].reshape(128, 8, 128).transpose(1, 0, 2)
    out["yi"] = out["yf"]
    cf, sf = (
        np.einsum("kz,cd->czkd", w / math.sqrt(NZ), np.eye(8)).reshape(128, 2, 32)
        for w in cos_sin(np.arange(MZ), np.arange(NZ), NZ)
    )
    zf = np.zeros((2, 128, 2, 2, 32))
    zf[0, :, :, 0], zf[1, :, :, 0], zf[1, :, :, 1], zf[0, :, :, 1] = cf, sf, cf, -sf
    out["zf"] = np.concatenate(split(zf.reshape(256, 128)), axis=1)
    ci, si = (
        np.einsum("kz,op->zokp", w / math.sqrt(NZ), np.eye(16)).reshape(128, 2, 64)
        for w in cos_sin(np.arange(MZ), np.arange(ZL), NZ)
    )
    zi = np.zeros((2, 128, 2, 2, 64))
    zi[0, :, :, 0], zi[0, :, :, 1], zi[1, :, :, 0], zi[1, :, :, 1] = ci, -si, si, ci
    out["zi"] = split(zi.reshape(256, 256))[0]
    kx = np.arange(MX) - MX // 2
    cx, sx = cos_sin(kx, np.arange(GX), GX)
    cr = (cx / 8.0).astype(np.float32).astype(jnp.bfloat16).astype(np.float64)
    sr = (-sx / 8.0).astype(np.float32).astype(jnp.bfloat16).astype(np.float64)
    cr, sr = cr.reshape(8, 4, 8, 2, 4), sr.reshape(8, 4, 8, 2, 4)
    xf = np.zeros((4, 2, 8, 4, 4, 8, 2, 4, 2))
    for k in range(4):
        for a in range(2):
            sign = -1.0 if k * a % 2 else 1.0
            real, imag = sign * cr[:, :, :, a], sign * sr[:, :, :, a]
            xf[k, 0, :, k, :, :, a, :, 0], xf[k, 0, :, k, :, :, a, :, 1] = real, -imag
            xf[k, 1, :, k, :, :, a, :, 0], xf[k, 1, :, k, :, :, a, :, 1] = imag, real
    xf = xf.reshape(4, 256, 128).transpose(1, 0, 2).reshape(256, 512)
    out["xf"] = xf.astype(np.float32).astype(jnp.bfloat16)
    ic, is_ = (cx / 8.0).T.reshape(GX, 8, 1, 4), (sx / 8.0).T.reshape(GX, 8, 1, 4)
    xi = np.zeros((2, GX, 2, 8, 4, 4))
    xi[0, :, 0], xi[0, :, 1] = ic, -is_
    xi[1, :, 0], xi[1, :, 1] = is_, ic
    out["xi"] = np.concatenate(split(xi.reshape(128, 256)))
    return out


def iotas(shape):
    return lax.broadcasted_iota(jnp.int32, shape, 0), lax.broadcasted_iota(jnp.int32, shape, 1)


def halves(value):
    high = value.astype(BF16)
    return high, (value - high.astype(F32)).astype(BF16)


def dot(a, b, contract=((1,), (0,))):
    return lax.dot_general(a, b, (contract, ((), ())), preferred_element_type=F32)


def gelu(v):
    return 0.5 * v * (1.0 + jnp.tanh(ROOT * (v + 0.044715 * (v * v * v))))


def call(kernel, outs, in_specs, scratch=(), mib=16, flops=10**7, size=2**20):
    return pl.pallas_call(
        kernel,
        out_shape=[jax.ShapeDtypeStruct(s, d) for s, d in outs],
        in_specs=in_specs,
        out_specs=[VMEM] * len(outs),
        scratch_shapes=list(scratch),
        compiler_params=pltpu.CompilerParams(vmem_limit_bytes=mib << 20),
        cost_estimate=pl.CostEstimate(flops=flops, bytes_accessed=size, transcendentals=0),
    )


def rows_of(refs, field, slot, half):
    f, s, fp, sp = refs
    own, other = (s, sp) if field == 5 else (f.at[field], fp.at[field])
    start = 16 * (slot % 8) + 8 * half
    return (own if slot < 8 else other)[pl.ds(pl.multiple_of(start, 8), 8), :]


def edge_rows(f, s, out, rows):
    bottom = lax.axis_index("ga") == 0
    for field in range(6):
        for h in range(2):
            lanes = slice(128 * h, 128 * h + 128)
            rows[field, h] = s[:, lanes] if field == 5 else f[field, :, lanes]
            for d in range(3):
                first = rows[field, h, pl.ds(d, 8, stride=XL), :]
                last = rows[field, h, pl.ds(XL - 1 - d, 8, stride=XL), :]
                out[field, h, 8 * d : 8 * d + 8, :] = jnp.where(bottom, first, last)


def pack_own(f, s, after, own, rows):
    edge_rows(f, s, own, rows)


def pack_other(fp, sp, own, message, other, rows):
    edge_rows(fp, sp, other, rows)
    message[:, :, 0:24, :] = own[...]
    message[:, :, 24:48, :] = other[...]


def pack_y(f, s, fp, sp, message, far, near, outer):
    refs = (f, s, fp, sp)
    a = lax.axis_index("ga")
    row = lax.broadcasted_iota(jnp.int32, (8, 128), 0)
    beyond = jnp.where(a == 1, row, 7 - row) < 3
    lane = lax.broadcasted_iota(jnp.int32, (16, 128), 1) // 4
    lows, highs = jnp.zeros((16, 128), F32), jnp.zeros((16, 128), F32)
    for field in range(6):
        for h in range(2):
            for which in range(2):
                for d in range(3):
                    at = 24 * which + 8 * d
                    value = message[field, h, at : at + 8, :]
                    to = 64 * (1 - which)
                    outer[field, h, pl.ds(to + d, 8, stride=8), :] = value
                    outer[field, h, pl.ds(to + 7 - d, 8, stride=8), :] = value
        for slot in range(16):
            inner, block = rows_of(refs, field, slot, a), rows_of(refs, field, slot, 1 - a)
            edge = slice(8 * slot, 8 * slot + 8)
            for h in range(2):
                kept = block[:, 128 * h : 128 * h + 128]
                outer[field, h, edge, :] = jnp.where(beyond, outer[field, h, edge, :], kept)
            base = 64 * (field % 2) + 4 * slot
            here = lane == base // 4
            first = jnp.concatenate([inner[:, :128], outer[field, 0, edge, :]], axis=0)
            last = jnp.concatenate([inner[:, 128:], outer[field, 1, edge, :]], axis=0)
            lows = jnp.where(here, pltpu.roll(first, base, 1) if base else first, lows)
            highs = jnp.where(here, pltpu.roll(last, (base + 4) % 128, 1) if base != 124 else last, highs)
        if field % 2:
            even = lax.axis_index("gy") % 2 == 0
            far[field // 2] = jnp.where(even, lows, highs)
            near[field // 2] = jnp.where(even, highs, lows)


def stencil(f, s, fp, sp, got, far, near, last, a, b, stiff, outer):
    refs = (f, s, fp, sp)
    core = lax.axis_index("ga")
    even = lax.axis_index("gy") % 2 == 0
    first_lanes = lax.broadcasted_iota(jnp.int32, (16, 128), 1) < 64
    row = lax.broadcasted_iota(jnp.int32, (8, 128), 0)
    beyond = jnp.where(core == 1, row, 7 - row) < 3
    for field in range(6):
        for h in range(2):
            for which in range(2):
                for d in range(3):
                    at = 24 * which + 8 * d
                    value = got[field, h, at : at + 8, :]
                    to = 64 * (1 - which)
                    outer[h, pl.ds(to + d, 8, stride=8), :] = value
                    outer[h, pl.ds(to + 7 - d, 8, stride=8), :] = value
        one, two = near[field // 2], far[field // 2]
        above, below = jnp.where(even, one, two), jnp.where(even, two, one)
        for slot in range(16):
            to = stiff.at[slot] if field == 5 else a.at[field, slot]
            to[0:8, 0:256] = rows_of(refs, field, slot, core)
            block = rows_of(refs, field, slot, 1 - core)
            for h in range(2):
                lanes = slice(128 * h, 128 * h + 128)
                edge = outer[h, 8 * slot : 8 * slot + 8, :]
                to[8:16, lanes] = jnp.where(beyond, edge, block[:, lanes])
            base = 64 * (field % 2) + 4 * slot
            up = pltpu.roll(above, 128 - base, 1) if base else above
            down = pltpu.roll(below, 124 - base, 1) if base != 124 else below
            to[:, 256:384] = jnp.where(first_lanes, up, down)

    def terms(src, field, slot, crop):
        mid = src[field, slot]
        up, down = src[field, (slot + 1) & 15], src[field, (slot + 15) & 15]
        xp, xm = pltpu.roll(mid, 15, 0), pltpu.roll(mid, 1, 0)
        yp, ym = pltpu.roll(mid, 383, 1), pltpu.roll(mid, 1, 1)
        if crop:
            mid, up, down, xp, xm, yp, ym = (v[0:8, 0:256] for v in (mid, up, down, xp, xm, yp, ym))
        total = 0.1 * mid + 0.12 * xp + 0.18 * xm + 0.17 * yp + 0.13 * ym
        return total + 0.14 * up + 0.16 * down, xp - xm, yp - ym, up - down

    def advance(src, slot, crop, store):
        vx, east, _, _ = terms(src, 1, slot, crop)
        vy, _, north, _ = terms(src, 2, slot, crop)
        vz, _, _, depth = terms(src, 3, slot, crop)
        div = 0.1 * (east + north + depth)
        store(0, terms(src, 0, slot, crop)[0] - div)
        pressure, east, north, depth = terms(src, 4, slot, crop)
        store(1, vx - 0.1 * east)
        store(2, vy - 0.1 * north)
        store(3, vz - 0.1 * depth)
        store(4, pressure - (stiff[slot, 0:8, 0:256] if crop else stiff[slot]) * div)

    for src, dst in ((a, b), (b, a), (a, None)):

        def body(slot, carry, src=src, dst=dst):
            def store(field, new):
                if dst is None:
                    rows = pl.ds(pl.multiple_of(slot * 8, 8), 8)
                    for h in range(2):
                        last[field, h, rows, :] = new[:, 128 * h : 128 * h + 128]
                else:
                    dst[field, slot] = new

            advance(src, slot, dst is None, store)
            return carry

        lax.fori_loop(0, 16, body, 0, unroll=True)


def lift_rows(values, weight, bias):
    rows = []
    for c in range(C):
        v = bias[c] + values[0] * weight[0, c]
        for field in range(1, 5):
            v = v + values[field] * weight[field, c]
        rows.append(gelu(v))
    return jnp.concatenate(rows, axis=0).astype(BF16)


def pointwise(keep, got, weight, bias, mix, obias, out, wide):
    a = lax.axis_index("ga")
    wide[pl.ds(pl.multiple_of(160 * a, 8), 160), :] = keep[...]
    wide[pl.ds(pl.multiple_of(160 * (1 - a), 8), 160), :] = got[...]
    row, lane = iotas((256, 32))
    pick = (row // 8 == lane).astype(BF16)
    bias_o = jnp.sum(jnp.where(row // 8 == lane, obias[...], 0.0), axis=1, keepdims=True)
    by_row = dot(pick, mix[...], ((1,), (1,))).astype(BF16)
    row, lane = iotas((256, 256))
    spread = jnp.where(row % 8 == lane % 8, dot(by_row, pick, ((1,), (1,))), 0.0).astype(BF16)

    def body(z, carry):
        values = [wide[pl.ds(8 * field + z, 8, stride=40), :] for field in range(5)]
        out[z] = dot(spread, lift_rows(values, weight, bias)) + bias_o
        return carry

    lax.fori_loop(0, ZL, body, 0)


def forward(
    last, after, weight, bias, yf_far, zf_far, keep, send, out, sums, lifted, modes, yf, zf, sems
):
    copies = [
        pltpu.make_async_copy(yf_far.at[lax.axis_index("gy")], yf, sems.at[0]),
        pltpu.make_async_copy(zf_far, zf, sems.at[1]),
    ]
    for copy in copies:
        copy.start()
    for half in range(2):
        for x in range(4):
            for field in range(5):
                at = 160 * half + 40 * x + 8 * field
                for h in range(2):
                    even = last[field, h, pl.ds(64 * half + 2 * x, 8, stride=8), :]
                    odd = last[field, h, pl.ds(64 * half + 2 * x + 1, 8, stride=8), :]
                    sums[at : at + 8, 128 * h : 128 * h + 128] = even + odd
    value = sums[...]
    high = value.astype(BF16)
    low = (value - high.astype(F32)).astype(BF16)
    row, lane = iotas((256, 128))
    table = jnp.where(row // 2 == lane, 0.25, 0.0).astype(BF16)
    mean = dot(high, table) + dot(low, table)
    keep[...] = mean[:160]
    send[...] = mean[160:]
    for x in range(4):
        at = [40 * x + 8 * field for field in range(5)]
        values = [jnp.concatenate([mean[r : r + 8], mean[r + 160 : r + 168]], axis=0) for r in at]
        lifted[x] = lift_rows(values, weight, bias)
    copies[0].wait()
    for x in range(4):
        modes[x] = dot(yf[...], lifted[x], ((1,), (1,)))
    copies[1].wait()
    parts = []
    for group in range(4):
        lanes = slice(128 * group, 128 * group + 128)
        stack = [
            jnp.concatenate([modes[x, 0:64, lanes], modes[x, 64:128, lanes]], axis=1)
            for x in range(4)
        ]
        m_high, m_low = halves(jnp.concatenate(stack, axis=0))
        both = dot(m_high, zf[...])
        parts.append(both[:, :128] + both[:, 128:] + dot(m_low, zf[:, :128]))
    lane = lax.broadcasted_iota(jnp.int32, (256, 128), 1) // 32
    for part in range(4):
        total = parts[part]
        for group in range(4):
            if group != part:
                moved = pltpu.roll(parts[group], (32 * (group - part)) % 128, 1)
                total = jnp.where(lane == group, moved, total)
        for x in range(4):
            rows = pl.ds(8 * (part // 2) + 2 * x + part % 2, 64, stride=16)
            out[rows, :] = total[64 * x : 64 * x + 64]


def mix_modes(got, weights_far, xf, xi, after, out, weights, sem):
    copy = pltpu.make_async_copy(weights_far, weights, sem)
    copy.start()
    total = got[:, 0]
    for j in range(1, 8):
        total = total + got[:, j]
    both = jnp.concatenate(halves(total.reshape(128, 128)), axis=0)
    row, lane = iotas((128, 512))
    spread = (row // 8 % 4 == lane // 128) & (row // 32 * 8 + row % 8 == lane % 128 // 4)
    wide = dot(both, spread.astype(BF16)).astype(BF16)
    pieces = [
        jnp.concatenate([wide[:128, 128 * k : 128 * k + 128], wide[128:, 128 * k : 128 * k + 128]], axis=1)
        for k in range(4)
    ]
    modes = dot(xf[...], jnp.concatenate(pieces, axis=0))
    modes = modes[:, :128] + modes[:, 128:]
    real, imag = modes[:128], modes[128:]
    highs, lows = [], []
    copy.wait()
    for i in range(8):
        wr = weights[8 * i : 8 * i + 8, 0:16, :].astype(F32).reshape(128, 128)
        wi = weights[8 * i : 8 * i + 8, 16:32, :].astype(F32).reshape(128, 128)
        high, low = halves(
            jnp.concatenate([wr * real - wi * imag, wr * imag + wi * real], axis=0)
        )
        highs.append(high)
        lows.append(low)
    row, lane = iotas((1024, 128))
    gather = (lane // 64 * 16 + lane % 16 == 4 * (row // 128) + row % 4).astype(BF16)
    parts = [jnp.concatenate(part, axis=1) for part in (highs, lows)]
    total = dot(jnp.concatenate(parts, axis=0), gather)
    total = total[:256] + total[256:]
    row, lane = iotas((256, 128))
    total = jnp.where((row // 4) % 4 == (lane // 16) % 4, total, 0.0)
    back = dot(xi[...], jnp.concatenate(halves(total), axis=1))
    back = back[:128, :128] + back[:128, 128:] + back[128:, :128]
    real, imag = back[:64], back[64:]
    lane = lax.broadcasted_iota(jnp.int32, (64, 128), 1)
    parts = [
        jnp.where(lane < 64, real, pltpu.roll(imag, 64, 1)),
        jnp.where(lane < 64, pltpu.roll(real, 64, 1), imag),
    ]
    odd = (lane // 16) % 2 == 1
    for a in range(2):
        signed = [jnp.where(odd, -part, part) for part in parts] if a else parts
        for i in range(8):
            rows = slice(8 * i, 8 * i + 8)
            tile = jnp.concatenate([part[rows] for part in signed], axis=0).astype(BF16)
            for j in range(8):
                out[i, j, a] = tile


def finish(got, direct, yi_far, zi_far, out, rows, spectral, yi, zi, sems):
    copies = [
        pltpu.make_async_copy(yi_far.at[lax.axis_index("gy")], yi, sems.at[0]),
        pltpu.make_async_copy(zi_far, zi, sems.at[1]),
    ]
    for copy in copies:
        copy.start()
    rows[...] = got[...].astype(F32)
    for copy in copies:
        copy.wait()
    by_z = []
    for part in range(2):
        stack = []
        for x in range(8):
            pair = [rows[pl.ds(16 * a + 8 * part + x, 64, stride=32), :] for a in range(2)]
            stack.append(jnp.concatenate(pair, axis=1).astype(BF16))
        by_z.append(dot(zi[...], jnp.concatenate(stack, axis=0), ((1,), (1,))))
    blank = jnp.zeros((64, 128), BF16)

    real, imag = yi[0:64, :], yi[64:128, :]
    pieces = [[real, blank], [blank, real], [imag, blank], [blank, imag]]
    twice = jnp.concatenate([jnp.concatenate(row, axis=1) for row in pieces], axis=0)
    for pair in range(4):
        lanes = slice(128 * pair, 128 * pair + 128)
        value = jnp.concatenate(
            [jnp.concatenate([v[:128, lanes], v[128:, lanes]], axis=1) for v in by_z], axis=0
        )
        high, low = halves(value)
        both = dot(high, twice) + dot(low, twice)
        for x in range(2):
            spectral[pl.ds(2 * pair + x, 256, stride=8), :] = both[:, 128 * x : 128 * x + 128]
    for part in range(2):
        for z in range(ZL):
            at = 128 * (8 * part + z)
            branch = spectral[at : at + 128, :].astype(BF16).astype(F32)
            total = gelu(direct[z, 128 * part : 128 * part + 128, :] + branch)
            out[z, 16 * part : 16 * part + 16] = total.reshape(16, 8, 128).astype(BF16)


def turn_weights(weights, out, wide):
    for chunk in range(16):
        turned = weights[128 * chunk : 128 * chunk + 128, :].T
        for ri in range(2):
            wide[:, 16 * ri + chunk, :] = turned[64 * ri : 64 * ri + 64]
    out[...] = wide[...].astype(BF16)


def shards(fields, stiffness, lift_weight, lift_bias, mix_weight, spectral_weight, output_bias):
    table = {name: jnp.asarray(value) for name, value in tables().items()}
    everyone = ("gx", "gy", "ga")

    def exchange(value, axis):
        return lax.all_to_all(value, axis, split_axis=0, concat_axis=0, tiled=True)

    anywhere = pl.BlockSpec(memory_space=pl.ANY)
    f = fields.reshape(5, 128, 256)
    s = stiffness.reshape(128, 256)
    swap = [(0, 1), (1, 0)]
    fp, sp = lax.ppermute(f, "ga", swap), lax.ppermute(s, "ga", swap)
    rows = pltpu.VMEM((6, 2, 128, 128), F32)
    edges = ((6, 2, 24, 128), F32)
    [turned] = call(
        turn_weights, [((64, 32, 128), BF16)], [VMEM], [pltpu.VMEM((64, 32, 128), F32)]
    )(spectral_weight.reshape(2048, 128))
    [own] = call(pack_own, [edges], [VMEM] * 2 + [anywhere], [rows])(f, s, turned)
    [message] = call(
        pack_other, [((6, 2, 48, 128), F32)], [VMEM] * 3, [pltpu.VMEM(*edges), rows]
    )(fp, sp, own)
    across = [(2 * i, 2 * ((i - 1) % 8) + 1) for i in range(8)]
    across += [(2 * i + 1, 2 * ((i + 1) % 8)) for i in range(8)]
    got = lax.ppermute(message, ("gx", "ga"), across)

    weights = exchange(turned, ("gx", "gy"))

    message = ((3, 16, 128), F32)
    far, near = call(
        pack_y,
        [message, message],
        [VMEM] * 5,
        [pltpu.VMEM((6, 2, 128, 128), F32)],
        flops=10**12,
    )(f, s, fp, sp, got)
    far = lax.ppermute(far, "gy", [(j, (j - 1 + 2 * (j % 2)) % 8) for j in range(8)])
    near = lax.ppermute(near, "gy", [(j, j + 1 - 2 * (j % 2)) for j in range(8)])
    [last] = call(
        stencil,
        [((5, 2, 128, 128), F32)],
        [VMEM] * 7,
        [
            pltpu.VMEM((5, 16, 16, 384), F32),
            pltpu.VMEM((5, 16, 16, 384), F32),
            pltpu.VMEM((16, 16, 384), F32),
            pltpu.VMEM((2, 128, 128), F32),
        ],
    )(f, s, fp, sp, got, far, near)
    keep, send, modes = call(
        forward,
        [((160, 128), F32), ((160, 128), F32), ((1024, 128), F32)],
        [VMEM, anywhere, SMEM, SMEM, anywhere, anywhere],
        [
            pltpu.VMEM((320, 256), F32),
            pltpu.VMEM((4, 512, 128), BF16),
            pltpu.VMEM((4, 128, 512), F32),
            pltpu.VMEM((128, 128), BF16),
            pltpu.VMEM((256, 256), BF16),
            pltpu.SemaphoreType.DMA((2,)),
        ],
    )(last, weights, lift_weight, lift_bias, table["yf"], table["zf"])
    modes = exchange(modes.reshape(128, 8, 128), everyone)
    [direct] = call(
        pointwise,
        [((8, 256, 128), F32)],
        [VMEM, VMEM, SMEM, SMEM, VMEM, VMEM],
        [pltpu.VMEM((320, 128), F32)],
        flops=3 * 10**8,
    )(keep, lax.ppermute(send, "ga", swap), lift_weight, lift_bias, mix_weight, output_bias.reshape(1, C))

    [mixed] = call(
        mix_modes,
        [((8, 8, 2, 16, 128), BF16)],
        [VMEM, anywhere, VMEM, VMEM, anywhere],
        [pltpu.VMEM((64, 32, 128), BF16), pltpu.SemaphoreType.DMA],
    )(modes.reshape(8, 8, 16, 128), weights, table["xf"], table["xi"], direct)
    mixed = exchange(mixed.reshape(128, 16, 128), everyone)
    [out] = call(
        finish,
        [((8, 32, 8, 128), BF16)],
        [VMEM, VMEM, anywhere, anywhere],
        [
            pltpu.VMEM((2048, 128), F32),
            pltpu.VMEM((2048, 128), F32),
            pltpu.VMEM((128, 128), BF16),
            pltpu.VMEM((256, 256), BF16),
            pltpu.SemaphoreType.DMA((2,)),
        ],
    )(mixed.reshape(2048, 128), direct, table["yi"], table["zi"])
    return out


def solution(mesh):
    placed = (
        P(None, "ga", "gx", "gy"),
        P("ga", "gx", "gy"),
        P(),
        P(),
        P(),
        P("ga", "gy", None, "gx", None),
        P(),
    )
    return jax.shard_map(
        shards, mesh=mesh, in_specs=placed, out_specs=P("ga", None, "gx", "gy"), check_vma=False
    )
```

```python
import functools
import math

import jax
import jax.numpy as jnp
import numpy as np
from jax import lax
from jax.experimental import pallas as pl
from jax.experimental.pallas import tpu as pltpu
from jax.sharding import PartitionSpec as P

NZ, C, MX, MY, MZ, GX, GY = 16, 32, 32, 64, 8, 64, 1024
ZL, XL, YL = 8, 16, 256
F32, BF16 = jnp.float32, jnp.bfloat16
ROOT = math.sqrt(2.0 / math.pi)
VMEM = pl.BlockSpec(memory_space=pltpu.VMEM)
SMEM = pl.BlockSpec(memory_space=pltpu.SMEM)


def cos_sin(freq, points, length):
    turn = np.mod(np.outer(freq, points), length) * (2.0 * np.pi / length)
    return np.cos(turn), np.sin(turn)


def split(table):
    table = np.asarray(table, np.float32)
    high = table.astype(jnp.bfloat16)
    low = (table - high.astype(np.float32)).astype(jnp.bfloat16)
    return high, low


@functools.cache
def tables():
    out = {}
    ky = np.arange(MY) - MY // 2
    cy, sy = cos_sin(ky, np.arange(GY), GY)
    rows = np.concatenate([cy, -sy]) / math.sqrt(GY)
    out["yf"] = split(rows)[0].reshape(128, 8, 128).transpose(1, 0, 2)
    out["yi"] = out["yf"]
    cf, sf = (
        np.einsum("kz,cd->czkd", w / math.sqrt(NZ), np.eye(8)).reshape(128, 2, 32)
        for w in cos_sin(np.arange(MZ), np.arange(NZ), NZ)
    )
    zf = np.zeros((2, 128, 2, 2, 32))
    zf[0, :, :, 0], zf[1, :, :, 0], zf[1, :, :, 1], zf[0, :, :, 1] = cf, sf, cf, -sf
    out["zf"] = np.concatenate(split(zf.reshape(256, 128)), axis=1)
    ci, si = (
        np.einsum("kz,op->zokp", w / math.sqrt(NZ), np.eye(16)).reshape(128, 2, 64)
        for w in cos_sin(np.arange(MZ), np.arange(ZL), NZ)
    )
    zi = np.zeros((2, 128, 2, 2, 64))
    zi[0, :, :, 0], zi[0, :, :, 1], zi[1, :, :, 0], zi[1, :, :, 1] = ci, -si, si, ci
    out["zi"] = split(zi.reshape(256, 256))[0]
    kx = np.arange(MX) - MX // 2
    cx, sx = cos_sin(kx, np.arange(GX), GX)
    cr = (cx / 8.0).astype(np.float32).astype(jnp.bfloat16).astype(np.float64)
    sr = (-sx / 8.0).astype(np.float32).astype(jnp.bfloat16).astype(np.float64)
    cr, sr = cr.reshape(8, 4, 8, 2, 4), sr.reshape(8, 4, 8, 2, 4)
    xf = np.zeros((4, 2, 8, 4, 4, 8, 2, 4, 2))
    for k in range(4):
        for a in range(2):
            sign = -1.0 if k * a % 2 else 1.0
            real, imag = sign * cr[:, :, :, a], sign * sr[:, :, :, a]
            xf[k, 0, :, k, :, :, a, :, 0], xf[k, 0, :, k, :, :, a, :, 1] = real, -imag
            xf[k, 1, :, k, :, :, a, :, 0], xf[k, 1, :, k, :, :, a, :, 1] = imag, real
    xf = xf.reshape(4, 256, 128).transpose(1, 0, 2).reshape(256, 512)
    out["xf"] = xf.astype(np.float32).astype(jnp.bfloat16)
    ic, is_ = (cx / 8.0).T.reshape(GX, 8, 1, 4), (sx / 8.0).T.reshape(GX, 8, 1, 4)
    xi = np.zeros((2, GX, 2, 8, 4, 4))
    xi[0, :, 0], xi[0, :, 1] = ic, -is_
    xi[1, :, 0], xi[1, :, 1] = is_, ic
    out["xi"] = np.concatenate(split(xi.reshape(128, 256)))
    return out


def iotas(shape):
    return lax.broadcasted_iota(jnp.int32, shape, 0), lax.broadcasted_iota(jnp.int32, shape, 1)


def halves(value):
    high = value.astype(BF16)
    return high, (value - high.astype(F32)).astype(BF16)


def dot(a, b, contract=((1,), (0,))):
    return lax.dot_general(a, b, (contract, ((), ())), preferred_element_type=F32)


def gelu(v):
    return 0.5 * v * (1.0 + jnp.tanh(ROOT * (v + 0.044715 * (v * v * v))))


def call(kernel, outs, in_specs, scratch=(), mib=16, flops=10**7, size=2**20, out_spec=VMEM):
    return pl.pallas_call(
        kernel,
        out_shape=[jax.ShapeDtypeStruct(s, d) for s, d in outs],
        in_specs=in_specs,
        out_specs=[out_spec] * len(outs),
        scratch_shapes=list(scratch),
        compiler_params=pltpu.CompilerParams(vmem_limit_bytes=mib << 20),
        cost_estimate=pl.CostEstimate(flops=flops, bytes_accessed=size, transcendentals=0),
    )


def rows_of(refs, field, slot, half):
    f, s, fp, sp = refs
    own, other = (s, sp) if field == 5 else (f.at[field], fp.at[field])
    start = 16 * (slot % 8) + 8 * half
    return (own if slot < 8 else other)[pl.ds(pl.multiple_of(start, 8), 8), :]


def edge_rows(f, s, out, rows):
    bottom = lax.axis_index("ga") == 0
    for field in range(6):
        for h in range(2):
            lanes = slice(128 * h, 128 * h + 128)
            rows[field, h] = s[:, lanes] if field == 5 else f[field, :, lanes]
            for d in range(3):
                first = rows[field, h, pl.ds(d, 8, stride=XL), :]
                last = rows[field, h, pl.ds(XL - 1 - d, 8, stride=XL), :]
                out[field, h, 8 * d : 8 * d + 8, :] = jnp.where(bottom, first, last)


def pack_own(f, s, after, own, rows):
    edge_rows(f, s, own, rows)


def pack_other(fp, sp, own, message, other, rows):
    edge_rows(fp, sp, other, rows)
    message[:, :, 0:24, :] = own[...]
    message[:, :, 24:48, :] = other[...]


def pack_y(f, s, fp, sp, message, near, far, outer):
    refs = (f, s, fp, sp)
    a = lax.axis_index("ga")
    row = lax.broadcasted_iota(jnp.int32, (8, 128), 0)
    beyond = jnp.where(a == 1, row, 7 - row) < 3
    lane = lax.broadcasted_iota(jnp.int32, (16, 128), 1) // 4
    lows, highs = jnp.zeros((16, 128), F32), jnp.zeros((16, 128), F32)
    for field in range(6):
        for h in range(2):
            for which in range(2):
                for d in range(3):
                    at = 24 * which + 8 * d
                    value = message[field, h, at : at + 8, :]
                    to = 64 * (1 - which)
                    outer[field, h, pl.ds(to + d, 8, stride=8), :] = value
                    outer[field, h, pl.ds(to + 7 - d, 8, stride=8), :] = value
        for slot in range(16):
            inner, block = rows_of(refs, field, slot, a), rows_of(refs, field, slot, 1 - a)
            edge = slice(8 * slot, 8 * slot + 8)
            for h in range(2):
                kept = block[:, 128 * h : 128 * h + 128]
                outer[field, h, edge, :] = jnp.where(beyond, outer[field, h, edge, :], kept)
            base = 64 * (field % 2) + 4 * slot
            here = lane == base // 4
            first = jnp.concatenate([inner[:, :128], outer[field, 0, edge, :]], axis=0)
            last = jnp.concatenate([inner[:, 128:], outer[field, 1, edge, :]], axis=0)
            lows = jnp.where(here, pltpu.roll(first, base, 1) if base else first, lows)
            highs = jnp.where(here, pltpu.roll(last, (base + 4) % 128, 1) if base != 124 else last, highs)
        if field % 2:
            even = lax.axis_index("gy") % 2 == 0
            far[field // 2] = jnp.where(even, lows, highs)
            near[field // 2] = jnp.where(even, highs, lows)


def stencil(f, s, fp, sp, got, near, far, last, a, b, stiff, outer):
    refs = (f, s, fp, sp)
    core = lax.axis_index("ga")
    even = lax.axis_index("gy") % 2 == 0
    first_lanes = lax.broadcasted_iota(jnp.int32, (16, 128), 1) < 64
    row = lax.broadcasted_iota(jnp.int32, (8, 128), 0)
    beyond = jnp.where(core == 1, row, 7 - row) < 3
    for field in range(6):
        for h in range(2):
            for which in range(2):
                for d in range(3):
                    at = 24 * which + 8 * d
                    value = got[field, h, at : at + 8, :]
                    to = 64 * (1 - which)
                    outer[h, pl.ds(to + d, 8, stride=8), :] = value
                    outer[h, pl.ds(to + 7 - d, 8, stride=8), :] = value
        one, two = near[field // 2], far[field // 2]
        above, below = jnp.where(even, one, two), jnp.where(even, two, one)
        for slot in range(16):
            to = stiff.at[slot] if field == 5 else a.at[field, slot]
            to[0:8, 0:256] = rows_of(refs, field, slot, core)
            block = rows_of(refs, field, slot, 1 - core)
            for h in range(2):
                lanes = slice(128 * h, 128 * h + 128)
                edge = outer[h, 8 * slot : 8 * slot + 8, :]
                to[8:16, lanes] = jnp.where(beyond, edge, block[:, lanes])
            base = 64 * (field % 2) + 4 * slot
            up = pltpu.roll(above, 128 - base, 1) if base else above
            down = pltpu.roll(below, 124 - base, 1) if base != 124 else below
            to[:, 256:384] = jnp.where(first_lanes, up, down)

    def terms(src, field, slot, crop):
        mid = src[field, slot]
        up, down = src[field, (slot + 1) & 15], src[field, (slot + 15) & 15]
        xp, xm = pltpu.roll(mid, 15, 0), pltpu.roll(mid, 1, 0)
        yp, ym = pltpu.roll(mid, 383, 1), pltpu.roll(mid, 1, 1)
        if crop:
            mid, up, down, xp, xm, yp, ym = (v[0:8, 0:256] for v in (mid, up, down, xp, xm, yp, ym))
        total = 0.1 * mid + 0.12 * xp + 0.18 * xm + 0.17 * yp + 0.13 * ym
        return total + 0.14 * up + 0.16 * down, xp - xm, yp - ym, up - down

    def advance(src, slot, crop, store):
        vx, east, _, _ = terms(src, 1, slot, crop)
        vy, _, north, _ = terms(src, 2, slot, crop)
        vz, _, _, depth = terms(src, 3, slot, crop)
        div = 0.1 * (east + north + depth)
        store(0, terms(src, 0, slot, crop)[0] - div)
        pressure, east, north, depth = terms(src, 4, slot, crop)
        store(1, vx - 0.1 * east)
        store(2, vy - 0.1 * north)
        store(3, vz - 0.1 * depth)
        store(4, pressure - (stiff[slot, 0:8, 0:256] if crop else stiff[slot]) * div)

    for src, dst in ((a, b), (b, a), (a, None)):

        def body(slot, carry, src=src, dst=dst):
            def store(field, new):
                if dst is None:
                    rows = pl.ds(pl.multiple_of(slot * 8, 8), 8)
                    for h in range(2):
                        last[field, h, rows, :] = new[:, 128 * h : 128 * h + 128]
                else:
                    dst[field, slot] = new

            advance(src, slot, dst is None, store)
            return carry

        lax.fori_loop(0, 16, body, 0, unroll=True)


def lift_rows(values, weight, bias):
    rows = []
    for c in range(C):
        v = bias[c] + values[0] * weight[0, c]
        for field in range(1, 5):
            v = v + values[field] * weight[field, c]
        rows.append(gelu(v))
    return jnp.concatenate(rows, axis=0).astype(BF16)


def pointwise(keep, got, weight, bias, mix, obias, out, wide):
    a = lax.axis_index("ga")
    wide[pl.ds(pl.multiple_of(160 * a, 8), 160), :] = keep[...]
    wide[pl.ds(pl.multiple_of(160 * (1 - a), 8), 160), :] = got[...]
    row, lane = iotas((256, 32))
    pick = (row // 8 == lane).astype(BF16)
    bias_o = jnp.sum(jnp.where(row // 8 == lane, obias[...], 0.0), axis=1, keepdims=True)
    by_row = dot(pick, mix[...], ((1,), (1,))).astype(BF16)
    row, lane = iotas((256, 256))
    spread = jnp.where(row % 8 == lane % 8, dot(by_row, pick, ((1,), (1,))), 0.0).astype(BF16)

    def body(z, carry):
        values = [wide[pl.ds(8 * field + z, 8, stride=40), :] for field in range(5)]
        out[z] = dot(spread, lift_rows(values, weight, bias)) + bias_o
        return carry

    lax.fori_loop(0, ZL, body, 0)


def forward(
    last, after, weight, bias, yf_far, zf_far, keep, send, out, sums, lifted, modes, yf, zf, sems
):
    copies = [
        pltpu.make_async_copy(yf_far.at[lax.axis_index("gy")], yf, sems.at[0]),
        pltpu.make_async_copy(zf_far, zf, sems.at[1]),
    ]
    for copy in copies:
        copy.start()
    for half in range(2):
        for x in range(4):
            for field in range(5):
                at = 160 * half + 40 * x + 8 * field
                for h in range(2):
                    even = last[field, h, pl.ds(64 * half + 2 * x, 8, stride=8), :]
                    odd = last[field, h, pl.ds(64 * half + 2 * x + 1, 8, stride=8), :]
                    sums[at : at + 8, 128 * h : 128 * h + 128] = even + odd
    value = sums[...]
    high = value.astype(BF16)
    low = (value - high.astype(F32)).astype(BF16)
    row, lane = iotas((256, 128))
    table = jnp.where(row // 2 == lane, 0.25, 0.0).astype(BF16)
    mean = dot(high, table) + dot(low, table)
    keep[...] = mean[:160]
    send[...] = mean[160:]
    for x in range(4):
        at = [40 * x + 8 * field for field in range(5)]
        values = [jnp.concatenate([mean[r : r + 8], mean[r + 160 : r + 168]], axis=0) for r in at]
        lifted[x] = lift_rows(values, weight, bias)
    copies[0].wait()
    for x in range(4):
        modes[x] = dot(yf[...], lifted[x], ((1,), (1,)))
    copies[1].wait()
    parts = []
    for group in range(4):
        lanes = slice(128 * group, 128 * group + 128)
        stack = [
            jnp.concatenate([modes[x, 0:64, lanes], modes[x, 64:128, lanes]], axis=1)
            for x in range(4)
        ]
        m_high, m_low = halves(jnp.concatenate(stack, axis=0))
        both = dot(m_high, zf[...])
        parts.append(both[:, :128] + both[:, 128:] + dot(m_low, zf[:, :128]))
    lane = lax.broadcasted_iota(jnp.int32, (256, 128), 1) // 32
    for part in range(4):
        total = parts[part]
        for group in range(4):
            if group != part:
                moved = pltpu.roll(parts[group], (32 * (group - part)) % 128, 1)
                total = jnp.where(lane == group, moved, total)
        for x in range(4):
            rows = pl.ds(8 * (part // 2) + 2 * x + part % 2, 64, stride=16)
            out[rows, :] = total[64 * x : 64 * x + 64]


def mix_modes(got, weights_far, xf, xi, after, out, weights, sem):
    copy = pltpu.make_async_copy(weights_far, weights, sem)
    copy.start()
    total = got[:, 0]
    for j in range(1, 8):
        total = total + got[:, j]
    both = jnp.concatenate(halves(total.reshape(128, 128)), axis=0)
    row, lane = iotas((128, 512))
    spread = (row // 8 % 4 == lane // 128) & (row // 32 * 8 + row % 8 == lane % 128 // 4)
    wide = dot(both, spread.astype(BF16)).astype(BF16)
    pieces = [
        jnp.concatenate([wide[:128, 128 * k : 128 * k + 128], wide[128:, 128 * k : 128 * k + 128]], axis=1)
        for k in range(4)
    ]
    modes = dot(xf[...], jnp.concatenate(pieces, axis=0))
    modes = modes[:, :128] + modes[:, 128:]
    real, imag = modes[:128], modes[128:]
    highs, lows = [], []
    copy.wait()
    for i in range(8):
        wr = weights[8 * i : 8 * i + 8, 0:16, :].astype(F32).reshape(128, 128)
        wi = weights[8 * i : 8 * i + 8, 16:32, :].astype(F32).reshape(128, 128)
        high, low = halves(
            jnp.concatenate([wr * real - wi * imag, wr * imag + wi * real], axis=0)
        )
        highs.append(high)
        lows.append(low)
    row, lane = iotas((1024, 128))
    gather = (lane // 64 * 16 + lane % 16 == 4 * (row // 128) + row % 4).astype(BF16)
    parts = [jnp.concatenate(part, axis=1) for part in (highs, lows)]
    total = dot(jnp.concatenate(parts, axis=0), gather)
    total = total[:256] + total[256:]
    row, lane = iotas((256, 128))
    total = jnp.where((row // 4) % 4 == (lane // 16) % 4, total, 0.0)
    back = dot(xi[...], jnp.concatenate(halves(total), axis=1))
    back = back[:128, :128] + back[:128, 128:] + back[128:, :128]
    real, imag = back[:64], back[64:]
    lane = lax.broadcasted_iota(jnp.int32, (64, 128), 1)
    parts = [
        jnp.where(lane < 64, real, pltpu.roll(imag, 64, 1)),
        jnp.where(lane < 64, pltpu.roll(real, 64, 1), imag),
    ]
    odd = (lane // 16) % 2 == 1
    for a in range(2):
        signed = [jnp.where(odd, -part, part) for part in parts] if a else parts
        for i in range(8):
            rows = slice(8 * i, 8 * i + 8)
            tile = jnp.concatenate([part[rows] for part in signed], axis=0).astype(BF16)
            for j in range(8):
                out[i, j, a] = tile


def finish(got, direct, yi_far, zi_far, out_far, rows, spectral, yi, zi, out, sems, out_sems):
    copies = [
        pltpu.make_async_copy(yi_far.at[lax.axis_index("gy")], yi, sems.at[0]),
        pltpu.make_async_copy(zi_far, zi, sems.at[1]),
    ]
    for copy in copies:
        copy.start()
    rows[...] = got[...].astype(F32)
    copies[1].wait()
    by_z = []
    for part in range(2):
        stack = []
        for x in range(8):
            pair = [rows[pl.ds(16 * a + 8 * part + x, 64, stride=32), :] for a in range(2)]
            stack.append(jnp.concatenate(pair, axis=1).astype(BF16))
        by_z.append(dot(zi[...], jnp.concatenate(stack, axis=0), ((1,), (1,))))
    blank = jnp.zeros((64, 128), BF16)

    copies[0].wait()
    real, imag = yi[0:64, :], yi[64:128, :]
    pieces = [[real, blank], [blank, real], [imag, blank], [blank, imag]]
    twice = jnp.concatenate([jnp.concatenate(row, axis=1) for row in pieces], axis=0)
    for pair in range(4):
        lanes = slice(128 * pair, 128 * pair + 128)
        value = jnp.concatenate(
            [jnp.concatenate([v[:128, lanes], v[128:, lanes]], axis=1) for v in by_z], axis=0
        )
        high, low = halves(value)
        both = dot(high, twice) + dot(low, twice)
        for x in range(2):
            spectral[pl.ds(2 * pair + x, 256, stride=8), :] = both[:, 128 * x : 128 * x + 128]
    writes = []
    for z in range(ZL):
        for part in range(2):
            at = 128 * (8 * part + z)
            branch = spectral[at : at + 128, :].astype(BF16).astype(F32)
            total = gelu(direct[z, 128 * part : 128 * part + 128, :] + branch)
            out[z, 16 * part : 16 * part + 16] = total.reshape(16, 8, 128).astype(BF16)
        writes.append(pltpu.make_async_copy(out.at[z], out_far.at[z], out_sems.at[z]))
        writes[z].start()
    for write in writes:
        write.wait()


def turn_weights(weights, out, wide):
    for chunk in range(16):
        turned = weights[128 * chunk : 128 * chunk + 128, :].T
        for ri in range(2):
            wide[:, 16 * ri + chunk, :] = turned[64 * ri : 64 * ri + 64]
    out[...] = wide[...].astype(BF16)


def shards(fields, stiffness, lift_weight, lift_bias, mix_weight, spectral_weight, output_bias):
    table = {name: jnp.asarray(value) for name, value in tables().items()}
    everyone = ("gx", "gy", "ga")

    def exchange(value, axis):
        return lax.all_to_all(value, axis, split_axis=0, concat_axis=0, tiled=True)

    anywhere = pl.BlockSpec(memory_space=pl.ANY)
    f = fields.reshape(5, 128, 256)
    s = stiffness.reshape(128, 256)
    swap = [(0, 1), (1, 0)]
    fp, sp = lax.ppermute(f, "ga", swap), lax.ppermute(s, "ga", swap)
    rows = pltpu.VMEM((6, 2, 128, 128), F32)
    edges = ((6, 2, 24, 128), F32)
    [turned] = call(
        turn_weights, [((64, 32, 128), BF16)], [VMEM], [pltpu.VMEM((64, 32, 128), F32)]
    )(spectral_weight.reshape(2048, 128))
    [own] = call(pack_own, [edges], [VMEM] * 2 + [anywhere], [rows])(f, s, turned)
    [message] = call(
        pack_other, [((6, 2, 48, 128), F32)], [VMEM] * 3, [pltpu.VMEM(*edges), rows]
    )(fp, sp, own)
    across = [(2 * i, 2 * ((i - 1) % 8) + 1) for i in range(8)]
    across += [(2 * i + 1, 2 * ((i + 1) % 8)) for i in range(8)]
    got = lax.ppermute(message, ("gx", "ga"), across)

    weights = exchange(turned, ("gx", "gy"))

    message = ((3, 16, 128), F32)
    near, far = call(
        pack_y,
        [message, message],
        [VMEM] * 5,
        [pltpu.VMEM((6, 2, 128, 128), F32)],
        flops=10**12,
    )(f, s, fp, sp, got)
    near = lax.ppermute(near, "gy", [(j, j + 1 - 2 * (j % 2)) for j in range(8)])
    far = lax.ppermute(far, "gy", [(j, (j - 1 + 2 * (j % 2)) % 8) for j in range(8)])
    [last] = call(
        stencil,
        [((5, 2, 128, 128), F32)],
        [VMEM] * 7,
        [
            pltpu.VMEM((5, 16, 16, 384), F32),
            pltpu.VMEM((5, 16, 16, 384), F32),
            pltpu.VMEM((16, 16, 384), F32),
            pltpu.VMEM((2, 128, 128), F32),
        ],
    )(f, s, fp, sp, got, near, far)
    keep, send, modes = call(
        forward,
        [((160, 128), F32), ((160, 128), F32), ((1024, 128), F32)],
        [VMEM, anywhere, SMEM, SMEM, anywhere, anywhere],
        [
            pltpu.VMEM((320, 256), F32),
            pltpu.VMEM((4, 512, 128), BF16),
            pltpu.VMEM((4, 128, 512), F32),
            pltpu.VMEM((128, 128), BF16),
            pltpu.VMEM((256, 256), BF16),
            pltpu.SemaphoreType.DMA((2,)),
        ],
    )(last, weights, lift_weight, lift_bias, table["yf"], table["zf"])
    modes = exchange(modes.reshape(128, 8, 128), everyone)
    [direct] = call(
        pointwise,
        [((8, 256, 128), F32)],
        [VMEM, VMEM, SMEM, SMEM, VMEM, VMEM],
        [pltpu.VMEM((320, 128), F32)],
        flops=3 * 10**8,
    )(keep, lax.ppermute(send, "ga", swap), lift_weight, lift_bias, mix_weight, output_bias.reshape(1, C))

    [mixed] = call(
        mix_modes,
        [((8, 8, 2, 16, 128), BF16)],
        [VMEM, anywhere, VMEM, VMEM, anywhere],
        [pltpu.VMEM((64, 32, 128), BF16), pltpu.SemaphoreType.DMA],
    )(modes.reshape(8, 8, 16, 128), weights, table["xf"], table["xi"], direct)
    mixed = exchange(mixed.reshape(128, 16, 128), everyone)
    [out] = call(
        finish,
        [((8, 32, 8, 128), BF16)],
        [VMEM, VMEM, anywhere, anywhere],
        [
            pltpu.VMEM((2048, 128), F32),
            pltpu.VMEM((2048, 128), F32),
            pltpu.VMEM((128, 128), BF16),
            pltpu.VMEM((256, 256), BF16),
            pltpu.VMEM((8, 32, 8, 128), BF16),
            pltpu.SemaphoreType.DMA((2,)),
            pltpu.SemaphoreType.DMA((8,)),
        ],
        out_spec=anywhere,
    )(mixed.reshape(2048, 128), direct, table["yi"], table["zi"])
    return out


def solution(mesh):
    placed = (
        P(None, "ga", "gx", "gy"),
        P("ga", "gx", "gy"),
        P(),
        P(),
        P(),
        P("ga", "gy", None, "gx", None),
        P(),
    )
    return jax.shard_map(
        shards, mesh=mesh, in_specs=placed, out_specs=P("ga", None, "gx", "gy"), check_vma=False
    )
```

```python
import functools
import math

import jax
import jax.numpy as jnp
import numpy as np
from jax import lax
from jax.experimental import pallas as pl
from jax.experimental.pallas import tpu as pltpu
from jax.sharding import PartitionSpec as P

NZ, C, MX, MY, MZ, GX, GY = 16, 32, 32, 64, 8, 64, 1024
ZL, XL, YL = 8, 16, 256
F32, BF16 = jnp.float32, jnp.bfloat16
ROOT = math.sqrt(2.0 / math.pi)
VMEM = pl.BlockSpec(memory_space=pltpu.VMEM)
SMEM = pl.BlockSpec(memory_space=pltpu.SMEM)


def cos_sin(freq, points, length):
    turn = np.mod(np.outer(freq, points), length) * (2.0 * np.pi / length)
    return np.cos(turn), np.sin(turn)


def split(table):
    table = np.asarray(table, np.float32)
    high = table.astype(jnp.bfloat16)
    low = (table - high.astype(np.float32)).astype(jnp.bfloat16)
    return high, low


@functools.cache
def tables():
    out = {}
    ky = np.arange(MY) - MY // 2
    cy, sy = cos_sin(ky, np.arange(GY), GY)
    rows = np.concatenate([cy, -sy]) / math.sqrt(GY)
    out["yf"] = split(rows)[0].reshape(128, 8, 128).transpose(1, 0, 2)
    out["yi"] = out["yf"]
    cf, sf = (
        np.einsum("kz,cd->czkd", w / math.sqrt(NZ), np.eye(8)).reshape(128, 2, 32)
        for w in cos_sin(np.arange(MZ), np.arange(NZ), NZ)
    )
    zf = np.zeros((2, 128, 2, 2, 32))
    zf[0, :, :, 0], zf[1, :, :, 0], zf[1, :, :, 1], zf[0, :, :, 1] = cf, sf, cf, -sf
    out["zf"] = np.concatenate(split(zf.reshape(256, 128)), axis=1)
    ci, si = (
        np.einsum("kz,op->zokp", w / math.sqrt(NZ), np.eye(16)).reshape(128, 2, 64)
        for w in cos_sin(np.arange(MZ), np.arange(ZL), NZ)
    )
    zi = np.zeros((2, 128, 2, 2, 64))
    zi[0, :, :, 0], zi[0, :, :, 1], zi[1, :, :, 0], zi[1, :, :, 1] = ci, -si, si, ci
    out["zi"] = split(zi.reshape(256, 256))[0]
    kx = np.arange(MX) - MX // 2
    cx, sx = cos_sin(kx, np.arange(GX), GX)
    cr = (cx / 8.0).astype(np.float32).astype(jnp.bfloat16).astype(np.float64)
    sr = (-sx / 8.0).astype(np.float32).astype(jnp.bfloat16).astype(np.float64)
    cr, sr = cr.reshape(8, 4, 8, 2, 4), sr.reshape(8, 4, 8, 2, 4)
    xf = np.zeros((4, 2, 8, 4, 4, 8, 2, 4, 2))
    for k in range(4):
        for a in range(2):
            sign = -1.0 if k * a % 2 else 1.0
            real, imag = sign * cr[:, :, :, a], sign * sr[:, :, :, a]
            xf[k, 0, :, k, :, :, a, :, 0], xf[k, 0, :, k, :, :, a, :, 1] = real, -imag
            xf[k, 1, :, k, :, :, a, :, 0], xf[k, 1, :, k, :, :, a, :, 1] = imag, real
    xf = xf.reshape(4, 256, 128).transpose(1, 0, 2).reshape(256, 512)
    out["xf"] = xf.astype(np.float32).astype(jnp.bfloat16)
    ic, is_ = (cx / 8.0).T.reshape(GX, 8, 1, 4), (sx / 8.0).T.reshape(GX, 8, 1, 4)
    xi = np.zeros((2, GX, 2, 8, 4, 4))
    xi[0, :, 0], xi[0, :, 1] = ic, -is_
    xi[1, :, 0], xi[1, :, 1] = is_, ic
    out["xi"] = np.concatenate(split(xi.reshape(128, 256)))
    return out


def iotas(shape):
    return lax.broadcasted_iota(jnp.int32, shape, 0), lax.broadcasted_iota(jnp.int32, shape, 1)


def halves(value):
    high = value.astype(BF16)
    return high, (value - high.astype(F32)).astype(BF16)


def dot(a, b, contract=((1,), (0,))):
    return lax.dot_general(a, b, (contract, ((), ())), preferred_element_type=F32)


def gelu(v):
    return 0.5 * v * (1.0 + jnp.tanh(ROOT * (v + 0.044715 * (v * v * v))))


def call(kernel, outs, in_specs, scratch=(), mib=16, flops=10**7, size=2**20):
    return pl.pallas_call(
        kernel,
        out_shape=[jax.ShapeDtypeStruct(s, d) for s, d in outs],
        in_specs=in_specs,
        out_specs=[VMEM] * len(outs),
        scratch_shapes=list(scratch),
        compiler_params=pltpu.CompilerParams(vmem_limit_bytes=mib << 20),
        cost_estimate=pl.CostEstimate(flops=flops, bytes_accessed=size, transcendentals=0),
    )


def rows_of(refs, field, slot, half):
    f, s, fp, sp = refs
    own, other = (s, sp) if field == 5 else (f.at[field], fp.at[field])
    start = 16 * (slot % 8) + 8 * half
    return (own if slot < 8 else other)[pl.ds(pl.multiple_of(start, 8), 8), :]


def edge_rows(f, s, out, rows):
    bottom = lax.axis_index("ga") == 0
    for field in range(6):
        for h in range(2):
            lanes = slice(128 * h, 128 * h + 128)
            rows[field, h] = s[:, lanes] if field == 5 else f[field, :, lanes]
            for d in range(3):
                first = rows[field, h, pl.ds(d, 8, stride=XL), :]
                last = rows[field, h, pl.ds(XL - 1 - d, 8, stride=XL), :]
                out[field, h, 8 * d : 8 * d + 8, :] = jnp.where(bottom, first, last)


def pack_own(f, s, after, own, rows):
    edge_rows(f, s, own, rows)


def pack_other(fp, sp, own, message, other, rows):
    edge_rows(fp, sp, other, rows)
    message[:, :, 0:24, :] = own[...]
    message[:, :, 24:48, :] = other[...]


def pack_y(f, s, fp, sp, message, far, near, outer):
    refs = (f, s, fp, sp)
    a = lax.axis_index("ga")
    row = lax.broadcasted_iota(jnp.int32, (8, 128), 0)
    beyond = jnp.where(a == 1, row, 7 - row) < 3
    lane = lax.broadcasted_iota(jnp.int32, (16, 128), 1) // 4
    lows, highs = jnp.zeros((16, 128), F32), jnp.zeros((16, 128), F32)
    for field in range(6):
        for h in range(2):
            for which in range(2):
                for d in range(3):
                    at = 24 * which + 8 * d
                    value = message[field, h, at : at + 8, :]
                    to = 64 * (1 - which)
                    outer[field, h, pl.ds(to + d, 8, stride=8), :] = value
                    outer[field, h, pl.ds(to + 7 - d, 8, stride=8), :] = value
        for slot in range(16):
            inner, block = rows_of(refs, field, slot, a), rows_of(refs, field, slot, 1 - a)
            edge = slice(8 * slot, 8 * slot + 8)
            for h in range(2):
                kept = block[:, 128 * h : 128 * h + 128]
                outer[field, h, edge, :] = jnp.where(beyond, outer[field, h, edge, :], kept)
            base = 64 * (field % 2) + 4 * slot
            here = lane == base // 4
            first = jnp.concatenate([inner[:, :128], outer[field, 0, edge, :]], axis=0)
            last = jnp.concatenate([inner[:, 128:], outer[field, 1, edge, :]], axis=0)
            lows = jnp.where(here, pltpu.roll(first, base, 1) if base else first, lows)
            highs = jnp.where(here, pltpu.roll(last, (base + 4) % 128, 1) if base != 124 else last, highs)
        if field % 2:
            even = lax.axis_index("gy") % 2 == 0
            far[field // 2] = jnp.where(even, lows, highs)
            near[field // 2] = jnp.where(even, highs, lows)


def stencil(f, s, fp, sp, got, far, near, last, a, b, stiff, outer):
    refs = (f, s, fp, sp)
    core = lax.axis_index("ga")
    even = lax.axis_index("gy") % 2 == 0
    first_lanes = lax.broadcasted_iota(jnp.int32, (16, 128), 1) < 64
    row = lax.broadcasted_iota(jnp.int32, (8, 128), 0)
    beyond = jnp.where(core == 1, row, 7 - row) < 3
    for field in range(6):
        for h in range(2):
            for which in range(2):
                for d in range(3):
                    at = 24 * which + 8 * d
                    value = got[field, h, at : at + 8, :]
                    to = 64 * (1 - which)
                    outer[h, pl.ds(to + d, 8, stride=8), :] = value
                    outer[h, pl.ds(to + 7 - d, 8, stride=8), :] = value
        one, two = near[field // 2], far[field // 2]
        above, below = jnp.where(even, one, two), jnp.where(even, two, one)
        for slot in range(16):
            to = stiff.at[slot] if field == 5 else a.at[field, slot]
            to[0:8, 0:256] = rows_of(refs, field, slot, core)
            block = rows_of(refs, field, slot, 1 - core)
            for h in range(2):
                lanes = slice(128 * h, 128 * h + 128)
                edge = outer[h, 8 * slot : 8 * slot + 8, :]
                to[8:16, lanes] = jnp.where(beyond, edge, block[:, lanes])
            base = 64 * (field % 2) + 4 * slot
            up = pltpu.roll(above, 128 - base, 1) if base else above
            down = pltpu.roll(below, 124 - base, 1) if base != 124 else below
            to[:, 256:384] = jnp.where(first_lanes, up, down)

    def terms(src, field, slot, crop):
        mid = src[field, slot]
        up, down = src[field, (slot + 1) & 15], src[field, (slot + 15) & 15]
        xp, xm = pltpu.roll(mid, 15, 0), pltpu.roll(mid, 1, 0)
        yp, ym = pltpu.roll(mid, 383, 1), pltpu.roll(mid, 1, 1)
        if crop:
            mid, up, down, xp, xm, yp, ym = (v[0:8, 0:256] for v in (mid, up, down, xp, xm, yp, ym))
        total = 0.1 * mid + 0.12 * xp + 0.18 * xm + 0.17 * yp + 0.13 * ym
        return total + 0.14 * up + 0.16 * down, xp - xm, yp - ym, up - down

    def advance(src, slot, crop, store):
        vx, east, _, _ = terms(src, 1, slot, crop)
        vy, _, north, _ = terms(src, 2, slot, crop)
        vz, _, _, depth = terms(src, 3, slot, crop)
        div = 0.1 * (east + north + depth)
        store(0, terms(src, 0, slot, crop)[0] - div)
        pressure, east, north, depth = terms(src, 4, slot, crop)
        store(1, vx - 0.1 * east)
        store(2, vy - 0.1 * north)
        store(3, vz - 0.1 * depth)
        store(4, pressure - (stiff[slot, 0:8, 0:256] if crop else stiff[slot]) * div)

    for src, dst in ((a, b), (b, a), (a, None)):

        def body(slot, carry, src=src, dst=dst):
            def store(field, new):
                if dst is None:
                    rows = pl.ds(pl.multiple_of(slot * 8, 8), 8)
                    for h in range(2):
                        last[field, h, rows, :] = new[:, 128 * h : 128 * h + 128]
                else:
                    dst[field, slot] = new

            advance(src, slot, dst is None, store)
            return carry

        lax.fori_loop(0, 16, body, 0, unroll=True)


def lift_rows(values, weight, bias):
    rows = []
    for c in range(C):
        v = bias[c] + values[0] * weight[0, c]
        for field in range(1, 5):
            v = v + values[field] * weight[field, c]
        rows.append(gelu(v))
    return jnp.concatenate(rows, axis=0).astype(BF16)


def pointwise(keep, got, weight, bias, mix, obias, out, wide):
    a = lax.axis_index("ga")
    wide[pl.ds(pl.multiple_of(160 * a, 8), 160), :] = keep[...]
    wide[pl.ds(pl.multiple_of(160 * (1 - a), 8), 160), :] = got[...]
    row, lane = iotas((256, 32))
    pick = (row // 8 == lane).astype(BF16)
    bias_o = jnp.sum(jnp.where(row // 8 == lane, obias[...], 0.0), axis=1, keepdims=True)
    by_row = dot(pick, mix[...], ((1,), (1,))).astype(BF16)
    row, lane = iotas((256, 256))
    spread = jnp.where(row % 8 == lane % 8, dot(by_row, pick, ((1,), (1,))), 0.0).astype(BF16)

    def body(z, carry):
        values = [wide[pl.ds(8 * field + z, 8, stride=40), :] for field in range(5)]
        out[z] = dot(spread, lift_rows(values, weight, bias)) + bias_o
        return carry

    lax.fori_loop(0, ZL, body, 0)


def forward(
    last, after, weight, bias, yf_far, zf_far, keep, send, out, sums, lifted, modes, yf, zf, sems
):
    copies = [
        pltpu.make_async_copy(yf_far.at[lax.axis_index("gy")], yf, sems.at[0]),
        pltpu.make_async_copy(zf_far, zf, sems.at[1]),
    ]
    for copy in copies:
        copy.start()
    for half in range(2):
        for x in range(4):
            for field in range(5):
                at = 160 * half + 40 * x + 8 * field
                for h in range(2):
                    even = last[field, h, pl.ds(64 * half + 2 * x, 8, stride=8), :]
                    odd = last[field, h, pl.ds(64 * half + 2 * x + 1, 8, stride=8), :]
                    sums[at : at + 8, 128 * h : 128 * h + 128] = even + odd
    value = sums[...]
    high = value.astype(BF16)
    low = (value - high.astype(F32)).astype(BF16)
    row, lane = iotas((256, 128))
    table = jnp.where(row // 2 == lane, 0.25, 0.0).astype(BF16)
    mean = dot(high, table) + dot(low, table)
    keep[...] = mean[:160]
    send[...] = mean[160:]
    for x in range(4):
        at = [40 * x + 8 * field for field in range(5)]
        values = [jnp.concatenate([mean[r : r + 8], mean[r + 160 : r + 168]], axis=0) for r in at]
        lifted[x] = lift_rows(values, weight, bias)
    copies[0].wait()
    for x in range(4):
        modes[x] = dot(yf[...], lifted[x], ((1,), (1,)))
    copies[1].wait()
    parts = []
    for group in range(4):
        lanes = slice(128 * group, 128 * group + 128)
        stack = [
            jnp.concatenate([modes[x, 0:64, lanes], modes[x, 64:128, lanes]], axis=1)
            for x in range(4)
        ]
        both = dot(jnp.concatenate(stack, axis=0).astype(BF16), zf[...])
        parts.append(both[:, :128] + both[:, 128:])
    lane = lax.broadcasted_iota(jnp.int32, (256, 128), 1) // 32
    for part in range(4):
        total = parts[part]
        for group in range(4):
            if group != part:
                moved = pltpu.roll(parts[group], (32 * (group - part)) % 128, 1)
                total = jnp.where(lane == group, moved, total)
        for x in range(4):
            rows = pl.ds(8 * (part // 2) + 2 * x + part % 2, 64, stride=16)
            out[rows, :] = total[64 * x : 64 * x + 64]


def mix_modes(got, weights_far, xf, xi, after, out, weights, sem):
    copy = pltpu.make_async_copy(weights_far, weights, sem)
    copy.start()
    total = got[:, 0]
    for j in range(1, 8):
        total = total + got[:, j]
    both = jnp.concatenate(halves(total.reshape(128, 128)), axis=0)
    row, lane = iotas((128, 512))
    spread = (row // 8 % 4 == lane // 128) & (row // 32 * 8 + row % 8 == lane % 128 // 4)
    wide = dot(both, spread.astype(BF16)).astype(BF16)
    pieces = [
        jnp.concatenate([wide[:128, 128 * k : 128 * k + 128], wide[128:, 128 * k : 128 * k + 128]], axis=1)
        for k in range(4)
    ]
    modes = dot(xf[...], jnp.concatenate(pieces, axis=0))
    modes = modes[:, :128] + modes[:, 128:]
    real, imag = modes[:128], modes[128:]
    copy.wait()
    products = []
    for i in range(8):
        wr = weights[8 * i : 8 * i + 8, 0:16, :].astype(F32).reshape(128, 128)
        wi = weights[8 * i : 8 * i + 8, 16:32, :].astype(F32).reshape(128, 128)
        product = jnp.concatenate([wr * real - wi * imag, wr * imag + wi * real], axis=0)
        products.append(product.astype(BF16))
    row, lane = iotas((1024, 128))
    gather = (lane // 64 * 16 + lane % 16 == 4 * (row // 128) + row % 4).astype(BF16)
    total = dot(jnp.concatenate(products, axis=1), gather)
    row, lane = iotas((256, 128))
    total = jnp.where((row // 4) % 4 == (lane // 16) % 4, total, 0.0)
    back = dot(xi[...], jnp.concatenate(halves(total), axis=1))
    back = back[:128, :128] + back[:128, 128:] + back[128:, :128]
    real, imag = back[:64], back[64:]
    lane = lax.broadcasted_iota(jnp.int32, (64, 128), 1)
    parts = [
        jnp.where(lane < 64, real, pltpu.roll(imag, 64, 1)),
        jnp.where(lane < 64, pltpu.roll(real, 64, 1), imag),
    ]
    odd = (lane // 16) % 2 == 1
    for a in range(2):
        signed = [jnp.where(odd, -part, part) for part in parts] if a else parts
        for i in range(8):
            rows = slice(8 * i, 8 * i + 8)
            tile = jnp.concatenate([part[rows] for part in signed], axis=0).astype(BF16)
            for j in range(8):
                out[i, j, a] = tile


def finish(got, direct, yi_far, zi_far, out, rows, spectral, yi, zi, sems):
    copies = [
        pltpu.make_async_copy(yi_far.at[lax.axis_index("gy")], yi, sems.at[0]),
        pltpu.make_async_copy(zi_far, zi, sems.at[1]),
    ]
    for copy in copies:
        copy.start()
    rows[...] = got[...].astype(F32)
    copies[1].wait()
    by_z = []
    for part in range(2):
        stack = []
        for x in range(8):
            pair = [rows[pl.ds(16 * a + 8 * part + x, 64, stride=32), :] for a in range(2)]
            stack.append(jnp.concatenate(pair, axis=1).astype(BF16))
        by_z.append(dot(zi[...], jnp.concatenate(stack, axis=0), ((1,), (1,))))
    blank = jnp.zeros((64, 128), BF16)

    copies[0].wait()
    real, imag = yi[0:64, :], yi[64:128, :]
    pieces = [[real, blank], [blank, real], [imag, blank], [blank, imag]]
    twice = jnp.concatenate([jnp.concatenate(row, axis=1) for row in pieces], axis=0)
    for pair in range(4):
        lanes = slice(128 * pair, 128 * pair + 128)
        value = jnp.concatenate(
            [jnp.concatenate([v[:128, lanes], v[128:, lanes]], axis=1) for v in by_z], axis=0
        )
        both = dot(value.astype(BF16), twice)
        for x in range(2):
            spectral[pl.ds(2 * pair + x, 256, stride=8), :] = both[:, 128 * x : 128 * x + 128]
    for part in range(2):
        for z in range(ZL):
            at = 128 * (8 * part + z)
            branch = spectral[at : at + 128, :].astype(BF16).astype(F32)
            total = gelu(direct[z, 128 * part : 128 * part + 128, :] + branch)
            out[z, 16 * part : 16 * part + 16] = total.reshape(16, 8, 128).astype(BF16)


def turn_weights(weights, out, wide):
    for chunk in range(16):
        turned = weights[128 * chunk : 128 * chunk + 128, :].T
        for ri in range(2):
            wide[:, 16 * ri + chunk, :] = turned[64 * ri : 64 * ri + 64]
    out[...] = wide[...].astype(BF16)


def shards(fields, stiffness, lift_weight, lift_bias, mix_weight, spectral_weight, output_bias):
    table = {name: jnp.asarray(value) for name, value in tables().items()}
    everyone = ("gx", "gy", "ga")

    def exchange(value, axis):
        return lax.all_to_all(value, axis, split_axis=0, concat_axis=0, tiled=True)

    anywhere = pl.BlockSpec(memory_space=pl.ANY)
    f = fields.reshape(5, 128, 256)
    s = stiffness.reshape(128, 256)
    swap = [(0, 1), (1, 0)]
    fp, sp = lax.ppermute(f, "ga", swap), lax.ppermute(s, "ga", swap)
    rows = pltpu.VMEM((6, 2, 128, 128), F32)
    edges = ((6, 2, 24, 128), F32)
    [turned] = call(
        turn_weights, [((64, 32, 128), BF16)], [VMEM], [pltpu.VMEM((64, 32, 128), F32)]
    )(spectral_weight.reshape(2048, 128))
    [own] = call(pack_own, [edges], [VMEM] * 2 + [anywhere], [rows])(f, s, turned)
    [message] = call(
        pack_other, [((6, 2, 48, 128), F32)], [VMEM] * 3, [pltpu.VMEM(*edges), rows]
    )(fp, sp, own)
    across = [(2 * i, 2 * ((i - 1) % 8) + 1) for i in range(8)]
    across += [(2 * i + 1, 2 * ((i + 1) % 8)) for i in range(8)]
    got = lax.ppermute(message, ("gx", "ga"), across)

    weights = exchange(turned, ("gx", "gy"))

    message = ((3, 16, 128), F32)
    far, near = call(
        pack_y,
        [message, message],
        [VMEM] * 5,
        [pltpu.VMEM((6, 2, 128, 128), F32)],
        flops=10**12,
    )(f, s, fp, sp, got)
    far = lax.ppermute(far, "gy", [(j, (j - 1 + 2 * (j % 2)) % 8) for j in range(8)])
    near = lax.ppermute(near, "gy", [(j, j + 1 - 2 * (j % 2)) for j in range(8)])
    [last] = call(
        stencil,
        [((5, 2, 128, 128), F32)],
        [VMEM] * 7,
        [
            pltpu.VMEM((5, 16, 16, 384), F32),
            pltpu.VMEM((5, 16, 16, 384), F32),
            pltpu.VMEM((16, 16, 384), F32),
            pltpu.VMEM((2, 128, 128), F32),
        ],
    )(f, s, fp, sp, got, far, near)
    keep, send, modes = call(
        forward,
        [((160, 128), F32), ((160, 128), F32), ((1024, 128), F32)],
        [VMEM, anywhere, SMEM, SMEM, anywhere, anywhere],
        [
            pltpu.VMEM((320, 256), F32),
            pltpu.VMEM((4, 512, 128), BF16),
            pltpu.VMEM((4, 128, 512), F32),
            pltpu.VMEM((128, 128), BF16),
            pltpu.VMEM((256, 256), BF16),
            pltpu.SemaphoreType.DMA((2,)),
        ],
    )(last, weights, lift_weight, lift_bias, table["yf"], table["zf"])
    modes = exchange(modes.reshape(128, 8, 128), everyone)
    [direct] = call(
        pointwise,
        [((8, 256, 128), F32)],
        [VMEM, VMEM, SMEM, SMEM, VMEM, VMEM],
        [pltpu.VMEM((320, 128), F32)],
        flops=3 * 10**8,
    )(keep, lax.ppermute(send, "ga", swap), lift_weight, lift_bias, mix_weight, output_bias.reshape(1, C))

    [mixed] = call(
        mix_modes,
        [((8, 8, 2, 16, 128), BF16)],
        [VMEM, anywhere, VMEM, VMEM, anywhere],
        [pltpu.VMEM((64, 32, 128), BF16), pltpu.SemaphoreType.DMA],
    )(modes.reshape(8, 8, 16, 128), weights, table["xf"], table["xi"], direct)
    mixed = exchange(mixed.reshape(128, 16, 128), everyone)
    [out] = call(
        finish,
        [((8, 32, 8, 128), BF16)],
        [VMEM, VMEM, anywhere, anywhere],
        [
            pltpu.VMEM((2048, 128), F32),
            pltpu.VMEM((2048, 128), F32),
            pltpu.VMEM((128, 128), BF16),
            pltpu.VMEM((256, 256), BF16),
            pltpu.SemaphoreType.DMA((2,)),
        ],
    )(mixed.reshape(2048, 128), direct, table["yi"], table["zi"])
    return out


def solution(mesh):
    placed = (
        P(None, "ga", "gx", "gy"),
        P("ga", "gx", "gy"),
        P(),
        P(),
        P(),
        P("ga", "gy", None, "gx", None),
        P(),
    )
    return jax.shard_map(
        shards, mesh=mesh, in_specs=placed, out_specs=P("ga", None, "gx", "gy"), check_vma=False
    )
```

```python
import functools
import math

import jax
import jax.numpy as jnp
import numpy as np
from jax import lax
from jax.experimental import pallas as pl
from jax.experimental.pallas import tpu as pltpu
from jax.sharding import PartitionSpec as P

NZ, C, MX, MY, MZ, GX, GY = 16, 32, 32, 64, 8, 64, 1024
ZL, XL, YL = 8, 16, 256
F32, BF16 = jnp.float32, jnp.bfloat16
ROOT = math.sqrt(2.0 / math.pi)
VMEM = pl.BlockSpec(memory_space=pltpu.VMEM)
SMEM = pl.BlockSpec(memory_space=pltpu.SMEM)


def cos_sin(freq, points, length):
    turn = np.mod(np.outer(freq, points), length) * (2.0 * np.pi / length)
    return np.cos(turn), np.sin(turn)


def split(table):
    table = np.asarray(table, np.float32)
    high = table.astype(jnp.bfloat16)
    low = (table - high.astype(np.float32)).astype(jnp.bfloat16)
    return high, low


@functools.cache
def tables():
    out = {}
    ky = np.arange(MY) - MY // 2
    cy, sy = cos_sin(ky, np.arange(GY), GY)
    rows = np.concatenate([cy, -sy]) / math.sqrt(GY)
    out["yf"] = split(rows)[0].reshape(128, 8, 128).transpose(1, 0, 2)
    out["yi"] = out["yf"]
    cf, sf = (
        np.einsum("kz,cd->czkd", w / math.sqrt(NZ), np.eye(8)).reshape(128, 2, 32)
        for w in cos_sin(np.arange(MZ), np.arange(NZ), NZ)
    )
    zf = np.zeros((2, 128, 2, 2, 32))
    zf[0, :, :, 0], zf[1, :, :, 0], zf[1, :, :, 1], zf[0, :, :, 1] = cf, sf, cf, -sf
    out["zf"] = np.concatenate(split(zf.reshape(256, 128)), axis=1)
    ci, si = (
        np.einsum("kz,op->zokp", w / math.sqrt(NZ), np.eye(16)).reshape(128, 2, 64)
        for w in cos_sin(np.arange(MZ), np.arange(ZL), NZ)
    )
    zi = np.zeros((2, 128, 2, 2, 64))
    zi[0, :, :, 0], zi[0, :, :, 1], zi[1, :, :, 0], zi[1, :, :, 1] = ci, -si, si, ci
    out["zi"] = split(zi.reshape(256, 256))[0]
    kx = np.arange(MX) - MX // 2
    cx, sx = cos_sin(kx, np.arange(GX), GX)
    cr = (cx / 8.0).astype(np.float32).astype(jnp.bfloat16).astype(np.float64)
    sr = (-sx / 8.0).astype(np.float32).astype(jnp.bfloat16).astype(np.float64)
    cr, sr = cr.reshape(8, 4, 8, 2, 4), sr.reshape(8, 4, 8, 2, 4)
    xf = np.zeros((4, 2, 8, 4, 4, 8, 2, 4, 2))
    for k in range(4):
        for a in range(2):
            sign = -1.0 if k * a % 2 else 1.0
            real, imag = sign * cr[:, :, :, a], sign * sr[:, :, :, a]
            xf[k, 0, :, k, :, :, a, :, 0], xf[k, 0, :, k, :, :, a, :, 1] = real, -imag
            xf[k, 1, :, k, :, :, a, :, 0], xf[k, 1, :, k, :, :, a, :, 1] = imag, real
    xf = xf.reshape(4, 256, 128).transpose(1, 0, 2).reshape(256, 512)
    out["xf"] = xf.astype(np.float32).astype(jnp.bfloat16)
    ic, is_ = (cx / 8.0).T.reshape(GX, 8, 1, 4), (sx / 8.0).T.reshape(GX, 8, 1, 4)
    xi = np.zeros((2, GX, 2, 8, 4, 4))
    xi[0, :, 0], xi[0, :, 1] = ic, -is_
    xi[1, :, 0], xi[1, :, 1] = is_, ic
    out["xi"] = np.concatenate(split(xi.reshape(128, 256)))
    return out


def iotas(shape):
    return lax.broadcasted_iota(jnp.int32, shape, 0), lax.broadcasted_iota(jnp.int32, shape, 1)


def halves(value):
    high = value.astype(BF16)
    return high, (value - high.astype(F32)).astype(BF16)


def dot(a, b, contract=((1,), (0,))):
    return lax.dot_general(a, b, (contract, ((), ())), preferred_element_type=F32)


def gelu(v):
    return 0.5 * v * (1.0 + jnp.tanh(ROOT * (v + 0.044715 * (v * v * v))))


def call(kernel, outs, in_specs, scratch=(), mib=16, flops=10**7, size=2**20):
    return pl.pallas_call(
        kernel,
        out_shape=[jax.ShapeDtypeStruct(s, d) for s, d in outs],
        in_specs=in_specs,
        out_specs=[VMEM] * len(outs),
        scratch_shapes=list(scratch),
        compiler_params=pltpu.CompilerParams(vmem_limit_bytes=mib << 20),
        cost_estimate=pl.CostEstimate(flops=flops, bytes_accessed=size, transcendentals=0),
    )


def rows_of(refs, field, slot, half):
    f, s, fp, sp = refs
    own, other = (s, sp) if field == 5 else (f.at[field], fp.at[field])
    start = 16 * (slot % 8) + 8 * half
    return (own if slot < 8 else other)[pl.ds(pl.multiple_of(start, 8), 8), :]


def edge_rows(f, s, out, rows):
    bottom = lax.axis_index("ga") == 0
    for field in range(6):
        for h in range(2):
            lanes = slice(128 * h, 128 * h + 128)
            rows[field, h] = s[:, lanes] if field == 5 else f[field, :, lanes]
            for d in range(3):
                first = rows[field, h, pl.ds(d, 8, stride=XL), :]
                last = rows[field, h, pl.ds(XL - 1 - d, 8, stride=XL), :]
                out[field, h, 8 * d : 8 * d + 8, :] = jnp.where(bottom, first, last)


def pack_own(f, s, after, own, rows):
    edge_rows(f, s, own, rows)


def pack_other(fp, sp, own, message, other, rows):
    edge_rows(fp, sp, other, rows)
    message[:, :, 0:24, :] = own[...]
    message[:, :, 24:48, :] = other[...]


def pack_y(f, s, fp, sp, message, far, near, outer):
    refs = (f, s, fp, sp)
    a = lax.axis_index("ga")
    row = lax.broadcasted_iota(jnp.int32, (8, 128), 0)
    beyond = jnp.where(a == 1, row, 7 - row) < 3
    lane = lax.broadcasted_iota(jnp.int32, (16, 128), 1) // 4
    lows, highs = jnp.zeros((16, 128), F32), jnp.zeros((16, 128), F32)
    for field in range(6):
        for h in range(2):
            for which in range(2):
                for d in range(3):
                    at = 24 * which + 8 * d
                    value = message[field, h, at : at + 8, :]
                    to = 64 * (1 - which)
                    outer[field, h, pl.ds(to + d, 8, stride=8), :] = value
                    outer[field, h, pl.ds(to + 7 - d, 8, stride=8), :] = value
        for slot in range(16):
            inner, block = rows_of(refs, field, slot, a), rows_of(refs, field, slot, 1 - a)
            edge = slice(8 * slot, 8 * slot + 8)
            for h in range(2):
                kept = block[:, 128 * h : 128 * h + 128]
                outer[field, h, edge, :] = jnp.where(beyond, outer[field, h, edge, :], kept)
            base = 64 * (field % 2) + 4 * slot
            here = lane == base // 4
            first = jnp.concatenate([inner[:, :128], outer[field, 0, edge, :]], axis=0)
            last = jnp.concatenate([inner[:, 128:], outer[field, 1, edge, :]], axis=0)
            lows = jnp.where(here, pltpu.roll(first, base, 1) if base else first, lows)
            highs = jnp.where(here, pltpu.roll(last, (base + 4) % 128, 1) if base != 124 else last, highs)
        if field % 2:
            even = lax.axis_index("gy") % 2 == 0
            far[field // 2] = jnp.where(even, lows, highs)
            near[field // 2] = jnp.where(even, highs, lows)


def stencil(f, s, fp, sp, got, far, near, last, a, b, stiff, outer):
    refs = (f, s, fp, sp)
    core = lax.axis_index("ga")
    even = lax.axis_index("gy") % 2 == 0
    first_lanes = lax.broadcasted_iota(jnp.int32, (16, 128), 1) < 64
    row = lax.broadcasted_iota(jnp.int32, (8, 128), 0)
    beyond = jnp.where(core == 1, row, 7 - row) < 3
    for field in range(6):
        for h in range(2):
            for which in range(2):
                for d in range(3):
                    at = 24 * which + 8 * d
                    value = got[field, h, at : at + 8, :]
                    to = 64 * (1 - which)
                    outer[h, pl.ds(to + d, 8, stride=8), :] = value
                    outer[h, pl.ds(to + 7 - d, 8, stride=8), :] = value
        one, two = near[field // 2], far[field // 2]
        above, below = jnp.where(even, one, two), jnp.where(even, two, one)
        for slot in range(16):
            to = stiff.at[slot] if field == 5 else a.at[field, slot]
            to[0:8, 0:256] = rows_of(refs, field, slot, core)
            block = rows_of(refs, field, slot, 1 - core)
            for h in range(2):
                lanes = slice(128 * h, 128 * h + 128)
                edge = outer[h, 8 * slot : 8 * slot + 8, :]
                to[8:16, lanes] = jnp.where(beyond, edge, block[:, lanes])
            base = 64 * (field % 2) + 4 * slot
            up = pltpu.roll(above, 128 - base, 1) if base else above
            down = pltpu.roll(below, 124 - base, 1) if base != 124 else below
            to[:, 256:384] = jnp.where(first_lanes, up, down)

    def terms(src, field, slot, crop):
        mid = src[field, slot]
        up, down = src[field, (slot + 1) & 15], src[field, (slot + 15) & 15]
        xp, xm = pltpu.roll(mid, 15, 0), pltpu.roll(mid, 1, 0)
        yp, ym = pltpu.roll(mid, 383, 1), pltpu.roll(mid, 1, 1)
        if crop:
            mid, up, down, xp, xm, yp, ym = (v[0:8, 0:256] for v in (mid, up, down, xp, xm, yp, ym))
        total = 0.1 * mid + 0.12 * xp + 0.18 * xm + 0.17 * yp + 0.13 * ym
        return total + 0.14 * up + 0.16 * down, xp - xm, yp - ym, up - down

    def advance(src, slot, crop, store):
        vx, east, _, _ = terms(src, 1, slot, crop)
        vy, _, north, _ = terms(src, 2, slot, crop)
        vz, _, _, depth = terms(src, 3, slot, crop)
        div = 0.1 * (east + north + depth)
        store(0, terms(src, 0, slot, crop)[0] - div)
        pressure, east, north, depth = terms(src, 4, slot, crop)
        store(1, vx - 0.1 * east)
        store(2, vy - 0.1 * north)
        store(3, vz - 0.1 * depth)
        store(4, pressure - (stiff[slot, 0:8, 0:256] if crop else stiff[slot]) * div)

    for src, dst in ((a, b), (b, a), (a, None)):

        def body(slot, carry, src=src, dst=dst):
            def store(field, new):
                if dst is None:
                    rows = pl.ds(pl.multiple_of(slot * 8, 8), 8)
                    for h in range(2):
                        last[field, h, rows, :] = new[:, 128 * h : 128 * h + 128]
                else:
                    dst[field, slot] = new

            advance(src, slot, dst is None, store)
            return carry

        lax.fori_loop(0, 16, body, 0, unroll=True)


def lift_rows(values, weight, bias):
    rows = []
    for c in range(C):
        v = bias[c] + values[0] * weight[0, c]
        for field in range(1, 5):
            v = v + values[field] * weight[field, c]
        rows.append(gelu(v))
    return jnp.concatenate(rows, axis=0).astype(BF16)


def pointwise(keep, got, weight, bias, mix, obias, out, wide):
    a = lax.axis_index("ga")
    wide[pl.ds(pl.multiple_of(160 * a, 8), 160), :] = keep[...]
    wide[pl.ds(pl.multiple_of(160 * (1 - a), 8), 160), :] = got[...]
    row, lane = iotas((256, 32))
    pick = (row // 8 == lane).astype(BF16)
    bias_o = jnp.sum(jnp.where(row // 8 == lane, obias[...], 0.0), axis=1, keepdims=True)
    by_row = dot(pick, mix[...], ((1,), (1,))).astype(BF16)
    row, lane = iotas((256, 256))
    spread = jnp.where(row % 8 == lane % 8, dot(by_row, pick, ((1,), (1,))), 0.0).astype(BF16)

    def body(z, carry):
        values = [wide[pl.ds(8 * field + z, 8, stride=40), :] for field in range(5)]
        out[z] = dot(spread, lift_rows(values, weight, bias)) + bias_o
        return carry

    lax.fori_loop(0, ZL, body, 0)


def forward(
    last, after, weight, bias, yf_far, zf_far, keep, send, out, sums, lifted, modes, yf, zf, sems
):
    copies = [
        pltpu.make_async_copy(yf_far.at[lax.axis_index("gy")], yf, sems.at[0]),
        pltpu.make_async_copy(zf_far, zf, sems.at[1]),
    ]
    for copy in copies:
        copy.start()
    for half in range(2):
        for x in range(4):
            for field in range(5):
                at = 160 * half + 40 * x + 8 * field
                for h in range(2):
                    even = last[field, h, pl.ds(64 * half + 2 * x, 8, stride=8), :]
                    odd = last[field, h, pl.ds(64 * half + 2 * x + 1, 8, stride=8), :]
                    sums[at : at + 8, 128 * h : 128 * h + 128] = even + odd
    value = sums[...]
    high = value.astype(BF16)
    low = (value - high.astype(F32)).astype(BF16)
    row, lane = iotas((256, 128))
    table = jnp.where(row // 2 == lane, 0.25, 0.0).astype(BF16)
    mean = dot(high, table) + dot(low, table)
    keep[...] = mean[:160]
    send[...] = mean[160:]
    for x in range(4):
        at = [40 * x + 8 * field for field in range(5)]
        values = [jnp.concatenate([mean[r : r + 8], mean[r + 160 : r + 168]], axis=0) for r in at]
        lifted[x] = lift_rows(values, weight, bias)
    copies[0].wait()
    for x in range(4):
        modes[x] = dot(yf[...], lifted[x], ((1,), (1,)))
    copies[1].wait()
    parts = []
    for group in range(4):
        lanes = slice(128 * group, 128 * group + 128)
        stack = [
            jnp.concatenate([modes[x, 0:64, lanes], modes[x, 64:128, lanes]], axis=1)
            for x in range(4)
        ]
        both = dot(jnp.concatenate(stack, axis=0).astype(BF16), zf[...])
        parts.append(both[:, :128] + both[:, 128:])
    lane = lax.broadcasted_iota(jnp.int32, (256, 128), 1) // 32
    for part in range(4):
        total = parts[part]
        for group in range(4):
            if group != part:
                moved = pltpu.roll(parts[group], (32 * (group - part)) % 128, 1)
                total = jnp.where(lane == group, moved, total)
        for x in range(4):
            rows = pl.ds(8 * (part // 2) + 2 * x + part % 2, 64, stride=16)
            out[rows, :] = total[64 * x : 64 * x + 64]


def mix_modes(got, weights_far, xf, xi, after, out, weights, sem):
    copy = pltpu.make_async_copy(weights_far, weights, sem)
    copy.start()
    total = got[:, 0]
    for j in range(1, 8):
        total = total + got[:, j]
    both = jnp.concatenate(halves(total.reshape(128, 128)), axis=0)
    row, lane = iotas((128, 512))
    spread = (row // 8 % 4 == lane // 128) & (row // 32 * 8 + row % 8 == lane % 128 // 4)
    wide = dot(both, spread.astype(BF16)).astype(BF16)
    pieces = [
        jnp.concatenate([wide[:128, 128 * k : 128 * k + 128], wide[128:, 128 * k : 128 * k + 128]], axis=1)
        for k in range(4)
    ]
    modes = dot(xf[...], jnp.concatenate(pieces, axis=0))
    modes = modes[:, :128] + modes[:, 128:]
    real, imag = modes[:128], modes[128:]
    copy.wait()
    products = []
    for i in range(8):
        wr = weights[8 * i : 8 * i + 8, 0:16, :].astype(F32).reshape(128, 128)
        wi = weights[8 * i : 8 * i + 8, 16:32, :].astype(F32).reshape(128, 128)
        product = jnp.concatenate([wr * real - wi * imag, wr * imag + wi * real], axis=0)
        products.append(product.astype(BF16))
    row, lane = iotas((1024, 128))
    gather = (lane // 64 * 16 + lane % 16 == 4 * (row // 128) + row % 4).astype(BF16)
    total = dot(jnp.concatenate(products, axis=1), gather)
    row, lane = iotas((256, 128))
    total = jnp.where((row // 4) % 4 == (lane // 16) % 4, total, 0.0)
    back = dot(xi[...], jnp.concatenate(halves(total), axis=1))
    back = back[:128, :128] + back[:128, 128:] + back[128:, :128]
    real, imag = back[:64], back[64:]
    lane = lax.broadcasted_iota(jnp.int32, (64, 128), 1)
    parts = [
        jnp.where(lane < 64, real, pltpu.roll(imag, 64, 1)),
        jnp.where(lane < 64, pltpu.roll(real, 64, 1), imag),
    ]
    odd = (lane // 16) % 2 == 1
    for a in range(2):
        signed = [jnp.where(odd, -part, part) for part in parts] if a else parts
        for i in range(8):
            rows = slice(8 * i, 8 * i + 8)
            tile = jnp.concatenate([part[rows] for part in signed], axis=0).astype(BF16)
            for j in range(8):
                out[i, j, a] = tile


def finish(got, direct, yi_far, zi_far, out, rows, spectral, yi, zi, sems):
    copies = [
        pltpu.make_async_copy(yi_far.at[lax.axis_index("gy")], yi, sems.at[0]),
        pltpu.make_async_copy(zi_far, zi, sems.at[1]),
    ]
    for copy in copies:
        copy.start()
    for ky in range(64):
        rows[33 * ky : 33 * ky + 32, :] = got[32 * ky : 32 * ky + 32, :].astype(F32)
    copies[1].wait()
    by_z = []
    for part in range(2):
        stack = []
        for x in range(8):
            pair = [rows[pl.ds(16 * a + 8 * part + x, 64, stride=33), :] for a in range(2)]
            stack.append(jnp.concatenate(pair, axis=1).astype(BF16))
        by_z.append(dot(zi[...], jnp.concatenate(stack, axis=0), ((1,), (1,))))
    blank = jnp.zeros((64, 128), BF16)

    copies[0].wait()
    real, imag = yi[0:64, :], yi[64:128, :]
    pieces = [[real, blank], [blank, real], [imag, blank], [blank, imag]]
    twice = jnp.concatenate([jnp.concatenate(row, axis=1) for row in pieces], axis=0)
    for pair in range(4):
        lanes = slice(128 * pair, 128 * pair + 128)
        value = jnp.concatenate(
            [jnp.concatenate([v[:128, lanes], v[128:, lanes]], axis=1) for v in by_z], axis=0
        )
        both = dot(value.astype(BF16), twice)
        for x in range(2):
            spectral[pl.ds(2 * pair + x, 256, stride=9), :] = both[:, 128 * x : 128 * x + 128]
    for part in range(2):
        for z in range(ZL):
            first = 16 * (8 * part + z)
            branch = [spectral[9 * n : 9 * n + 8, :] for n in range(first, first + 16)]
            branch = jnp.concatenate(branch, axis=0).astype(BF16).astype(F32)
            total = gelu(direct[z, 128 * part : 128 * part + 128, :] + branch)
            out[z, 16 * part : 16 * part + 16] = total.reshape(16, 8, 128).astype(BF16)


def turn_weights(weights, out, wide):
    for chunk in range(16):
        turned = weights[128 * chunk : 128 * chunk + 128, :].T
        for ri in range(2):
            wide[:, 16 * ri + chunk, :] = turned[64 * ri : 64 * ri + 64]
    out[...] = wide[...].astype(BF16)


def shards(fields, stiffness, lift_weight, lift_bias, mix_weight, spectral_weight, output_bias):
    table = {name: jnp.asarray(value) for name, value in tables().items()}
    everyone = ("gx", "gy", "ga")

    def exchange(value, axis):
        return lax.all_to_all(value, axis, split_axis=0, concat_axis=0, tiled=True)

    anywhere = pl.BlockSpec(memory_space=pl.ANY)
    f = fields.reshape(5, 128, 256)
    s = stiffness.reshape(128, 256)
    swap = [(0, 1), (1, 0)]
    fp, sp = lax.ppermute(f, "ga", swap), lax.ppermute(s, "ga", swap)
    rows = pltpu.VMEM((6, 2, 128, 128), F32)
    edges = ((6, 2, 24, 128), F32)
    [turned] = call(
        turn_weights, [((64, 32, 128), BF16)], [VMEM], [pltpu.VMEM((64, 32, 128), F32)]
    )(spectral_weight.reshape(2048, 128))
    [own] = call(pack_own, [edges], [VMEM] * 2 + [anywhere], [rows])(f, s, turned)
    [message] = call(
        pack_other, [((6, 2, 48, 128), F32)], [VMEM] * 3, [pltpu.VMEM(*edges), rows]
    )(fp, sp, own)
    across = [(2 * i, 2 * ((i - 1) % 8) + 1) for i in range(8)]
    across += [(2 * i + 1, 2 * ((i + 1) % 8)) for i in range(8)]
    got = lax.ppermute(message, ("gx", "ga"), across)

    weights = exchange(turned, ("gx", "gy"))

    message = ((3, 16, 128), F32)
    far, near = call(
        pack_y,
        [message, message],
        [VMEM] * 5,
        [pltpu.VMEM((6, 2, 128, 128), F32)],
        flops=10**12,
    )(f, s, fp, sp, got)
    far = lax.ppermute(far, "gy", [(j, (j - 1 + 2 * (j % 2)) % 8) for j in range(8)])
    near = lax.ppermute(near, "gy", [(j, j + 1 - 2 * (j % 2)) for j in range(8)])
    [last] = call(
        stencil,
        [((5, 2, 128, 128), F32)],
        [VMEM] * 7,
        [
            pltpu.VMEM((5, 16, 16, 384), F32),
            pltpu.VMEM((5, 16, 16, 384), F32),
            pltpu.VMEM((16, 16, 384), F32),
            pltpu.VMEM((2, 128, 128), F32),
        ],
    )(f, s, fp, sp, got, far, near)
    keep, send, modes = call(
        forward,
        [((160, 128), F32), ((160, 128), F32), ((1024, 128), F32)],
        [VMEM, anywhere, SMEM, SMEM, anywhere, anywhere],
        [
            pltpu.VMEM((320, 256), F32),
            pltpu.VMEM((4, 512, 128), BF16),
            pltpu.VMEM((4, 128, 512), F32),
            pltpu.VMEM((128, 128), BF16),
            pltpu.VMEM((256, 256), BF16),
            pltpu.SemaphoreType.DMA((2,)),
        ],
    )(last, weights, lift_weight, lift_bias, table["yf"], table["zf"])
    modes = exchange(modes.reshape(128, 8, 128), everyone)
    [direct] = call(
        pointwise,
        [((8, 256, 128), F32)],
        [VMEM, VMEM, SMEM, SMEM, VMEM, VMEM],
        [pltpu.VMEM((320, 128), F32)],
        flops=3 * 10**8,
    )(keep, lax.ppermute(send, "ga", swap), lift_weight, lift_bias, mix_weight, output_bias.reshape(1, C))

    [mixed] = call(
        mix_modes,
        [((8, 8, 2, 16, 128), BF16)],
        [VMEM, anywhere, VMEM, VMEM, anywhere],
        [pltpu.VMEM((64, 32, 128), BF16), pltpu.SemaphoreType.DMA],
    )(modes.reshape(8, 8, 16, 128), weights, table["xf"], table["xi"], direct)
    mixed = exchange(mixed.reshape(128, 16, 128), everyone)
    [out] = call(
        finish,
        [((8, 32, 8, 128), BF16)],
        [VMEM, VMEM, anywhere, anywhere],
        [
            pltpu.VMEM((64 * 33, 128), F32),
            pltpu.VMEM((256 * 9, 128), F32),
            pltpu.VMEM((128, 128), BF16),
            pltpu.VMEM((256, 256), BF16),
            pltpu.SemaphoreType.DMA((2,)),
        ],
    )(mixed.reshape(2048, 128), direct, table["yi"], table["zi"])
    return out


def solution(mesh):
    placed = (
        P(None, "ga", "gx", "gy"),
        P("ga", "gx", "gy"),
        P(),
        P(),
        P(),
        P("ga", "gy", None, "gx", None),
        P(),
    )
    return jax.shard_map(
        shards, mesh=mesh, in_specs=placed, out_specs=P("ga", None, "gx", "gy"), check_vma=False
    )
```

```python
import functools
import math

import jax
import jax.numpy as jnp
import numpy as np
from jax import lax
from jax.experimental import pallas as pl
from jax.experimental.pallas import tpu as pltpu
from jax.sharding import PartitionSpec as P

NZ, C, MX, MY, MZ, GX, GY = 16, 32, 32, 64, 8, 64, 1024
ZL, XL, YL = 8, 16, 256
F32, BF16 = jnp.float32, jnp.bfloat16
ROOT = math.sqrt(2.0 / math.pi)
VMEM = pl.BlockSpec(memory_space=pltpu.VMEM)
SMEM = pl.BlockSpec(memory_space=pltpu.SMEM)


def cos_sin(freq, points, length):
    turn = np.mod(np.outer(freq, points), length) * (2.0 * np.pi / length)
    return np.cos(turn), np.sin(turn)


def split(table):
    table = np.asarray(table, np.float32)
    high = table.astype(jnp.bfloat16)
    low = (table - high.astype(np.float32)).astype(jnp.bfloat16)
    return high, low


@functools.cache
def tables():
    out = {}
    ky = np.arange(MY) - MY // 2
    cy, sy = cos_sin(ky, np.arange(GY), GY)
    rows = np.concatenate([cy, -sy]) / math.sqrt(GY)
    out["yf"] = split(rows)[0].reshape(128, 8, 128).transpose(1, 0, 2)
    out["yi"] = out["yf"]
    cf, sf = (
        np.einsum("kz,cd->czkd", w / math.sqrt(NZ), np.eye(8)).reshape(128, 2, 32)
        for w in cos_sin(np.arange(MZ), np.arange(NZ), NZ)
    )
    zf = np.zeros((2, 128, 2, 2, 32))
    zf[0, :, :, 0], zf[1, :, :, 0], zf[1, :, :, 1], zf[0, :, :, 1] = cf, sf, cf, -sf
    out["zf"] = np.concatenate(split(zf.reshape(256, 128)), axis=1)
    ci, si = (
        np.einsum("kz,op->zokp", w / math.sqrt(NZ), np.eye(16)).reshape(128, 2, 64)
        for w in cos_sin(np.arange(MZ), np.arange(ZL), NZ)
    )
    zi = np.zeros((2, 128, 2, 2, 64))
    zi[0, :, :, 0], zi[0, :, :, 1], zi[1, :, :, 0], zi[1, :, :, 1] = ci, -si, si, ci
    out["zi"] = split(zi.reshape(256, 256))[0]
    kx = np.arange(MX) - MX // 2
    cx, sx = cos_sin(kx, np.arange(GX), GX)
    cr = (cx / 8.0).astype(np.float32).astype(jnp.bfloat16).astype(np.float64)
    sr = (-sx / 8.0).astype(np.float32).astype(jnp.bfloat16).astype(np.float64)
    cr, sr = cr.reshape(8, 4, 8, 2, 4), sr.reshape(8, 4, 8, 2, 4)
    xf = np.zeros((4, 2, 8, 4, 4, 8, 2, 4, 2))
    for k in range(4):
        for a in range(2):
            sign = -1.0 if k * a % 2 else 1.0
            real, imag = sign * cr[:, :, :, a], sign * sr[:, :, :, a]
            xf[k, 0, :, k, :, :, a, :, 0], xf[k, 0, :, k, :, :, a, :, 1] = real, -imag
            xf[k, 1, :, k, :, :, a, :, 0], xf[k, 1, :, k, :, :, a, :, 1] = imag, real
    xf = xf.reshape(4, 256, 128).transpose(1, 0, 2).reshape(256, 512)
    out["xf"] = xf.astype(np.float32).astype(jnp.bfloat16)
    ic, is_ = (cx / 8.0).T.reshape(GX, 8, 1, 4), (sx / 8.0).T.reshape(GX, 8, 1, 4)
    xi = np.zeros((2, GX, 2, 8, 4, 4))
    xi[0, :, 0], xi[0, :, 1] = ic, -is_
    xi[1, :, 0], xi[1, :, 1] = is_, ic
    out["xi"] = np.concatenate(split(xi.reshape(128, 256)))
    return out


def iotas(shape):
    return lax.broadcasted_iota(jnp.int32, shape, 0), lax.broadcasted_iota(jnp.int32, shape, 1)


def halves(value):
    high = value.astype(BF16)
    return high, (value - high.astype(F32)).astype(BF16)


def dot(a, b, contract=((1,), (0,))):
    return lax.dot_general(a, b, (contract, ((), ())), preferred_element_type=F32)


def gelu(v):
    return 0.5 * v * (1.0 + jnp.tanh(ROOT * (v + 0.044715 * (v * v * v))))


def call(kernel, outs, in_specs, scratch=(), mib=16, flops=10**7, size=2**20):
    return pl.pallas_call(
        kernel,
        out_shape=[jax.ShapeDtypeStruct(s, d) for s, d in outs],
        in_specs=in_specs,
        out_specs=[VMEM] * len(outs),
        scratch_shapes=list(scratch),
        compiler_params=pltpu.CompilerParams(vmem_limit_bytes=mib << 20),
        cost_estimate=pl.CostEstimate(flops=flops, bytes_accessed=size, transcendentals=0),
    )


def rows_of(refs, field, slot, half):
    f, s, fp, sp = refs
    own, other = (s, sp) if field == 5 else (f.at[field], fp.at[field])
    start = 16 * (slot % 8) + 8 * half
    return (own if slot < 8 else other)[pl.ds(pl.multiple_of(start, 8), 8), :]


def edge_rows(f, s, out, rows):
    bottom = lax.axis_index("ga") == 0
    for field in range(6):
        for h in range(2):
            lanes = slice(128 * h, 128 * h + 128)
            rows[field, h] = s[:, lanes] if field == 5 else f[field, :, lanes]
            for d in range(3):
                first = rows[field, h, pl.ds(d, 8, stride=XL), :]
                last = rows[field, h, pl.ds(XL - 1 - d, 8, stride=XL), :]
                out[field, h, 8 * d : 8 * d + 8, :] = jnp.where(bottom, first, last)


def pack_own(f, s, after, own, rows):
    edge_rows(f, s, own, rows)


def pack_other(fp, sp, own, message, other, rows):
    edge_rows(fp, sp, other, rows)
    message[:, :, 0:24, :] = own[...]
    message[:, :, 24:48, :] = other[...]


def pack_y(f, s, fp, sp, message, far, near, outer):
    refs = (f, s, fp, sp)
    a = lax.axis_index("ga")
    row = lax.broadcasted_iota(jnp.int32, (8, 128), 0)
    beyond = jnp.where(a == 1, row, 7 - row) < 3
    lane = lax.broadcasted_iota(jnp.int32, (16, 128), 1) // 4
    lows, highs = jnp.zeros((16, 128), F32), jnp.zeros((16, 128), F32)
    for field in range(6):
        for h in range(2):
            for which in range(2):
                for d in range(3):
                    at = 24 * which + 8 * d
                    value = message[field, h, at : at + 8, :]
                    to = 64 * (1 - which)
                    outer[field, h, pl.ds(to + d, 8, stride=8), :] = value
                    outer[field, h, pl.ds(to + 7 - d, 8, stride=8), :] = value
        for slot in range(16):
            inner, block = rows_of(refs, field, slot, a), rows_of(refs, field, slot, 1 - a)
            edge = slice(8 * slot, 8 * slot + 8)
            for h in range(2):
                kept = block[:, 128 * h : 128 * h + 128]
                outer[field, h, edge, :] = jnp.where(beyond, outer[field, h, edge, :], kept)
            base = 64 * (field % 2) + 4 * slot
            here = lane == base // 4
            first = jnp.concatenate([inner[:, :128], outer[field, 0, edge, :]], axis=0)
            last = jnp.concatenate([inner[:, 128:], outer[field, 1, edge, :]], axis=0)
            lows = jnp.where(here, pltpu.roll(first, base, 1) if base else first, lows)
            highs = jnp.where(here, pltpu.roll(last, (base + 4) % 128, 1) if base != 124 else last, highs)
        if field % 2:
            even = lax.axis_index("gy") % 2 == 0
            far[field // 2] = jnp.where(even, lows, highs)
            near[field // 2] = jnp.where(even, highs, lows)


def stencil(f, s, fp, sp, got, far, near, last, a, b, stiff, outer):
    refs = (f, s, fp, sp)
    core = lax.axis_index("ga")
    even = lax.axis_index("gy") % 2 == 0
    first_lanes = lax.broadcasted_iota(jnp.int32, (16, 128), 1) < 64
    row = lax.broadcasted_iota(jnp.int32, (8, 128), 0)
    beyond = jnp.where(core == 1, row, 7 - row) < 3
    for field in range(6):
        for h in range(2):
            for which in range(2):
                for d in range(3):
                    at = 24 * which + 8 * d
                    value = got[field, h, at : at + 8, :]
                    to = 64 * (1 - which)
                    outer[h, pl.ds(to + d, 8, stride=8), :] = value
                    outer[h, pl.ds(to + 7 - d, 8, stride=8), :] = value
        one, two = near[field // 2], far[field // 2]
        above, below = jnp.where(even, one, two), jnp.where(even, two, one)
        for slot in range(16):
            to = stiff.at[slot] if field == 5 else a.at[field, slot]
            to[0:8, 0:256] = rows_of(refs, field, slot, core)
            block = rows_of(refs, field, slot, 1 - core)
            for h in range(2):
                lanes = slice(128 * h, 128 * h + 128)
                edge = outer[h, 8 * slot : 8 * slot + 8, :]
                to[8:16, lanes] = jnp.where(beyond, edge, block[:, lanes])
            base = 64 * (field % 2) + 4 * slot
            up = pltpu.roll(above, 128 - base, 1) if base else above
            down = pltpu.roll(below, 124 - base, 1) if base != 124 else below
            to[:, 256:384] = jnp.where(first_lanes, up, down)

    def terms(src, field, slot, crop):
        mid = src[field, slot]
        up, down = src[field, (slot + 1) & 15], src[field, (slot + 15) & 15]
        xp, xm = pltpu.roll(mid, 15, 0), pltpu.roll(mid, 1, 0)
        yp, ym = pltpu.roll(mid, 383, 1), pltpu.roll(mid, 1, 1)
        if crop:
            mid, up, down, xp, xm, yp, ym = (v[0:8, 0:256] for v in (mid, up, down, xp, xm, yp, ym))
        total = 0.1 * mid + 0.12 * xp + 0.18 * xm + 0.17 * yp + 0.13 * ym
        return total + 0.14 * up + 0.16 * down, xp - xm, yp - ym, up - down

    def advance(src, slot, crop, store):
        vx, east, _, _ = terms(src, 1, slot, crop)
        vy, _, north, _ = terms(src, 2, slot, crop)
        vz, _, _, depth = terms(src, 3, slot, crop)
        div = 0.1 * (east + north + depth)
        store(0, terms(src, 0, slot, crop)[0] - div)
        pressure, east, north, depth = terms(src, 4, slot, crop)
        store(1, vx - 0.1 * east)
        store(2, vy - 0.1 * north)
        store(3, vz - 0.1 * depth)
        store(4, pressure - (stiff[slot, 0:8, 0:256] if crop else stiff[slot]) * div)

    for src, dst in ((a, b), (b, a), (a, None)):

        def body(slot, carry, src=src, dst=dst):
            def store(field, new):
                if dst is None:
                    rows = pl.ds(slot * 9, 8)
                    for h in range(2):
                        last[field, h, rows, :] = new[:, 128 * h : 128 * h + 128]
                else:
                    dst[field, slot] = new

            advance(src, slot, dst is None, store)
            return carry

        lax.fori_loop(0, 16, body, 0, unroll=True)


def lift_rows(values, weight, bias):
    rows = []
    for c in range(C):
        v = bias[c] + values[0] * weight[0, c]
        for field in range(1, 5):
            v = v + values[field] * weight[field, c]
        rows.append(gelu(v))
    return jnp.concatenate(rows, axis=0).astype(BF16)


def pointwise(keep, got, weight, bias, mix, obias, out, wide):
    a = lax.axis_index("ga")
    wide[pl.ds(pl.multiple_of(160 * a, 8), 160), :] = keep[...]
    wide[pl.ds(pl.multiple_of(160 * (1 - a), 8), 160), :] = got[...]
    row, lane = iotas((256, 32))
    pick = (row // 8 == lane).astype(BF16)
    bias_o = jnp.sum(jnp.where(row // 8 == lane, obias[...], 0.0), axis=1, keepdims=True)
    by_row = dot(pick, mix[...], ((1,), (1,))).astype(BF16)
    row, lane = iotas((256, 256))
    spread = jnp.where(row % 8 == lane % 8, dot(by_row, pick, ((1,), (1,))), 0.0).astype(BF16)

    def body(z, carry):
        values = [wide[pl.ds(8 * field + z, 8, stride=40), :] for field in range(5)]
        out[z] = dot(spread, lift_rows(values, weight, bias)) + bias_o
        return carry

    lax.fori_loop(0, ZL, body, 0)


def forward(
    last, after, weight, bias, yf_far, zf_far, keep, send, out, sums, lifted, modes, yf, zf, sems
):
    copies = [
        pltpu.make_async_copy(yf_far.at[lax.axis_index("gy")], yf, sems.at[0]),
        pltpu.make_async_copy(zf_far, zf, sems.at[1]),
    ]
    for copy in copies:
        copy.start()
    for half in range(2):
        for x in range(4):
            for field in range(5):
                at = 160 * half + 40 * x + 8 * field
                for h in range(2):
                    even = last[field, h, pl.ds(72 * half + 2 * x, 8, stride=9), :]
                    odd = last[field, h, pl.ds(72 * half + 2 * x + 1, 8, stride=9), :]
                    sums[at : at + 8, 128 * h : 128 * h + 128] = even + odd
    value = sums[...]
    high = value.astype(BF16)
    low = (value - high.astype(F32)).astype(BF16)
    row, lane = iotas((256, 128))
    table = jnp.where(row // 2 == lane, 0.25, 0.0).astype(BF16)
    mean = dot(high, table) + dot(low, table)
    keep[...] = mean[:160]
    send[...] = mean[160:]
    for x in range(4):
        at = [40 * x + 8 * field for field in range(5)]
        values = [jnp.concatenate([mean[r : r + 8], mean[r + 160 : r + 168]], axis=0) for r in at]
        lifted[x] = lift_rows(values, weight, bias)
    copies[0].wait()
    for x in range(4):
        modes[x] = dot(yf[...], lifted[x], ((1,), (1,)))
    copies[1].wait()
    parts = []
    for group in range(4):
        lanes = slice(128 * group, 128 * group + 128)
        stack = [
            jnp.concatenate([modes[x, 0:64, lanes], modes[x, 64:128, lanes]], axis=1)
            for x in range(4)
        ]
        both = dot(jnp.concatenate(stack, axis=0).astype(BF16), zf[...])
        parts.append(both[:, :128] + both[:, 128:])
    lane = lax.broadcasted_iota(jnp.int32, (256, 128), 1) // 32
    for part in range(4):
        total = parts[part]
        for group in range(4):
            if group != part:
                moved = pltpu.roll(parts[group], (32 * (group - part)) % 128, 1)
                total = jnp.where(lane == group, moved, total)
        for x in range(4):
            rows = pl.ds(8 * (part // 2) + 2 * x + part % 2, 64, stride=16)
            out[rows, :] = total[64 * x : 64 * x + 64]


def mix_modes(got, weights_far, xf, xi, after, out, weights, sem):
    copy = pltpu.make_async_copy(weights_far, weights, sem)
    copy.start()
    total = got[:, 0]
    for j in range(1, 8):
        total = total + got[:, j]
    both = jnp.concatenate(halves(total.reshape(128, 128)), axis=0)
    row, lane = iotas((128, 512))
    spread = (row // 8 % 4 == lane // 128) & (row // 32 * 8 + row % 8 == lane % 128 // 4)
    wide = dot(both, spread.astype(BF16)).astype(BF16)
    pieces = [
        jnp.concatenate([wide[:128, 128 * k : 128 * k + 128], wide[128:, 128 * k : 128 * k + 128]], axis=1)
        for k in range(4)
    ]
    modes = dot(xf[...], jnp.concatenate(pieces, axis=0))
    modes = modes[:, :128] + modes[:, 128:]
    real, imag = modes[:128], modes[128:]
    copy.wait()
    products = []
    for i in range(8):
        wr = weights[8 * i : 8 * i + 8, 0:16, :].astype(F32).reshape(128, 128)
        wi = weights[8 * i : 8 * i + 8, 16:32, :].astype(F32).reshape(128, 128)
        product = jnp.concatenate([wr * real - wi * imag, wr * imag + wi * real], axis=0)
        products.append(product.astype(BF16))
    row, lane = iotas((1024, 128))
    gather = (lane // 64 * 16 + lane % 16 == 4 * (row // 128) + row % 4).astype(BF16)
    total = dot(jnp.concatenate(products, axis=1), gather)
    row, lane = iotas((256, 128))
    total = jnp.where((row // 4) % 4 == (lane // 16) % 4, total, 0.0)
    back = dot(xi[...], jnp.concatenate(halves(total), axis=1))
    back = back[:128, :128] + back[:128, 128:] + back[128:, :128]
    real, imag = back[:64], back[64:]
    lane = lax.broadcasted_iota(jnp.int32, (64, 128), 1)
    parts = [
        jnp.where(lane < 64, real, pltpu.roll(imag, 64, 1)),
        jnp.where(lane < 64, pltpu.roll(real, 64, 1), imag),
    ]
    odd = (lane // 16) % 2 == 1
    for a in range(2):
        signed = [jnp.where(odd, -part, part) for part in parts] if a else parts
        for i in range(8):
            rows = slice(8 * i, 8 * i + 8)
            tile = jnp.concatenate([part[rows] for part in signed], axis=0).astype(BF16)
            for j in range(8):
                out[i, j, a] = tile


def finish(got, direct, yi_far, zi_far, out, rows, spectral, yi, zi, sems):
    copies = [
        pltpu.make_async_copy(yi_far.at[lax.axis_index("gy")], yi, sems.at[0]),
        pltpu.make_async_copy(zi_far, zi, sems.at[1]),
    ]
    for copy in copies:
        copy.start()
    for ky in range(64):
        rows[33 * ky : 33 * ky + 32, :] = got[32 * ky : 32 * ky + 32, :].astype(F32)
    copies[1].wait()
    by_z = []
    for part in range(2):
        stack = []
        for x in range(8):
            pair = [rows[pl.ds(16 * a + 8 * part + x, 64, stride=33), :] for a in range(2)]
            stack.append(jnp.concatenate(pair, axis=1).astype(BF16))
        by_z.append(dot(zi[...], jnp.concatenate(stack, axis=0), ((1,), (1,))))
    blank = jnp.zeros((64, 128), BF16)

    copies[0].wait()
    real, imag = yi[0:64, :], yi[64:128, :]
    pieces = [[real, blank], [blank, real], [imag, blank], [blank, imag]]
    twice = jnp.concatenate([jnp.concatenate(row, axis=1) for row in pieces], axis=0)
    for pair in range(4):
        lanes = slice(128 * pair, 128 * pair + 128)
        value = jnp.concatenate(
            [jnp.concatenate([v[:128, lanes], v[128:, lanes]], axis=1) for v in by_z], axis=0
        )
        both = dot(value.astype(BF16), twice)
        for x in range(2):
            spectral[pl.ds(2 * pair + x, 256, stride=9), :] = both[:, 128 * x : 128 * x + 128]
    for part in range(2):
        for z in range(ZL):
            first = 16 * (8 * part + z)
            branch = [spectral[9 * n : 9 * n + 8, :] for n in range(first, first + 16)]
            branch = jnp.concatenate(branch, axis=0).astype(BF16).astype(F32)
            total = gelu(direct[z, 128 * part : 128 * part + 128, :] + branch)
            out[z, 16 * part : 16 * part + 16] = total.reshape(16, 8, 128).astype(BF16)


def turn_weights(weights, out, wide):
    for chunk in range(16):
        turned = weights[128 * chunk : 128 * chunk + 128, :].T
        for ri in range(2):
            wide[:, 16 * ri + chunk, :] = turned[64 * ri : 64 * ri + 64]
    out[...] = wide[...].astype(BF16)


def shards(fields, stiffness, lift_weight, lift_bias, mix_weight, spectral_weight, output_bias):
    table = {name: jnp.asarray(value) for name, value in tables().items()}
    everyone = ("gx", "gy", "ga")

    def exchange(value, axis):
        return lax.all_to_all(value, axis, split_axis=0, concat_axis=0, tiled=True)

    anywhere = pl.BlockSpec(memory_space=pl.ANY)
    f = fields.reshape(5, 128, 256)
    s = stiffness.reshape(128, 256)
    swap = [(0, 1), (1, 0)]
    fp, sp = lax.ppermute(f, "ga", swap), lax.ppermute(s, "ga", swap)
    rows = pltpu.VMEM((6, 2, 128, 128), F32)
    edges = ((6, 2, 24, 128), F32)
    [turned] = call(
        turn_weights, [((64, 32, 128), BF16)], [VMEM], [pltpu.VMEM((64, 32, 128), F32)]
    )(spectral_weight.reshape(2048, 128))
    [own] = call(pack_own, [edges], [VMEM] * 2 + [anywhere], [rows])(f, s, turned)
    [message] = call(
        pack_other, [((6, 2, 48, 128), F32)], [VMEM] * 3, [pltpu.VMEM(*edges), rows]
    )(fp, sp, own)
    across = [(2 * i, 2 * ((i - 1) % 8) + 1) for i in range(8)]
    across += [(2 * i + 1, 2 * ((i + 1) % 8)) for i in range(8)]
    got = lax.ppermute(message, ("gx", "ga"), across)

    weights = exchange(turned, ("gx", "gy"))

    message = ((3, 16, 128), F32)
    far, near = call(
        pack_y,
        [message, message],
        [VMEM] * 5,
        [pltpu.VMEM((6, 2, 128, 128), F32)],
        flops=10**12,
    )(f, s, fp, sp, got)
    far = lax.ppermute(far, "gy", [(j, (j - 1 + 2 * (j % 2)) % 8) for j in range(8)])
    near = lax.ppermute(near, "gy", [(j, j + 1 - 2 * (j % 2)) for j in range(8)])
    [last] = call(
        stencil,
        [((5, 2, 144, 128), F32)],
        [VMEM] * 7,
        [
            pltpu.VMEM((5, 16, 16, 384), F32),
            pltpu.VMEM((5, 16, 16, 384), F32),
            pltpu.VMEM((16, 16, 384), F32),
            pltpu.VMEM((2, 128, 128), F32),
        ],
    )(f, s, fp, sp, got, far, near)
    keep, send, modes = call(
        forward,
        [((160, 128), F32), ((160, 128), F32), ((1024, 128), F32)],
        [VMEM, anywhere, SMEM, SMEM, anywhere, anywhere],
        [
            pltpu.VMEM((320, 256), F32),
            pltpu.VMEM((4, 512, 128), BF16),
            pltpu.VMEM((4, 128, 512), F32),
            pltpu.VMEM((128, 128), BF16),
            pltpu.VMEM((256, 256), BF16),
            pltpu.SemaphoreType.DMA((2,)),
        ],
    )(last, weights, lift_weight, lift_bias, table["yf"], table["zf"])
    modes = exchange(modes.reshape(128, 8, 128), everyone)
    [direct] = call(
        pointwise,
        [((8, 256, 128), F32)],
        [VMEM, VMEM, SMEM, SMEM, VMEM, VMEM],
        [pltpu.VMEM((320, 128), F32)],
        flops=3 * 10**8,
    )(keep, lax.ppermute(send, "ga", swap), lift_weight, lift_bias, mix_weight, output_bias.reshape(1, C))

    [mixed] = call(
        mix_modes,
        [((8, 8, 2, 16, 128), BF16)],
        [VMEM, anywhere, VMEM, VMEM, anywhere],
        [pltpu.VMEM((64, 32, 128), BF16), pltpu.SemaphoreType.DMA],
    )(modes.reshape(8, 8, 16, 128), weights, table["xf"], table["xi"], direct)
    mixed = exchange(mixed.reshape(128, 16, 128), everyone)
    [out] = call(
        finish,
        [((8, 32, 8, 128), BF16)],
        [VMEM, VMEM, anywhere, anywhere],
        [
            pltpu.VMEM((64 * 33, 128), F32),
            pltpu.VMEM((256 * 9, 128), F32),
            pltpu.VMEM((128, 128), BF16),
            pltpu.VMEM((256, 256), BF16),
            pltpu.SemaphoreType.DMA((2,)),
        ],
    )(mixed.reshape(2048, 128), direct, table["yi"], table["zi"])
    return out


def solution(mesh):
    placed = (
        P(None, "ga", "gx", "gy"),
        P("ga", "gx", "gy"),
        P(),
        P(),
        P(),
        P("ga", "gy", None, "gx", None),
        P(),
    )
    return jax.shard_map(
        shards, mesh=mesh, in_specs=placed, out_specs=P("ga", None, "gx", "gy"), check_vma=False
    )
```
